32 devices in a mesh: seq: 8 (over y, x, core), tp: 4 (over z).
Axes of the slice: x: 2, y: 2, z: 4, core: 2. Of those that a mesh axis runs over, the one named last changes fastest.
Arguments:
- tokens: float32 [8192, 1536], P(('seq', 'tp')), may hold values from -6 to 6
- inner_proj: bfloat16 [2, 1536, 2, 3072], P(None, 'seq', None, 'tp'), may hold values from -0.15625 to 0.15625
- step_proj: bfloat16 [2, 1536, 48], P(None, 'seq', 'tp'), may hold values from -0.15625 to 0.15625
- state_proj: bfloat16 [2, 1536, 256], P(None, ('seq', 'tp')), may hold values from -0.15625 to 0.15625
- inner_conv: float32 [2, 4, 3072], P(None, None, 'tp'), may hold values from -0.5 to 0.5
- state_conv: bfloat16 [2, 4, 256], P(None, None, ('seq', 'tp')), may hold values from -0.5 to 0.5
- decay_log: float32 [2, 48], P(None, 'tp'), may hold values from -1 to 1.5
- step_bias: float32 [2, 48], P(None, 'tp'), may hold values from -9 to -2
- skip_gain: float32 [2, 48], P(None, 'tp'), may hold values from 0.5 to 1.5
- gate_gain: float32 [2, 3072], P(None, 'tp'), may hold values from 0.5 to 1.5
- outer_proj: bfloat16 [2, 3072, 1536], P(None, 'tp', 'seq'), may hold values from -0.109375 to 0.109375
- norm_gains: bfloat16 [2, 2, 1536], P(None, None, ('seq', 'tp')), may hold values from 0.5 to 1.5
- router: bfloat16 [2, 1536, 16], P(None, ('seq', 'tp')), may hold values from -0.078125 to 0.078125
- expert_up: bfloat16 [2, 16, 1536, 1024], P(None, 'tp', 'seq'), may hold values from -0.15625 to 0.15625
- expert_down: bfloat16 [2, 16, 512, 1536], P(None, 'tp', 'seq'), may hold values from -0.75 to 0.75
- shared_up: bfloat16 [2, 1536, 2048], P(None, ('seq', 'tp')), may hold values from -0.15625 to 0.15625
- shared_down: bfloat16 [2, 1024, 1536], P(None, ('seq', 'tp')), may hold values from -0.25 to 0.25
- routes: int32 [2, 8192, 6], P(None, ('seq', 'tp')), may hold values from 0 to 15, all different within a row; in each aligned block of 256 rows (0 to 255, 256 to 511, ..., all dimensions but the last counted through in order) at most 120 rows name the same one
- packed_lengths: int32 [4], replicated, may hold values from 1 to 4096, 8192 in all
- cotangent: float32 [8192, 1536], P(('seq', 'tp')), may hold values from -6 to 6
Outputs:
- layer_output: float32 [8192, 1536], P(('seq', 'tp'))
- tokens_grad: float32 [8192, 1536], P(('seq', 'tp'))
- inner_proj_grad: float32 [2, 1536, 2, 3072], P(None, 'seq', None, 'tp')
- step_proj_grad: float32 [2, 1536, 48], P(None, 'seq', 'tp')
- state_proj_grad: float32 [2, 1536, 256], P(None, ('seq', 'tp'))
- inner_conv_grad: float32 [2, 4, 3072], P(None, None, 'tp')
- state_conv_grad: float32 [2, 4, 256], P(None, None, ('seq', 'tp'))
- decay_log_grad: float32 [2, 48], P(None, 'tp')
- step_bias_grad: float32 [2, 48], P(None, 'tp')
- skip_gain_grad: float32 [2, 48], P(None, 'tp')
- gate_gain_grad: float32 [2, 3072], P(None, 'tp')
- outer_proj_grad: float32 [2, 3072, 1536], P(None, 'tp', 'seq')
- norm_gains_grad: float32 [2, 2, 1536], P(None, None, ('seq', 'tp'))
- router_grad: float32 [2, 1536, 16], P(None, ('seq', 'tp'))
- expert_up_grad: float32 [2, 16, 1536, 1024], P(None, 'tp', 'seq')
- expert_down_grad: float32 [2, 16, 512, 1536], P(None, 'tp', 'seq')
- shared_up_grad: float32 [2, 1536, 2048], P(None, ('seq', 'tp'))
- shared_down_grad: float32 [2, 1024, 1536], P(None, ('seq', 'tp'))
The draws below stay inside these ranges and needn't reach their ends.
Inputs may be any that keep to these rules, and one draw needn't show every extreme that they name: `routes`: each row names 6 different experts. Within the 256 rows of one device, no expert is named by more than 120 rows, and in some device's rows one expert is named by exactly 120. `packed_lengths`: the lengths sum to 8192; the longest is exactly 4096.
All inputs are finite; a program needn't handle non-finite values.
Results may differ from the reference program's by a relative error of at most 0.02175.
Values may be sent and summed in bfloat16 or wider, within the bound.
No kernel may reach another device: no remote copies, remote signals or barrier semaphores. Data moves between devices by JAX's collectives and lax.ppermute only.
A program may use at most 512 MiB of HBM per device.

```python
import math
from functools import partial
import jax
import jax.numpy as jnp
import numpy as np
from jax import lax

D = 1536
HEADS = 48
HEAD_DIM = 64
STATE = 128
INNER = 3072
CONV_WIDTH = 4
EXPERT_FF = 512
SHARED_FF = 1024
TOP = 6
EXPERTS = 16
LAYERS = 2
BLOCK_LEN = 256
OWN_ROWS = 256
TOKENS = 8192
SEQ_MAX = 4096
SEQS = 4
CAP = 120


def steps_of(rng, shape, shards, least, high):
    def one(dim, blocks):
        steps = jax.random.uniform(jax.random.fold_in(jax.random.fold_in(rng, 6), dim), (blocks,), jnp.float32, least / len(shards), high / len(shards))
        return jnp.repeat(jnp.exp(steps), shape[dim] // blocks).reshape((-1,) + (1,) * (len(shape) - dim - 1))

    level = one(*shards[0])
    for cut in shards[1:]:
        level = level * one(*cut)
    return level


def length_profile(count, total, bound, lean):
    portions = [(1 << 20) // math.isqrt(rank ** lean) + 1 for rank in range(2, count + 1)]
    spare, given = total - bound - (count - 1), [1] * (count - 1)
    while spare > 0:
        movable = [i for i in range(count - 1) if given[i] < bound]
        mass, left = sum([portions[i] for i in movable]), spare
        for i in movable:
            extra = min(bound - given[i], max(1, left * portions[i] // mass), spare)
            given[i] = given[i] + extra
            spare = spare - extra
    return np.array([bound] + given)


def uneven(stream_key, number_of, total, limit, lean):
    if number_of == 2:
        one = jax.random.randint(stream_key, (), max(1, total - limit), min(limit, total - 1) + 1)
        return jnp.stack([one, total - one])
    tallies = jnp.asarray(length_profile(number_of, total, limit, lean), jnp.int32)
    couples = (number_of - 1) // 2
    donor, taker = tallies[1:1 + 2 * couples:2], tallies[2:2 + 2 * couples:2]
    room = jnp.minimum(donor - 1, limit - taker)
    moved = jax.random.randint(jax.random.fold_in(stream_key, 1), (couples,), 0, 1 << 20) % (room + 1)
    tallies = tallies.at[1:1 + 2 * couples:2].set(donor - moved).at[2:2 + 2 * couples:2].set(taker + moved)
    return tallies[jax.random.permutation(jax.random.fold_in(stream_key, 2), number_of)]


def assign_block(key, own, number, rows, count, top, limit, skew):
    order = jax.random.permutation(key, count)
    packed, common = portions_of(count, rows * top, limit, skew, True), portions_of(count, rows * top, limit, skew, False)
    places = jnp.arange(count)

    def named(lengths, rotation):
        used = int((lengths > 0).sum())
        fixed = max(1, used // 4)
        passed = fixed + (places - fixed + rotation * (used - fixed)) % max(1, count - fixed)
        return jnp.zeros((count,), jnp.int32).at[order[jnp.where(places < fixed, places, passed)]].set(jnp.asarray(lengths, jnp.int32))

    lengths = jnp.where(number % 4 == 0, named(packed, number // 4), named(common, number - number // 4 - 1))
    mixed = jax.random.permutation(jax.random.fold_in(own, 3), count)
    source_of, receiver = mixed[0:count // 2 * 2:2], mixed[1:count // 2 * 2:2]
    slack = jnp.minimum(lengths[source_of] - 1, limit - lengths[receiver]) // 2
    slack = jnp.where((source_of == order[0]) | (receiver == order[0]) | (lengths[receiver] == 0), 0, jnp.maximum(slack, 0))
    passed = jax.random.randint(jax.random.fold_in(own, 4), (count // 2,), 0, 1 << 20) % (slack + 1)
    lengths = lengths.at[source_of].add(-passed).at[receiver].add(passed)
    labels = jnp.searchsorted(jnp.cumsum(lengths), jnp.arange(rows * top), side="right").astype(jnp.int32)
    listing = labels.reshape(top, rows).T
    listing = listing[jax.random.permutation(jax.random.fold_in(own, 1), rows)]
    rotation = jax.random.randint(jax.random.fold_in(own, 2), (rows, 1), 0, top)
    return jnp.take_along_axis(listing, (jnp.arange(top)[None, :] + rotation) % top, axis=1)


def portions_of(amount, total, most, slope, full):
    loads = [(1 << 20) // math.isqrt(standing ** slope) + 1 for standing in range(1, amount + 1)]
    largest = most if full else min(most, max(-(-total // amount), total * loads[0] // sum(loads)))
    least = 1 if total - largest >= amount - 1 else 0
    holding, surplus = [largest] + [least] * (amount - 1), total - largest - least * (amount - 1)
    while surplus > 0:
        movable = [i for i in range(1, amount) if holding[i] < largest] or [i for i in range(1, amount) if holding[i] < most]
        whole, left = sum([loads[i] for i in movable]), surplus
        for i in movable:
            extra = min(most - holding[i], max(1, left * loads[i] // whole), surplus)
            holding[i] = holding[i] + extra
            surplus = surplus - extra
    return np.array(holding)


def centred(rng, extent, deviation, bound, shards=(), held_as=jnp.bfloat16):
    loudness = steps_of(rng, extent, shards, -0.22, 0.18) if shards else 1.0
    values = jax.random.normal(rng, extent, jnp.float32) * deviation * loudness
    return jnp.minimum(jnp.maximum(values, -bound), bound).astype(held_as)


def setup_inputs(seed: int = 0) -> dict:
    streams_of = jax.random.split(jax.random.key(seed), 21)
    tokens = centred(streams_of[0], (TOKENS, D), 1.0, 6.0, ((0, 32),), jnp.float32)
    inner_proj = centred(streams_of[1], (LAYERS, D, 2, INNER), D ** -0.5, 0.15625, ((1, 8), (3, 4)))
    step_proj = centred(streams_of[2], (LAYERS, D, HEADS), D ** -0.5, 0.15625, ((1, 8), (2, 4)))
    state_proj = centred(streams_of[3], (LAYERS, D, 2 * STATE), D ** -0.5, 0.15625, ((1, 32),))
    inner_conv = jnp.clip(jax.random.uniform(streams_of[4], (LAYERS, CONV_WIDTH, INNER), jnp.float32, -0.5, 0.5) * steps_of(streams_of[4], (LAYERS, CONV_WIDTH, INNER), ((2, 4),), -0.4, 0.0), -0.5, 0.5)
    state_conv = jnp.clip(jax.random.uniform(streams_of[5], (LAYERS, CONV_WIDTH, 2 * STATE), jnp.float32, -0.5, 0.5) * steps_of(streams_of[5], (LAYERS, CONV_WIDTH, 2 * STATE), ((2, 32),), -0.4, 0.0), -0.5, 0.5).astype(jnp.bfloat16)
    decay_log = jnp.clip(-1.0 + 2.5 * jax.random.uniform(streams_of[6], (LAYERS, HEADS), jnp.float32) ** steps_of(streams_of[6], (LAYERS, HEADS), ((1, 4),), -0.2, 0.2), -1.0, 1.5)
    step_bias = jnp.clip(-9.0 + 7.0 * jax.random.uniform(streams_of[7], (LAYERS, HEADS), jnp.float32) ** steps_of(streams_of[7], (LAYERS, HEADS), ((1, 4),), -0.2, 0.2), -9.0, -2.0)
    skip_gain = jnp.clip(0.5 + 1.0 * jax.random.uniform(streams_of[8], (LAYERS, HEADS), jnp.float32) ** steps_of(streams_of[8], (LAYERS, HEADS), ((1, 4),), -0.2, 0.2), 0.5, 1.5)
    gate_gain = jnp.clip(1.0 + 0.1 * jax.random.normal(streams_of[9], (LAYERS, INNER), jnp.float32), 0.5, 1.5)
    outer_proj = centred(streams_of[10], (LAYERS, INNER, D), INNER ** -0.5, 0.109375, ((1, 4), (2, 8)))
    norm_gains = jnp.clip(1.0 + 0.1 * jax.random.normal(streams_of[11], (LAYERS, 2, D), jnp.float32), 0.5, 1.5).astype(jnp.bfloat16)
    router = centred(streams_of[12], (LAYERS, D, EXPERTS), (4 * D) ** -0.5, 0.078125, ((1, 32),))
    expert_up = centred(streams_of[13], (LAYERS, EXPERTS, D, 2 * EXPERT_FF), D ** -0.5, 0.15625, ((1, 4), (2, 8)))
    expert_down = centred(streams_of[14], (LAYERS, EXPERTS, EXPERT_FF, D), (EXPERT_FF // 8) ** -0.5, 0.75, ((1, 4), (2, 8)))
    shared_up = centred(streams_of[15], (LAYERS, D, 2 * SHARED_FF), D ** -0.5, 0.15625, ((1, 32),))
    shared_down = centred(streams_of[16], (LAYERS, SHARED_FF, D), (SHARED_FF // 2) ** -0.5, 0.25, ((1, 32),))
    routes_keys = jax.random.split(jax.random.fold_in(streams_of[17], 1), LAYERS * TOKENS // OWN_ROWS)
    routes_turns = jax.random.permutation(jax.random.fold_in(streams_of[17], 3), LAYERS * TOKENS // OWN_ROWS)
    routes = jax.vmap(lambda own, number: assign_block(jax.random.fold_in(streams_of[17], 2), own, number, OWN_ROWS, EXPERTS, TOP, CAP, 1))(routes_keys, routes_turns).reshape((LAYERS, TOKENS, TOP))
    packed_lengths = uneven(streams_of[18], SEQS, TOKENS, SEQ_MAX, 1).astype(jnp.int32)
    cotangent = centred(streams_of[19], (TOKENS, D), 1.0, 6.0, ((0, 32),), jnp.float32)
    return dict(tokens=tokens, inner_proj=inner_proj, step_proj=step_proj, state_proj=state_proj, inner_conv=inner_conv, state_conv=state_conv, decay_log=decay_log, step_bias=step_bias, skip_gain=skip_gain, gate_gain=gate_gain, outer_proj=outer_proj, norm_gains=norm_gains, router=router, expert_up=expert_up, expert_down=expert_down, shared_up=shared_up, shared_down=shared_down, routes=routes, packed_lengths=packed_lengths, cotangent=cotangent)


epsilon = 1e-05
highest = lax.Precision.HIGHEST

@jax.custom_vjp
def low(v):
    return lax.optimization_barrier(v.astype(jnp.bfloat16)).astype(jnp.float32)

@jax.custom_vjp
def low_back(v):
    return v

def low_keep(v):
    return (low(v), None)

def low_pass(kept, grad):
    return (grad,)

def back_keep(v):
    return (v, None)

def back_low(kept, grad):
    return (low(grad),)
low.defvjp(low_keep, low_pass)
low_back.defvjp(back_keep, back_low)

def rms_norm(values, weight):
    return values * lax.rsqrt(lax.optimization_barrier(jnp.mean(values * values, axis=-1, keepdims=True)) + epsilon) * weight

def swiglu(hidden):
    half_width = hidden.shape[-1] // 2
    return jax.nn.silu(hidden[..., :half_width]) * hidden[..., half_width:]

def boundaries(packed_lengths, first_row, row_count, margin):
    seq_ends = jnp.cumsum(packed_lengths, dtype=jnp.int32)
    seq_starts = seq_ends - packed_lengths
    positions = first_row + jnp.arange(-margin, row_count, dtype=jnp.int32)
    return jnp.any(positions[:, None] == seq_starts[None, :], axis=1).astype(jnp.float32)

def conv_masks(starts_here, row_count, margin):
    stay_mask = 1.0 - starts_here
    running = jnp.ones((row_count,), jnp.float32)
    lag_list = [running]
    for offset in range(1, margin + 1):
        running = running * stay_mask[margin - offset + 1:margin - offset + 1 + row_count]
        lag_list.append(running)
    return jnp.stack(lag_list, 0)

def causal_conv(padded, conv_taps, lag_masks):
    row_count = lag_masks.shape[1]
    margin = padded.shape[0] - row_count
    summed = conv_taps[0] * padded[margin:]
    for offset in range(1, conv_taps.shape[0]):
        summed = summed + conv_taps[offset] * padded[margin - offset:margin - offset + row_count] * lag_masks[offset][:, None]
    return summed

def to_blocks(values, blocks):
    return values.reshape((blocks, values.shape[0] // blocks) + values.shape[1:])

def block_step(carry_state, block_data):
    inputs, key_rows, queries, log_rates, step_sizes, resets = block_data
    log_sums = jnp.cumsum(log_rates, axis=0)
    segment = jnp.cumsum(resets)
    order_ids = jnp.arange(log_rates.shape[0])
    same_run = (segment[:, None] == segment[None, :]) & (order_ids[None, :] <= order_ids[:, None])
    log_gap = log_sums[:, None, :] - log_sums[None, :, :]
    decay_table = jnp.where(same_run[:, :, None], jnp.exp(jnp.where(same_run[:, :, None], log_gap, 0.0)), 0.0)
    scores = jnp.dot(queries, key_rows.T, precision=highest)
    weights = decay_table * scores[:, :, None] * step_sizes[None, :, :]
    within = jnp.einsum('tsh,shp->thp', weights, inputs, precision=highest)
    entry_decay = jnp.exp(log_sums) * (segment == 0)[:, None]
    carried = jnp.einsum('tn,hpn->thp', queries, carry_state, precision=highest) * entry_decay[:, :, None]
    tail_decay = jnp.exp(log_sums[-1][None, :] - log_sums) * (segment == segment[-1])[:, None] * step_sizes
    through = jnp.exp(log_sums[-1]) * (segment[-1] == 0)
    new_state = through[:, None, None] * carry_state + jnp.einsum('sh,shp,sn->hpn', tail_decay, inputs, key_rows, precision=highest)
    return (new_state, within + carried)

def block_scan(heads_in, key_rows, queries, log_rates, step_sizes, resets):
    blocks = heads_in.shape[0] // BLOCK_LEN
    start_state = jnp.zeros((heads_in.shape[1], HEAD_DIM, STATE), jnp.float32)
    final_state, outputs = lax.scan(jax.checkpoint(block_step), start_state, (to_blocks(heads_in, blocks), to_blocks(key_rows, blocks), to_blocks(queries, blocks), to_blocks(log_rates, blocks), to_blocks(step_sizes, blocks), to_blocks(resets, blocks)))
    return (final_state, outputs.reshape(heads_in.shape))

def mixer_inputs(conv_in, bc_proj, edge_x, edge_bc, step_raw, x_taps, bc_taps, decay_log, step_bias, lag_masks):
    conv_out = jax.nn.silu(causal_conv(jnp.concatenate([edge_x, conv_in], 0), x_taps, lag_masks))
    bc_out = jax.nn.silu(causal_conv(jnp.concatenate([edge_bc, bc_proj], 0), bc_taps, lag_masks))
    step_sizes = jax.nn.softplus(step_raw + step_bias)
    log_rates = -jnp.exp(decay_log) * step_sizes
    heads_in = conv_out.reshape(conv_in.shape[0], -1, HEAD_DIM)
    return (heads_in, bc_out[:, :STATE], bc_out[:, STATE:], log_rates, step_sizes)

def slot_tables(expert_ids, capacity, experts):
    flat_ids = expert_ids.reshape(-1)
    onehot = (flat_ids[:, None] == jnp.arange(experts, dtype=jnp.int32)[None, :]).astype(jnp.int32)
    before = jnp.cumsum(onehot, axis=0, dtype=jnp.int32) - onehot
    position = lax.optimization_barrier(jnp.sum(before * onehot, axis=1)).astype(jnp.int32)
    slot_ids = (flat_ids * capacity + position).astype(jnp.int32)
    owners = jnp.full((experts * capacity,), flat_ids.shape[0], jnp.int32).at[slot_ids].set(jnp.arange(flat_ids.shape[0], dtype=jnp.int32))
    return (slot_ids, owners)

def routed_block(up_weights, down_weights, block_data):
    moe_rows, expert_ids, gate_weights = block_data
    slot_ids, owners = slot_tables(expert_ids, CAP, EXPERTS)
    padded = jnp.concatenate([moe_rows, jnp.zeros((1, D), jnp.float32)], 0)
    arrived = low_back(padded[owners // TOP]).reshape(EXPERTS, CAP, D)
    hidden = low_back(jnp.einsum('ecd,edf->ecf', arrived, up_weights, precision=highest))
    activated = low(swiglu(hidden))
    produced = low(low_back(jnp.einsum('ecf,efd->ecd', activated, down_weights, precision=highest)))
    picked = produced.reshape(EXPERTS * CAP, D)[slot_ids].reshape(OWN_ROWS, TOP, D)
    return lax.optimization_barrier(jnp.sum(gate_weights[:, :, None] * picked, axis=1))

def forward(float_args, routes, resets, lag_masks):
    tokens, inner_proj, step_proj, state_proj, inner_conv, state_conv, decay_log, step_bias, skip_gain, gate_gain, outer_proj, norm_gains, router, expert_up, expert_down, shared_up, shared_down = float_args
    margin = CONV_WIDTH - 1
    residual = tokens
    for layer_index in range(LAYERS):
        normed = low(rms_norm(residual, norm_gains[layer_index, 0]))
        zx_proj = low_back(jnp.dot(normed, inner_proj[layer_index].reshape(D, 2 * INNER), precision=highest))
        step_raw = low_back(jnp.dot(normed, step_proj[layer_index], precision=highest))
        bc_proj = jnp.dot(normed, state_proj[layer_index], precision=highest)
        gate_in = zx_proj[:, :INNER]
        heads_in, key_rows, queries, log_rates, step_sizes = mixer_inputs(zx_proj[:, INNER:], bc_proj, jnp.zeros((margin, INNER), jnp.float32), jnp.zeros((margin, 2 * STATE), jnp.float32), step_raw, inner_conv[layer_index], state_conv[layer_index], decay_log[layer_index], step_bias[layer_index], lag_masks)
        final_state, outputs = block_scan(heads_in, key_rows, queries, log_rates, step_sizes, resets)
        scanned = outputs + skip_gain[layer_index][None, :, None] * heads_in
        gated_out = scanned.reshape(TOKENS, INNER) * jax.nn.silu(gate_in)
        normed_gate = low(rms_norm(gated_out, gate_gain[layer_index]))
        residual = residual + low_back(jnp.dot(normed_gate, outer_proj[layer_index], precision=highest))
        moe_in = low(rms_norm(residual, norm_gains[layer_index, 1]))
        logits = jnp.dot(moe_in, router[layer_index], precision=highest)
        gate_weights = jax.nn.softmax(jnp.take_along_axis(logits, routes[layer_index], axis=1), axis=1)
        blocks = TOKENS // OWN_ROWS
        routed = lax.map(jax.checkpoint(partial(routed_block, expert_up[layer_index], expert_down[layer_index])), (moe_in.reshape(blocks, OWN_ROWS, D), routes[layer_index].reshape(blocks, OWN_ROWS, TOP), gate_weights.reshape(blocks, OWN_ROWS, TOP))).reshape(TOKENS, D)
        shared_hidden = low_back(jnp.dot(moe_in, shared_up[layer_index], precision=highest))
        shared_act = low(swiglu(shared_hidden))
        shared_out = low_back(jnp.dot(shared_act, shared_down[layer_index], precision=highest))
        residual = residual + routed + shared_out
    return residual

def reference(tokens, inner_proj, step_proj, state_proj, inner_conv, state_conv, decay_log, step_bias, skip_gain, gate_gain, outer_proj, norm_gains, router, expert_up, expert_down, shared_up, shared_down, routes, packed_lengths, cotangent):
    margin = CONV_WIDTH - 1
    starts_here = boundaries(packed_lengths, 0, TOKENS, margin)
    resets = starts_here[margin:]
    lag_masks = conv_masks(starts_here, TOKENS, margin)
    float_args = (tokens.astype(jnp.float32), inner_proj.astype(jnp.float32), step_proj.astype(jnp.float32), state_proj.astype(jnp.float32), inner_conv.astype(jnp.float32), state_conv.astype(jnp.float32), decay_log.astype(jnp.float32), step_bias.astype(jnp.float32), skip_gain.astype(jnp.float32), gate_gain.astype(jnp.float32), outer_proj.astype(jnp.float32), norm_gains.astype(jnp.float32), router.astype(jnp.float32), expert_up.astype(jnp.float32), expert_down.astype(jnp.float32), shared_up.astype(jnp.float32), shared_down.astype(jnp.float32))
    layer_output, pullback = jax.vjp(lambda *values: forward(values, routes, resets, lag_masks), *float_args)
    all_grads = pullback(cotangent.astype(jnp.float32))
    return (layer_output, all_grads[0], all_grads[1], all_grads[2], all_grads[3], all_grads[4], all_grads[5], all_grads[6], all_grads[7], all_grads[8], all_grads[9], all_grads[10], all_grads[11], all_grads[12], all_grads[13], all_grads[14], all_grads[15], all_grads[16])
```

```python
from functools import partial

import jax
import jax.numpy as jnp
from jax import lax
from jax.experimental import pallas as pl
from jax.experimental.layout import Layout, with_layout_constraint
from jax.experimental.pallas import tpu as pltpu
from jax.sharding import PartitionSpec as P

HEAD_DIM = 64
STATE = 128
TOP = 6
CHUNK = 256
LANES = 128
FF_BLOCK = 256
ROW_TILE = 256
FAR = -1e30

epsilon = 1e-05
highest = lax.Precision.HIGHEST
bf16 = jnp.bfloat16
f32 = jnp.float32

NN = (((1,), (0,)), ((), ()))
NT = (((1,), (1,)), ((), ()))
TN = (((0,), (0,)), ((), ()))


def mm(a, b, dims=NN, precision=None):
    return lax.dot_general(a, b, dims, precision=precision, preferred_element_type=f32)


def row_major(value):
    return with_layout_constraint(value, Layout(tuple(range(value.ndim))))


def tie(*values):
    return lax.optimization_barrier(values)


def hop_both(v, x, riders=(), axis="tp"):
    n, me = lax.axis_size(axis), lax.axis_index(axis)
    riders = tuple(riders)
    rel = {0: v}
    ahead = right = left = None
    if v is not None:
        ahead = (v, v)
    if x is not None:
        rows = x.shape[0] // n

        def piece(k):
            return lax.dynamic_slice_in_dim(x, jnp.clip(k, 0, n - 1) * rows, rows, 0)

        right, left = piece(n - 1 + me), piece(me - (n - 1))
    lead = 1 if v is not None and x is not None else 0
    for step in range(1, n + lead):
        held = []
        gathers, scatters = ahead is not None and step < n, right is not None and step > lead
        if gathers:
            held += list(ahead)
        if scatters:
            held += [right, left]
        if step > 1:
            count = len(held)
            extra = riders if step == 2 else ()
            if step == 2 and lead and scatters and not gathers:
                extra = riders
            held = list(tie(*held, *extra))
            if extra:
                riders = tuple(held[count:])
            held = held[:count]
        if gathers:
            ahead = (
                lax.ppermute(held[0], axis, [(i, i + 1) for i in range(step - 1, n - 1)]),
                lax.ppermute(held[1], axis, [(i, i - 1) for i in range(1, n - step + 1)]),
            )
            rel[-step], rel[step] = ahead
            held = held[2:]
        if scatters:
            s = step - lead
            right = lax.ppermute(held[0], axis, [(i, i + 1) for i in range(0, s)])
            left = lax.ppermute(held[1], axis, [(i, i - 1) for i in range(n - s, n)])
            if s < n - 1:
                right = (right.astype(f32) + piece(n - 1 - s + me).astype(f32)).astype(x.dtype)
                left = (left.astype(f32) + piece(me - (n - 1 - s)).astype(f32)).astype(x.dtype)
    gathered = total = None
    if v is not None:
        outs = []
        for j in range(n):
            out = rel[j]
            for m in range(1, n):
                out = jnp.where(me == m, rel[j - m], out)
            outs.append(out)
        gathered = jnp.concatenate(outs, 0)
    if x is not None:
        total = piece(me).astype(f32) + right.astype(f32) + left.astype(f32)
    return gathered, total, riders


def hop_gather(v):
    return hop_both(v, None)[0]


def hop_scatter(x):
    return hop_both(None, x)[1]


def pair_total(v, axis):
    n = lax.axis_size(axis)
    bit = 1
    while bit < n:
        v = v + lax.ppermute(v, axis, [(i, i ^ bit) for i in range(n)])
        bit *= 2
    return v


def pair_gather(v, axis="tp"):
    n, me = lax.axis_size(axis), lax.axis_index(axis)
    bit = 1
    while bit < n:
        other = lax.ppermute(v, axis, [(i, i ^ bit) for i in range(n)])
        high = (me & bit) > 0
        v = jnp.concatenate([jnp.where(high, other, v), jnp.where(high, v, other)], 0)
        bit *= 2
    return v


def pair_scatter(v, axis="tp"):
    n, me = lax.axis_size(axis), lax.axis_index(axis)
    bit = n // 2
    while bit:
        half = v.shape[0] // 2
        side = (me & bit) > 0
        first, second = v[:half], v[half:]
        got = lax.ppermute(
            jnp.where(side, first, second), axis, [(i, i ^ bit) for i in range(n)]
        )
        v = jnp.where(side, second, first).astype(f32) + got.astype(f32)
        v = v.astype(first.dtype) if bit > 1 else v
        bit //= 2
    return v


def pair_swap(v, axis="tp"):
    n, me = lax.axis_size(axis), lax.axis_index(axis)
    got = [lax.dynamic_index_in_dim(v, me, 0, keepdims=False)]
    for d in range(1, n):
        send = lax.dynamic_index_in_dim(v, me ^ d, 0, keepdims=False)
        got.append(lax.ppermute(send, axis, [(i, i ^ d) for i in range(n)]))
    outs = []
    for j in range(n):
        out = got[j]
        for m in range(1, n):
            out = jnp.where(me == m, got[j ^ m], out)
        outs.append(out)
    return jnp.stack(outs, 0)


def carried_state(through, state, direction):
    n = lax.axis_size("seq")

    def fetch(steps):
        high, low = split16(through)
        rows = [state.astype(bf16), high, low, jnp.zeros((14, state.shape[1]), bf16)]
        block = jnp.concatenate(rows, 0)
        got = []
        for step in steps:
            part = shift_seq(block, direction * step)
            decay = part[STATE : STATE + 1].astype(f32) + part[STATE + 1 : STATE + 2].astype(f32)
            got.append((decay, part[:STATE].astype(f32)))
        return got

    window = 0
    while window < n - 1:
        if window == 0:
            steps = [k for k in (1, 2, 3) if k < n]
            terms = fetch(steps)
            reach = 3
        else:
            steps = [k * window for k in (1, 2) if k * window < n]
            terms = [(through, state)] + fetch(steps)
            reach = 3 * window
        through, state = terms[0]
        for decay, part in terms[1:]:
            state = state + through * part
            through = through * decay
        window = reach
    return state


def shift_seq(v, steps):
    n = lax.axis_size("seq")
    first, last = max(0, -steps), min(n, n - steps)
    return lax.ppermute(v, "seq", [(i, i + steps) for i in range(first, last)])


def sigmoid(v):
    return 1.0 / (1.0 + jnp.exp(-v))


def shift_down(block, halo, j):
    rolled = pltpu.roll(block, j, 0)
    edge = pltpu.roll(halo, j, 0)
    row = lax.broadcasted_iota(jnp.int32, halo.shape, 0)
    return jnp.concatenate([jnp.where(row < j, edge, rolled[:8]), rolled[8:]], 0)


def shift_up(block, after, j):
    rows = block.shape[0]
    rolled = pltpu.roll(block, rows - j, 0)
    edge = pltpu.roll(after, 8 - j, 0)
    row = lax.broadcasted_iota(jnp.int32, after.shape, 0)
    return jnp.concatenate(
        [rolled[: rows - 8], jnp.where(row >= 8 - j, edge, rolled[rows - 8 :])], 0
    )


def conv_pre(block, halo, taps_ref, aux):
    pre = taps_ref[0:1, :] * block
    for j in (1, 2, 3):
        pre = pre + taps_ref[j : j + 1, :] * (aux[:, j : j + 1] * shift_down(block, halo, j))
    return pre


def softplus(v):
    return jnp.maximum(v, 0.0) + jnp.log(1.0 + jnp.exp(-jnp.abs(v)))


def split16(value):
    high = value.astype(bf16)
    return high, (value - high.astype(f32)).astype(bf16)


def widen(value, ex_ref):
    high, low = split16(value)
    return mm(jnp.concatenate([high, low], 1), ex_ref[...])


def head_sums(value, ex_ref):
    high, low = split16(value)
    spread = ex_ref[:LANES, :]
    return mm(high, spread, NT) + mm(low, spread, NT)


def triangle(n, upper=False):
    row = lax.broadcasted_iota(jnp.int32, (n, n), 0)
    col = lax.broadcasted_iota(jnp.int32, (n, n), 1)
    return jnp.where(row <= col if upper else row >= col, 1.0, 0.0).astype(f32)


def gap_mask(aux, auxr):
    n = aux.shape[0]
    row = lax.broadcasted_iota(jnp.int32, (n, n), 0)
    col = lax.broadcasted_iota(jnp.int32, (n, n), 1)
    return jnp.where((row >= col) & (aux[:, 4:5] == auxr[0:1, :]), 0.0, FAR).astype(f32)


def states_kernel(
    u_ref, bc_ref, dt_ref, edge_ref, taps_ref, head_ref, aux_ref, ex_ref,
    xs_ref, bcs_ref, lc_ref, lt_ref, dtv_ref, thr_ref, ent_ref, fin_ref,
    halo, state,
):
    c = pl.program_id(0)
    n, inner = xs_ref.shape

    @pl.when(c == 0)
    def _():
        halo[...] = edge_ref[...]
        state[...] = jnp.zeros_like(state)

    aux = aux_ref[...]
    block = jnp.concatenate([u_ref[...], bc_ref[...]], 1)
    pre = conv_pre(block, halo[...], taps_ref, aux)
    halo[...] = block[n - 8 :]
    act = pre * sigmoid(pre)
    xs = act[:, :inner]
    bcs = act[:, inner:].astype(bf16)
    dtv = softplus(dt_ref[...] + head_ref[0:1, :])
    lc = mm(triangle(n), head_ref[1:2, :] * dtv, precision=highest)
    total = lc[n - 1 : n, :]
    xs_ref[...] = xs.astype(bf16)
    bcs_ref[...] = bcs
    lc_ref[...] = lc
    lt_ref[...] = lc.T
    dtv_ref[...] = dtv
    scale = widen(jnp.exp(total - lc) * aux[:, 6:7] * dtv, ex_ref)
    through = jnp.exp(jnp.broadcast_to(total, (8, LANES))) * aux[n - 1 : n, 5:6]
    through = widen(through, ex_ref)
    thr_ref[0] = through
    ent_ref[0] = state[...]
    state[...] = through[0:1, :] * state[...] + mm(
        bcs[:, :STATE], (xs * scale).astype(bf16), TN
    )
    fin_ref[...] = state[...]


def intra_kernel(xs_ref, bcs_ref, lc_ref, lt_ref, dtv_ref, aux_ref, auxr_ref, ex_ref, y_ref):
    inner = xs_ref.shape[1]
    mask = gap_mask(aux_ref[...], auxr_ref[...])
    scores = mm(bcs_ref[:, STATE:], bcs_ref[:, :STATE], NT)
    xd = xs_ref[...].astype(f32) * widen(dtv_ref[...], ex_ref)
    lane = lax.broadcasted_iota(jnp.int32, (1, LANES), 1)
    for p in range(inner // LANES):
        pair = xd[:, p * LANES : (p + 1) * LANES]
        total = None
        for side in range(2):
            h = 2 * p + side
            decay = jnp.exp(lc_ref[:, h : h + 1] - lt_ref[h : h + 1, :] + mask)
            mine = (lane < HEAD_DIM) if side == 0 else (lane >= HEAD_DIM)
            term = mm((decay * scores).astype(bf16), jnp.where(mine, pair, 0.0).astype(bf16))
            total = term if total is None else total + term
        y_ref[:, p * LANES : (p + 1) * LANES] = total


def read_kernel(
    z_ref, yi_ref, xs_ref, bcs_ref, lc_ref, aux_ref, ex_ref, ent_ref, car_ref, thr_ref, rows_ref,
    y_ref, gg_ref, ss_ref, st_ref, pre,
):
    c = pl.program_id(0)

    @pl.when(c == 0)
    def _():
        pre[...] = jnp.ones_like(pre)

    entering = ent_ref[0] + pre[0:1, :] * car_ref[...]
    pre[...] = pre[...] * thr_ref[0]
    st_ref[0] = entering
    read = mm(bcs_ref[:, STATE:], entering.astype(bf16))
    entry = widen(jnp.exp(lc_ref[...]) * aux_ref[:, 5:6], ex_ref)
    y = yi_ref[...] + entry * read + rows_ref[0:1, :] * xs_ref[...].astype(f32)
    z = z_ref[...]
    gated = y * (z * sigmoid(z))
    y_ref[...] = y
    gg_ref[...] = (gated * rows_ref[1:2, :]).astype(bf16)
    ss_ref[...] = jnp.broadcast_to(
        jnp.sum(gated * gated, axis=1, keepdims=True), ss_ref.shape
    )


def gate_back_kernel(
    dg_ref, z_ref, y_ref, c2_ref, rows_ref, xs_ref, bcs_ref, lc_ref, aux_ref, ex_ref, thr_ref,
    dy_ref, dz_ref, lg_ref, fin_ref, acc_ref, run,
):
    @pl.when(pl.program_id(0) == 0)
    def _():
        run[...] = jnp.zeros_like(run)
        acc_ref[...] = jnp.zeros_like(acc_ref)

    z, y, back = z_ref[...], y_ref[...], dg_ref[...]
    sig = sigmoid(z)
    open_ = z * sig
    gated = y * open_
    d_gated = back * rows_ref[1:2, :] - gated * c2_ref[:, 0:1]
    dy = d_gated * open_
    dz_ref[...] = (d_gated * y * (sig * (1.0 + z * (1.0 - sig)))).astype(bf16)
    dy_ref[...] = dy.astype(bf16)
    acc_ref[0:1, :] += jnp.sum(back * gated, axis=0, keepdims=True)
    acc_ref[1:2, :] += jnp.sum(dy * xs_ref[...].astype(f32), axis=0, keepdims=True)
    entry = widen(jnp.exp(lc_ref[...]) * aux_ref[:, 5:6], ex_ref)
    lg_ref[0] = run[...]
    run[...] = thr_ref[0, 0:1, :] * run[...] + mm(
        bcs_ref[:, STATE:], (entry * dy).astype(bf16), TN
    )
    fin_ref[...] = run[...]


def scan_back_kernel(
    u_ref, bc_ref, uh_ref, bch_ref, edge_ref, dt_ref, dz_ref, taps_ref, head_ref, rows_ref, aux_ref, auxr_ref, ex_ref,
    lc_ref, lt_ref, dtv_ref, dy_ref, st_ref, lg_ref, car_ref, thr_ref,
    dp_ref, last_ref, back_ref, tacc_ref, hacc_ref,
    post, nxt, later,
):
    step = pl.program_id(0)
    chunks = pl.num_programs(0)
    n, inner = dy_ref.shape

    @pl.when(step == 0)
    def _():
        post[...] = jnp.ones_like(post)
        nxt[...] = jnp.zeros_like(nxt)
        tacc_ref[...] = jnp.zeros_like(tacc_ref)
        hacc_ref[...] = jnp.zeros_like(hacc_ref)
        later[...] = jnp.zeros_like(later)

    aux = aux_ref[...]
    block = jnp.concatenate([u_ref[...], bc_ref[...]], 1)
    halo = jnp.concatenate([uh_ref[...], bch_ref[...]], 1)
    halo = jnp.where(step == chunks - 1, edge_ref[...], halo)
    shifted = [block] + [aux[:, j : j + 1] * shift_down(block, halo, j) for j in (1, 2, 3)]
    pre = taps_ref[0:1, :] * block
    for j in (1, 2, 3):
        pre = pre + taps_ref[j : j + 1, :] * shifted[j]
    sig = sigmoid(pre)
    act = pre * sig
    slope = sig * (1.0 + pre * (1.0 - sig))
    xs = act[:, :inner]
    bcs = act[:, inner:].astype(bf16)
    keys, queries = bcs[:, :STATE], bcs[:, STATE:]
    lc, dtv = lc_ref[...], dtv_ref[...]
    total = lc[n - 1 : n, :]
    dt_wide = widen(dtv, ex_ref)
    tail_wide = widen(jnp.exp(total - lc) * aux[:, 6:7], ex_ref)
    entry_wide = widen(jnp.exp(lc) * aux[:, 5:6], ex_ref)
    xd = xs * dt_wide
    dy = dy_ref[...]
    dyf = dy.astype(f32)
    entering = st_ref[0]
    leaving = lg_ref[0] + post[0:1, :] * car_ref[...]
    post[...] = post[...] * thr_ref[0]
    ent16, lea16 = entering.astype(bf16), leaving.astype(bf16)

    row = lax.broadcasted_iota(jnp.int32, (n, n), 0)
    col = lax.broadcasted_iota(jnp.int32, (n, n), 1)
    mask = jnp.where((row <= col) & (aux[:, 4:5] == auxr_ref[0:1, :]), 0.0, FAR).astype(f32)
    scores = mm(keys, queries, NT)
    lane = lax.broadcasted_iota(jnp.int32, (1, LANES), 1)
    earlier = jnp.zeros((n, LANES), f32)
    d_scores = jnp.zeros((n, n), f32)
    parts = []
    for p in range(inner // LANES):
        cut = slice(p * LANES, (p + 1) * LANES)
        xd_pair, dy_pair = xd[:, cut].astype(bf16), dyf[:, cut]
        d_pair = None
        for side in range(2):
            h = 2 * p + side
            mine = (lane < HEAD_DIM) if side == 0 else (lane >= HEAD_DIM)
            dy_mine = jnp.where(mine, dy_pair, 0.0).astype(bf16)
            decay = jnp.exp(lt_ref[h : h + 1, :] - lc_ref[:, h : h + 1] + mask)
            weights = decay * scores
            d_weights = mm(xd_pair, dy_mine, NT)
            both = weights * d_weights
            earlier = jnp.where(lane == h, jnp.sum(both, axis=1, keepdims=True), earlier)
            later[h : h + 1, :] = jnp.sum(both, axis=0, keepdims=True)
            d_scores = d_scores + decay * d_weights
            term = mm(weights.astype(bf16), dy_mine)
            d_pair = term if d_pair is None else d_pair + term
        parts.append(d_pair)
    d_scores16 = d_scores.astype(bf16)
    through_lea = tail_wide * mm(keys, lea16)
    dxd = jnp.concatenate(parts, 1) + through_lea
    dxs = dt_wide * dxd + rows_ref[0:1, :] * dyf
    entry_dy = entry_wide * dyf
    d_queries = mm(d_scores16, keys, TN) + mm(entry_dy.astype(bf16), ent16, NT)
    d_keys = mm(d_scores16, queries) + mm((tail_wide * xd).astype(bf16), lea16, NT)
    d_act = jnp.concatenate([dxs, d_keys, d_queries], 1)
    dpre = d_act * slope

    into = head_sums(entry_dy * mm(queries, ent16), ex_ref)
    outof = head_sums(xd * through_lea, ex_ref)
    ends = head_sums(
        jnp.sum(entering * leaving, axis=0, keepdims=True) * thr_ref[0], ex_ref
    )
    d_log = later[...].T - earlier + into - outof
    row = lax.broadcasted_iota(jnp.int32, (n, 1), 0)
    d_log = d_log + jnp.where(
        row == n - 1, jnp.sum(outof, axis=0, keepdims=True) + ends[0:1, :], 0.0
    )
    d_rate = mm(triangle(n, True), d_log, precision=highest)
    d_dt = head_sums(xs * dxd, ex_ref) + d_rate * head_ref[1:2, :]
    d_step = d_dt * sigmoid(dt_ref[...] + head_ref[0:1, :])
    hacc_ref[0:1, :] += jnp.sum(d_rate * dtv, axis=0, keepdims=True) * head_ref[1:2, :]
    hacc_ref[1:2, :] += jnp.sum(d_step, axis=0, keepdims=True)

    d_block = taps_ref[0:1, :] * dpre
    tacc_ref[0:1, :] += jnp.sum(dpre * block, axis=0, keepdims=True)
    before = jnp.zeros((8, block.shape[1]), f32)
    row8 = lax.broadcasted_iota(jnp.int32, (8, 1), 0)
    for j in (1, 2, 3):
        tacc_ref[j : j + 1, :] += jnp.sum(dpre * shifted[j], axis=0, keepdims=True)
        lagged = taps_ref[j : j + 1, :] * (dpre * aux[:, j : j + 1])
        d_block = d_block + shift_up(lagged, nxt[j - 1], j)
        nxt[j - 1] = lagged[:8]
        before = before + jnp.where(row8 >= 8 - j, pltpu.roll(lagged[:8], 8 - j, 0), 0.0)
    back_ref[...] = before

    @pl.when(step == 0)
    def _():
        last_ref[...] = d_block[n - 8 :]

    dp_ref[:, :inner] = dz_ref[...]
    dp_ref[:, inner : inner + block.shape[1]] = d_block.astype(bf16)
    ends_at = inner + block.shape[1] + LANES
    dp_ref[:, inner + block.shape[1] : ends_at] = d_step.astype(bf16)
    dp_ref[:, ends_at:] = jnp.zeros((n, LANES), bf16)


def sds(shape, dtype):
    return jax.ShapeDtypeStruct(shape, dtype)


def params(mib):
    return pltpu.CompilerParams(
        dimension_semantics=("arbitrary",), vmem_limit_bytes=mib * 1024 * 1024
    )


def whole(shape):
    return pl.BlockSpec(shape, lambda c: (0,) * len(shape))


def mixer_specs(rows, inner, reverse):
    chunks = rows // CHUNK
    at = (lambda c: chunks - 1 - c) if reverse else (lambda c: c)
    return {
        "uh": pl.BlockSpec(
            (8, inner), lambda c: (jnp.maximum(at(c) * (CHUNK // 8) - 1, 0), 0)
        ),
        "bch": pl.BlockSpec(
            (8, 2 * STATE),
            lambda c: (jnp.maximum(at(c) * (CHUNK // 8) - 1, 0), inner // (2 * STATE)),
        ),
        "bc": pl.BlockSpec((CHUNK, 2 * STATE), lambda c: (at(c), inner // (2 * STATE))),
        "dt": pl.BlockSpec((CHUNK, LANES), lambda c: (at(c), (inner + 2 * STATE) // LANES)),
        "wide": pl.BlockSpec((CHUNK, inner), lambda c: (at(c), 0)),
        "bcs": pl.BlockSpec((CHUNK, 2 * STATE), lambda c: (at(c), 0)),
        "col": pl.BlockSpec((CHUNK, LANES), lambda c: (at(c), 0)),
        "lt": pl.BlockSpec((LANES, CHUNK), lambda c: (0, at(c))),
        "auxr": pl.BlockSpec((8, CHUNK), lambda c: (0, at(c))),
        "state": pl.BlockSpec((1, STATE, inner), lambda c: (at(c), 0, 0)),
        "thr": pl.BlockSpec((1, 8, inner), lambda c: (at(c), 0, 0)),
        "dp": pl.BlockSpec((CHUNK, 2 * inner + 2 * STATE + 2 * LANES), lambda c: (at(c), 0)),
        "edge": whole((8, inner + 2 * STATE)),
        "head": whole((8, LANES)),
        "rows": whole((8, inner)),
        "ex": whole((2 * LANES, inner)),
        "one": whole((STATE, inner)),
    }


def mixer_states(pu, edge, taps, head, aux, ex, inner):
    rows = pu.shape[0]
    chunks = rows // CHUNK
    s = mixer_specs(rows, inner, False)
    return pl.pallas_call(
        states_kernel,
        grid=(chunks,),
        in_specs=[
            s["wide"], s["bc"], s["dt"], s["edge"], s["edge"], s["head"], s["col"], s["ex"],
        ],
        out_specs=[
            s["wide"], s["bcs"], s["col"], s["lt"], s["col"], s["thr"], s["state"], s["one"],
        ],
        out_shape=[
            sds((rows, inner), bf16),
            sds((rows, 2 * STATE), bf16),
            sds((rows, LANES), f32),
            sds((LANES, rows), f32),
            sds((rows, LANES), f32),
            sds((chunks, 8, inner), f32),
            sds((chunks, STATE, inner), f32),
            sds((STATE, inner), f32),
        ],
        scratch_shapes=[
            pltpu.VMEM((8, inner + 2 * STATE), f32),
            pltpu.VMEM((STATE, inner), f32),
        ],
        compiler_params=params(32),
        name="mixer_states",
    )(pu, pu, pu, edge, taps, head, aux, ex)


def mixer_intra(xs, bcs, lc, lt, dtv, aux, auxr, ex):
    rows, inner = xs.shape
    s = mixer_specs(rows, inner, False)
    return pl.pallas_call(
        intra_kernel,
        grid=(rows // CHUNK,),
        in_specs=[
            s["wide"], s["bcs"], s["col"], s["lt"], s["col"], s["col"], s["auxr"], s["ex"],
        ],
        out_specs=s["wide"],
        out_shape=sds((rows, inner), f32),
        compiler_params=params(32),
        name="mixer_intra",
    )(xs, bcs, lc, lt, dtv, aux, auxr, ex)


def mixer_read(pz, yi, xs, bcs, lc, aux, ex, ent, carried, thr, head_rows):
    rows, inner = xs.shape
    chunks = rows // CHUNK
    s = mixer_specs(rows, inner, False)
    return pl.pallas_call(
        read_kernel,
        grid=(chunks,),
        in_specs=[
            s["wide"], s["wide"], s["wide"], s["bcs"], s["col"], s["col"], s["ex"],
            s["state"], s["one"], s["thr"], s["rows"],
        ],
        out_specs=[s["wide"], s["wide"], s["col"], s["state"]],
        out_shape=[
            sds((rows, inner), f32),
            sds((rows, inner), bf16),
            sds((rows, LANES), f32),
            sds((chunks, STATE, inner), f32),
        ],
        scratch_shapes=[pltpu.VMEM((8, inner), f32)],
        compiler_params=params(32),
        name="mixer_read",
    )(pz, yi, xs, bcs, lc, aux, ex, ent, carried, thr, head_rows)


def mixer_gate_back(dg, pz, y, c2, head_rows, xs, bcs, lc, aux, ex, thr):
    rows, inner = xs.shape
    chunks = rows // CHUNK
    s = mixer_specs(rows, inner, True)
    return pl.pallas_call(
        gate_back_kernel,
        grid=(chunks,),
        in_specs=[
            s["wide"], s["wide"], s["wide"], s["col"], s["rows"], s["wide"], s["bcs"],
            s["col"], s["col"], s["ex"], s["thr"],
        ],
        out_specs=[s["wide"], s["wide"], s["state"], s["one"], s["rows"]],
        out_shape=[
            sds((rows, inner), bf16),
            sds((rows, inner), bf16),
            sds((chunks, STATE, inner), f32),
            sds((STATE, inner), f32),
            sds((8, inner), f32),
        ],
        scratch_shapes=[pltpu.VMEM((STATE, inner), f32)],
        compiler_params=params(40),
        name="mixer_gate_back",
    )(dg, pz, y, c2, head_rows, xs, bcs, lc, aux, ex, thr)


def mixer_scan_back(
    pu, edge, dz, taps, head, head_rows, aux, auxr, ex, lc, lt, dtv, dy, st, lg, carried, thr
):
    rows, inner = dy.shape
    chunks = rows // CHUNK
    s = mixer_specs(rows, inner, True)
    wide = inner + 2 * STATE
    return pl.pallas_call(
        scan_back_kernel,
        grid=(chunks,),
        in_specs=[
            s["wide"], s["bc"], s["uh"], s["bch"], s["edge"], s["dt"], s["wide"], s["edge"],
            s["head"], s["rows"], s["col"], s["auxr"], s["ex"], s["col"], s["lt"], s["col"], s["wide"], s["state"], s["state"],
            s["one"], s["thr"],
        ],
        out_specs=[s["dp"], s["edge"], s["edge"], s["edge"], s["head"]],
        out_shape=[
            sds((rows, wide + inner + 2 * LANES), bf16),
            sds((8, wide), f32),
            sds((8, wide), f32),
            sds((8, wide), f32),
            sds((8, LANES), f32),
        ],
        scratch_shapes=[
            pltpu.VMEM((8, inner), f32),
            pltpu.VMEM((3, 8, wide), f32),
            pltpu.VMEM((LANES, CHUNK), f32),
        ],
        compiler_params=params(48),
        name="mixer_scan_back",
    )(
        pu, pu, pu, pu, edge, pu, dz, taps, head, head_rows, aux, auxr, ex, lc, lt, dtv, dy, st,
        lg, carried, thr,
    )


def up_kernel(x_ref, w_ref, gate_ref, pat_ref, h_ref, act_ref):
    for start in range(0, x_ref.shape[0], ROW_TILE):
        cut = slice(start, start + ROW_TILE)
        hidden = mm(x_ref[cut, :], w_ref[...])
        g, w = hidden[:, :FF_BLOCK], hidden[:, FF_BLOCK:]
        gate = mm(gate_ref[cut, :], pat_ref[...])
        h_ref[cut, :] = hidden.astype(bf16)
        act_ref[cut, :] = (g * sigmoid(g) * w * gate).astype(bf16)


def down_back_kernel(gs_ref, w_ref, h_ref, gate_ref, pat_ref, dh_ref, dgate_ref):
    @pl.when(pl.program_id(0) == 0)
    def _():
        dgate_ref[...] = jnp.zeros_like(dgate_ref)

    for start in range(0, gs_ref.shape[0], ROW_TILE):
        cut = slice(start, start + ROW_TILE)
        q = mm(gs_ref[cut, :], w_ref[...], NT)
        g = h_ref[cut, :FF_BLOCK].astype(f32)
        w = h_ref[cut, FF_BLOCK:].astype(f32)
        sig = sigmoid(g)
        opened = g * sig
        gate = mm(gate_ref[cut, :], pat_ref[...])
        dgate_ref[cut, :] += mm((opened * w * q).astype(bf16), pat_ref[...], NT)
        d_act = gate * q
        dh_ref[cut, :FF_BLOCK] = (d_act * w * (sig * (1.0 + g * (1.0 - sig)))).astype(bf16)
        dh_ref[cut, FF_BLOCK:] = (d_act * opened).astype(bf16)


def experts_up(x, w_up, gates, pattern):
    rows, depth = x.shape
    blocks = w_up.shape[1] // (2 * FF_BLOCK)
    return pl.pallas_call(
        up_kernel,
        grid=(blocks,),
        in_specs=[
            whole((rows, depth)),
            pl.BlockSpec((depth, 2 * FF_BLOCK), lambda i: (0, i)),
            whole((rows, LANES)),
            pl.BlockSpec((LANES, FF_BLOCK), lambda i: (0, i)),
        ],
        out_specs=[
            pl.BlockSpec((rows, 2 * FF_BLOCK), lambda i: (0, i)),
            pl.BlockSpec((rows, FF_BLOCK), lambda i: (0, i)),
        ],
        out_shape=[
            sds((rows, 2 * FF_BLOCK * blocks), bf16),
            sds((rows, FF_BLOCK * blocks), bf16),
        ],
        compiler_params=params(32),
        name="experts_up",
    )(x, w_up, gates, pattern)


def experts_down_back(gs, w_down, hidden, gates, pattern):
    rows, depth = gs.shape
    blocks = w_down.shape[0] // FF_BLOCK
    return pl.pallas_call(
        down_back_kernel,
        grid=(blocks,),
        in_specs=[
            whole((rows, depth)),
            pl.BlockSpec((FF_BLOCK, depth), lambda i: (i, 0)),
            pl.BlockSpec((rows, 2 * FF_BLOCK), lambda i: (0, i)),
            whole((rows, LANES)),
            pl.BlockSpec((LANES, FF_BLOCK), lambda i: (0, i)),
        ],
        out_specs=[
            pl.BlockSpec((rows, 2 * FF_BLOCK), lambda i: (0, i)),
            whole((rows, LANES)),
        ],
        out_shape=[
            sds((rows, 2 * FF_BLOCK * blocks), bf16),
            sds((rows, LANES), f32),
        ],
        compiler_params=params(32),
        name="experts_down_back",
    )(gs, w_down, hidden, gates, pattern)


def row_norm(values):
    return lax.rsqrt(jnp.mean(values * values, axis=-1, keepdims=True) + epsilon)


def norm_back(values, inverse, gain, grad):
    weighted = grad * gain
    mean = jnp.mean(weighted * values, axis=-1, keepdims=True)
    return inverse * weighted - values * (inverse * inverse * inverse * mean)


def pad_rows(parts, rows, width):
    value = jnp.concatenate([jnp.atleast_2d(part) for part in parts], 0)
    return jnp.pad(value, ((0, rows - value.shape[0]), (0, width - value.shape[1])))


def to_line(column):
    value = column.reshape(-1, LANES)
    return jnp.pad(value, ((0, 8 - value.shape[0]), (0, 0)))


def local(
    tokens, inner_proj, step_proj, state_proj, inner_conv, state_conv, decay_log, step_bias,
    skip_gain, gate_gain, outer_proj, norm_gains, router, expert_up, expert_down, shared_up,
    shared_down, routes, packed_lengths, cotangent,
):
    ns, nt = lax.axis_size("seq"), lax.axis_size("tp")
    sq, tp = lax.axis_index("seq"), lax.axis_index("tp")
    layers = inner_proj.shape[0]
    own, depth = tokens.shape
    rows = own * nt
    chunks = rows // CHUNK
    inner = gate_gain.shape[1]
    heads = decay_log.shape[1]
    inner_all = inner * nt
    cut = inner_proj.shape[1]
    fine = state_proj.shape[1]
    devices = ns * nt
    experts = router.shape[2]
    mine = expert_up.shape[1]
    ff = expert_down.shape[2] * ns
    ff_cut = expert_down.shape[2]
    shared = shared_down.shape[1] * ns
    sh_cut = shared_down.shape[1]
    tap_cut = state_conv.shape[2]
    width = inner + 2 * STATE
    hidden_units = mine * ff + shared
    ff_blocks = hidden_units // FF_BLOCK
    per_seq = mine * ff_cut + sh_cut

    ends = jnp.cumsum(packed_lengths, dtype=jnp.int32)
    starts = ends - packed_lengths

    def count(positions):
        return jnp.sum(
            (starts[None, :] <= positions[:, None]).astype(f32), axis=1
        )

    first = sq * rows
    here = first + jnp.arange(rows, dtype=jnp.int32)
    seg = count(here)
    chunk_of = jnp.arange(rows, dtype=jnp.int32) // CHUNK
    lags = [jnp.ones_like(seg)] + [(count(here - j) == seg).astype(f32) for j in (1, 2, 3)]
    alive = (count(first + chunk_of * CHUNK - 1) == seg).astype(f32)
    tail = (count(first + chunk_of * CHUNK + CHUNK - 1) == seg).astype(f32)
    aux = jnp.pad(jnp.stack(lags + [seg, alive, tail], 1), ((0, 0), (0, LANES - 7)))
    auxr = jnp.broadcast_to(seg[None, :], (8, rows))
    lane_head = jnp.arange(inner, dtype=jnp.int32) // HEAD_DIM
    ex_row = jnp.arange(2 * LANES, dtype=jnp.int32)[:, None] % LANES
    ex = (ex_row == lane_head[None, :]).astype(bf16)
    unit = jnp.arange(hidden_units, dtype=jnp.int32) % per_seq
    unit_gate = jnp.where(unit < mine * ff_cut, unit // ff_cut, mine)
    pat_row = jnp.arange(LANES, dtype=jnp.int32)[:, None]
    pattern = ((pat_row == unit_gate[None, :]) | (pat_row == 16 + unit_gate[None, :])).astype(bf16)

    inv1 = row_norm(tokens)
    scaled = (tokens * inv1).astype(bf16)
    smalls, ups = [], []
    for l in range(layers):
        taps_col = jnp.pad(state_conv[l].reshape(-1), (0, fine - 4 * tap_cut))[:, None]
        small = jnp.concatenate([state_proj[l], router[l], norm_gains[l].T, taps_col], 1)
        smalls.append(jnp.pad(small, ((0, 0), (0, 2 * STATE + LANES - small.shape[1]))))
        up = shared_up[l].reshape(fine, 2, ns, nt, sh_cut)
        ups.append(jnp.transpose(up, (3, 0, 1, 2, 4)).reshape(nt, fine, 2 * shared))
    plain, _, riders = hop_both(
        scaled,
        None,
        (jnp.concatenate(smalls, 1), expert_up, jnp.stack(ups, 1), routes, expert_down, shared_down),
    )
    small_all, expert_up, ups, routes, expert_down, shared_down = riders
    small_all = pair_gather(small_all)
    up_all = pair_swap(ups)

    def mixer_weights(l):
        dt_cols = jnp.pad(step_proj[l], ((0, 0), (0, LANES - heads)))
        small = small_all[:, l * (2 * STATE + LANES) : (l + 1) * (2 * STATE + LANES)]
        pack = jnp.concatenate(
            [
                inner_proj[l, :, 0],
                inner_proj[l, :, 1],
                small[:, : 2 * STATE],
                dt_cols,
                small[:, 2 * STATE :],
            ],
            1,
        )
        return pack, outer_proj[l].T

    def over_seq(value):
        return lax.all_gather(value, "seq", axis=0, tiled=True)

    def expert_weights(l):
        halves = jnp.transpose(expert_up[l].reshape(mine, cut, 2, ns, ff_cut), (2, 1, 3, 0, 4))
        halves = halves.reshape(2, cut, ns, mine * ff_cut)
        extra = jnp.transpose(up_all[:, l].reshape(cut, 2, ns, sh_cut), (1, 0, 2, 3))
        halves = jnp.concatenate([halves, extra], 3).reshape(2, cut, ff_blocks, FF_BLOCK)
        local_up = jnp.transpose(halves, (1, 2, 0, 3)).reshape(cut, 2 * hidden_units)
        local_down = jnp.concatenate(
            [expert_down[l].reshape(mine * ff_cut, depth), shared_down[l]], 0
        )
        return local_up, local_down

    packs = [list(mixer_weights(l) + expert_weights(l)) for l in range(layers)]
    plain, *packs[0][2:] = tie(plain, *packs[0][2:])
    w_in, w_out, w_up, w_down = [[None] * layers for _ in range(4)]
    w_in[0], w_out[0] = over_seq(packs[0][0]), over_seq(packs[0][1])

    named = jnp.any(
        routes[:, :, :, None] == jnp.arange(experts, dtype=jnp.int32), axis=2
    ).astype(bf16)
    named = pair_gather(
        jnp.transpose(named, (1, 0, 2)).reshape(own, layers * experts)
    ).reshape(rows, layers, experts)

    residual = tokens
    saved = []
    last_cot = None
    for l in range(layers):
        small_in = tie(w_in[l][:, inner + width + LANES :].astype(f32).T)[0]
        router_w = small_in[:experts].astype(bf16)
        gain1 = small_in[experts]
        gain2 = small_in[experts + 1]
        taps_bc = small_in[experts + 2].reshape(devices, fine)[:, : 4 * tap_cut]
        taps_bc = jnp.transpose(taps_bc.reshape(devices, 4, tap_cut), (1, 0, 2))
        taps_bc = taps_bc.reshape(4, 2 * STATE)
        taps = jnp.pad(
            jnp.concatenate([inner_conv[l], taps_bc], 1), ((0, 4), (0, 0))
        )
        head = pad_rows([step_bias[l], -jnp.exp(decay_log[l])], 8, LANES)
        head_rows = pad_rows([jnp.repeat(skip_gain[l], HEAD_DIM), gate_gain[l]], 8, inner)

        if l > 0:
            inv1 = row_norm(residual)
            scaled = (residual * inv1).astype(bf16)
            plain = hop_gather(scaled)
        normed = (plain.astype(f32) * gain1).astype(bf16)
        pu = mm(normed, w_in[l][:, inner : inner + width + LANES])
        edge = shift_seq(pu[rows - 8 :, :width], 1)
        xs, bcs, lc, lt, dtv, thr, ent, fin = mixer_states(pu, edge, taps, head, aux, ex, inner)
        through = thr[0, 0:1]
        for c in range(1, chunks):
            through = through * thr[c, 0:1]
        carried = carried_state(through, fin, 1)
        pz = mm(normed, w_in[l][:, :inner])
        cot16 = cotangent.astype(bf16)
        if l == 0:
            pz, cot16 = tie(pz, cot16)
        yi = mixer_intra(xs, bcs, lc, lt, dtv, aux, auxr, ex)
        carried, up_pack, down_pack = tie(carried, packs[l][2], packs[l][3])
        w_up[l], w_down[l] = over_seq(up_pack), over_seq(down_pack)
        y, gg, ss, st = mixer_read(pz, yi, xs, bcs, lc, aux, ex, ent, carried, thr, head_rows)
        squares = pair_total(ss[:, 0].reshape(rows // LANES, LANES), "tp")
        squares = lax.dynamic_slice_in_dim(
            squares, tp * (own // LANES), own // LANES, 0
        ).reshape(own)
        partial_out = mm(gg, w_out[l], NT).astype(bf16)
        if l == 0:
            last_cot, out_sum, _ = hop_both(cot16, partial_out)
            out_sum, last_cot = tie(out_sum, last_cot)
        else:
            out_sum = hop_scatter(partial_out)
        inv_gate = lax.rsqrt(squares / inner_all + epsilon)
        mixed = inv_gate[:, None] * out_sum
        mid = residual + mixed

        inv2 = row_norm(mid)
        moe_own = (mid * inv2 * gain2).astype(bf16)
        moe_in = hop_gather(moe_own)
        if l < layers - 1:
            moe_in, *packs[l + 1] = tie(moe_in, *packs[l + 1])
            w_in[l + 1], w_out[l + 1] = over_seq(packs[l + 1][0]), over_seq(packs[l + 1][1])
        logits = mm(moe_in, router_w, NT)
        mask = named[:, l] > 0
        peak = jnp.max(jnp.where(mask, logits, FAR), axis=1, keepdims=True)
        raised = jnp.where(mask, jnp.exp(jnp.where(mask, logits - peak, 0.0)), 0.0)
        gates = raised / jnp.sum(raised, axis=1, keepdims=True)
        gates_mine = lax.dynamic_slice_in_dim(gates, tp * mine, mine, 1)
        gates_mine = jnp.concatenate([gates_mine, jnp.ones((rows, 1), f32)], 1)
        high, low = split16(gates_mine)
        gate_cols = jnp.concatenate(
            [jnp.pad(part, ((0, 0), (0, 15 - mine))) for part in (high, low)], 1
        )
        gate_cols = jnp.pad(gate_cols, ((0, 0), (0, LANES - 32)))
        hidden, act = experts_up(moe_in, w_up[l], gate_cols, pattern)
        saved.append(
            dict(
                router_w=router_w, gain1=gain1, gain2=gain2, taps=taps, head=head,
                head_rows=head_rows, residual=residual, inv1=inv1, plain=plain, normed=normed,
                pu=pu, pz=pz, edge=edge, xs=xs, bcs=bcs, lc=lc, lt=lt, dtv=dtv, thr=thr,
                through=through, y=y, gg=gg, st=st, inv_gate=inv_gate, mixed=mixed,
                mid=mid, inv2=inv2, moe_own=moe_own, moe_in=moe_in, gates=gates,
                gate_cols=gate_cols, hidden=hidden, act=act,
            )
        )
        if l < layers - 1:
            residual = mid + hop_scatter(mm(act, w_down[l]).astype(bf16))

    def finish(r):
        late, early, sums = r["late"], r["early"], r["sums"]
        halves = r["up"].reshape(cut, ff_blocks, 2, FF_BLOCK)
        halves = jnp.transpose(halves, (2, 0, 1, 3)).reshape(2, cut, ns, per_seq)
        mine_up = halves[..., : mine * ff_cut].reshape(2, cut, ns, mine, ff_cut)
        mine_up = jnp.transpose(mine_up, (3, 1, 0, 2, 4)).reshape(mine, cut, 2 * ff)
        mine_up = row_major(mine_up)
        shared_cols = jnp.transpose(halves[..., mine * ff_cut :], (1, 0, 2, 3))
        shared_grad = pair_swap(shared_cols.reshape(nt, fine, 2 * shared))
        shared_grad = jnp.transpose(
            shared_grad.reshape(nt, fine, 2, ns, sh_cut), (1, 2, 3, 0, 4)
        ).reshape(fine, -1)
        common = pair_scatter(late[:, inner:])
        small = common[:, 2 * STATE + heads :]
        return [
            jnp.stack([early[:, inner:], late[:, :inner]], 1),
            late[:, width : width + heads].astype(f32),
            common[:, : 2 * STATE],
            sums[:4],
            small[: 4 * tap_cut, experts + 2].reshape(4, tap_cut),
            sums[6, :heads],
            sums[6, LANES : LANES + heads],
            jnp.sum(sums[5].reshape(heads, HEAD_DIM), axis=1),
            sums[4],
            early[:, :inner].T,
            jnp.transpose(small[:, experts : experts + 2]),
            small[:, :experts],
            mine_up,
            r["down"][: mine * ff_cut].reshape(mine, ff_cut, depth),
            shared_grad,
            r["down"][mine * ff_cut :],
        ]

    grad = cotangent
    finished = [None] * layers
    for l in reversed(range(layers)):
        k = saved[l]
        top = l == layers - 1
        gs = last_cot if top else hop_gather(grad.astype(bf16))
        if not top:
            gs, above["late"] = tie(gs, above["late"])
        else:
            last_out = mm(k["act"], w_down[l]).astype(bf16)
        d_hidden, d_gate = experts_down_back(
            gs, w_down[l], k["hidden"], k["gate_cols"], pattern
        )
        d_gate_all = jnp.zeros((rows, experts), f32)
        d_gate_all = lax.dynamic_update_slice(d_gate_all, d_gate[:, :mine], (0, tp * mine))
        per_line = LANES // experts
        d_gate_all = pair_total(d_gate_all.reshape(rows // per_line, LANES), "tp")
        d_gate_own = lax.dynamic_slice_in_dim(
            d_gate_all, tp * (own // per_line), own // per_line, 0
        ).reshape(own, experts)
        d_moe = hop_scatter(mm(d_hidden, w_up[l], NT).astype(bf16))
        up_part = mm(k["moe_in"], d_hidden, TN).astype(bf16)
        down_part = mm(k["act"], gs, TN).astype(bf16)
        if top:
            d_moe, up_part, last_out = tie(d_moe, up_part, last_out)
        else:
            d_moe, up_part = tie(d_moe, up_part)
        up_grad = lax.psum_scatter(up_part, "seq", scatter_dimension=0, tiled=True)
        gates_own = lax.dynamic_slice_in_dim(k["gates"], tp * own, own, 0)
        d_logits = gates_own * (
            d_gate_own - jnp.sum(gates_own * d_gate_own, axis=1, keepdims=True)
        )
        d_logits16 = d_logits.astype(bf16)
        router_grad = mm(k["moe_own"], d_logits16, TN)
        d_moe = d_moe + mm(d_logits16, k["router_w"])
        gain2_grad = jnp.sum(d_moe * k["mid"] * k["inv2"], axis=0)
        grad_mid = grad + norm_back(k["mid"], k["inv2"], k["gain2"], d_moe)

        inv_gate = k["inv_gate"]
        cross = inv_gate * inv_gate * jnp.sum(grad_mid * k["mixed"], axis=1) / inner_all
        cross_all = pair_gather(to_line(cross)).reshape(nt, 8 * LANES)[:, :own].reshape(rows)
        c2 = jnp.broadcast_to(cross_all[:, None], (rows, LANES))
        send = (grad_mid * inv_gate[:, None]).astype(bf16)
        if top:
            d_mixed, moe_out, _ = hop_both(send, last_out)
            residual = k["mid"] + moe_out
        else:
            d_mixed = hop_gather(send)
        d_mixed, down_part = tie(d_mixed, down_part)
        down_grad = lax.psum_scatter(down_part, "seq", scatter_dimension=0, tiled=True)
        dg = mm(d_mixed, w_out[l])
        dy, dz, lg, fin, acc = mixer_gate_back(
            dg, k["pz"], k["y"], c2, k["head_rows"], k["xs"], k["bcs"], k["lc"], aux, ex, k["thr"]
        )
        carried = carried_state(k["through"], fin, -1)
        early = jnp.concatenate(
            [
                row_major(mm(d_mixed, k["gg"], TN).astype(bf16)),
                row_major(mm(k["normed"], dz, TN).astype(bf16)),
            ],
            1,
        )
        carried, early, up_grad = tie(carried, early, up_grad)
        if top:
            carried, residual = tie(carried, residual)
        early = lax.psum_scatter(early, "seq", scatter_dimension=0, tiled=True)
        dp, last, back, tacc, hacc = mixer_scan_back(
            k["pu"], k["edge"], dz, k["taps"], k["head"], k["head_rows"], aux, auxr, ex,
            k["lc"], k["lt"], k["dtv"], dy, k["st"], lg, carried, k["thr"],
        )
        last = (last + shift_seq(back, -1)).astype(bf16)
        dp = lax.dynamic_update_slice(dp, last, (rows - 8, inner))
        dp, down_grad = tie(dp, down_grad)
        d_normed = mm(dp, w_in[l], NT)
        gain1_grad = jnp.sum(d_normed * k["plain"].astype(f32), axis=0)
        if top:
            d_own = hop_scatter(d_normed.astype(bf16))
        else:
            names = ("up", "down", "early", "late")
            _, d_own, riders = hop_both(
                None, d_normed.astype(bf16), [above[name] for name in names]
            )
            above.update(zip(names, riders))
            finished[l + 1] = finish(above)
        taps_col = jnp.transpose(tacc[:4, inner:].reshape(4, devices, tap_cut), (1, 0, 2))
        taps_col = jnp.pad(taps_col.reshape(devices, 4 * tap_cut), ((0, 0), (0, fine - 4 * tap_cut)))
        small = jnp.concatenate(
            [router_grad, gain1_grad[:, None], gain2_grad[:, None], taps_col.reshape(-1)[:, None]],
            1,
        )
        late = mm(k["normed"], dp[:, inner : inner + width + LANES], TN).astype(bf16)
        block = late[:, width:] + jnp.pad(
            small, ((0, 0), (heads, LANES - heads - small.shape[1]))
        ).astype(bf16)
        late = lax.dynamic_update_slice(late, block, (0, width))
        d_own, late, early = tie(d_own, late, early)
        late = lax.psum_scatter(late, "seq", scatter_dimension=0, tiled=True)
        sums = pair_total(
            jnp.concatenate(
                [tacc[:4, :inner], acc[:2], pad_rows([hacc[:2].reshape(-1)], 2, inner)], 0
            ),
            "seq",
        )
        grad = grad_mid + norm_back(k["residual"], k["inv1"], k["gain1"], d_own)
        above = dict(up=up_grad, down=down_grad, early=early, late=late, sums=sums)

    finished[0] = finish(above)
    stacked = [jnp.stack([part[i] for part in finished], 0).astype(f32) for i in range(16)]
    return (residual, grad, *stacked)


def solution(mesh):
    both = ("seq", "tp")
    in_specs = (
        P(both, None),
        P(None, "seq", None, "tp"),
        P(None, "seq", "tp"),
        P(None, both, None),
        P(None, None, "tp"),
        P(None, None, both),
        P(None, "tp"),
        P(None, "tp"),
        P(None, "tp"),
        P(None, "tp"),
        P(None, "tp", "seq"),
        P(None, None, both),
        P(None, both, None),
        P(None, "tp", "seq", None),
        P(None, "tp", "seq", None),
        P(None, both, None),
        P(None, both, None),
        P(None, both, None),
        P(),
        P(both, None),
    )
    out_specs = (
        P(both, None),
        P(both, None),
        P(None, "seq", None, "tp"),
        P(None, "seq", "tp"),
        P(None, both, None),
        P(None, None, "tp"),
        P(None, None, both),
        P(None, "tp"),
        P(None, "tp"),
        P(None, "tp"),
        P(None, "tp"),
        P(None, "tp", "seq"),
        P(None, None, both),
        P(None, both, None),
        P(None, "tp", "seq", None),
        P(None, "tp", "seq", None),
        P(None, both, None),
        P(None, both, None),
    )
    return jax.shard_map(local, mesh=mesh, in_specs=in_specs, out_specs=out_specs, check_vma=False)
```

```python
from functools import partial

import jax
import jax.numpy as jnp
from jax import lax
from jax.experimental import pallas as pl
from jax.experimental.layout import Layout, with_layout_constraint
from jax.experimental.pallas import tpu as pltpu
from jax.sharding import PartitionSpec as P

HEAD_DIM = 64
STATE = 128
TOP = 6
CHUNK = 256
LANES = 128
FF_BLOCK = 256
ROW_TILE = 256
FAR = -1e30

epsilon = 1e-05
highest = lax.Precision.HIGHEST
bf16 = jnp.bfloat16
f32 = jnp.float32

NN = (((1,), (0,)), ((), ()))
NT = (((1,), (1,)), ((), ()))
TN = (((0,), (0,)), ((), ()))


def mm(a, b, dims=NN, precision=None):
    return lax.dot_general(a, b, dims, precision=precision, preferred_element_type=f32)


def row_major(value):
    return with_layout_constraint(value, Layout(tuple(range(value.ndim))))


def tie(*values):
    return lax.optimization_barrier(values)


def hop_both(v, x, riders=(), axis="tp"):
    n, me = lax.axis_size(axis), lax.axis_index(axis)
    riders = tuple(riders)
    rel = {0: v}
    ahead = right = left = None
    if v is not None:
        ahead = (v, v)
    if x is not None:
        rows = x.shape[0] // n

        def piece(k):
            return lax.dynamic_slice_in_dim(x, jnp.clip(k, 0, n - 1) * rows, rows, 0)

        right, left = piece(n - 1 + me), piece(me - (n - 1))
    lead = 1 if v is not None and x is not None else 0
    for step in range(1, n + lead):
        held = []
        gathers, scatters = ahead is not None and step < n, right is not None and step > lead
        if gathers:
            held += list(ahead)
        if scatters:
            held += [right, left]
        if step > 1:
            count = len(held)
            extra = riders if step == 2 else ()
            if step == 2 and lead and scatters and not gathers:
                extra = riders
            held = list(tie(*held, *extra))
            if extra:
                riders = tuple(held[count:])
            held = held[:count]
        if gathers:
            ahead = (
                lax.ppermute(held[0], axis, [(i, i + 1) for i in range(step - 1, n - 1)]),
                lax.ppermute(held[1], axis, [(i, i - 1) for i in range(1, n - step + 1)]),
            )
            rel[-step], rel[step] = ahead
            held = held[2:]
        if scatters:
            s = step - lead
            right = lax.ppermute(held[0], axis, [(i, i + 1) for i in range(0, s)])
            left = lax.ppermute(held[1], axis, [(i, i - 1) for i in range(n - s, n)])
            if s < n - 1:
                right = (right.astype(f32) + piece(n - 1 - s + me).astype(f32)).astype(x.dtype)
                left = (left.astype(f32) + piece(me - (n - 1 - s)).astype(f32)).astype(x.dtype)
    gathered = total = None
    if v is not None:
        outs = []
        for j in range(n):
            out = rel[j]
            for m in range(1, n):
                out = jnp.where(me == m, rel[j - m], out)
            outs.append(out)
        gathered = jnp.concatenate(outs, 0)
    if x is not None:
        total = piece(me).astype(f32) + right.astype(f32) + left.astype(f32)
    return gathered, total, riders


def choose(options, me):
    out = options[0]
    for m in range(1, len(options)):
        out = jnp.where(me == m, options[m], out)
    return out


def gather_work(v, work, axis="tp"):
    n, me = lax.axis_size(axis), lax.axis_index(axis)
    near = [sorted((j for j in range(n) if j != m), key=lambda j: abs(j - m)) for m in range(n)]
    right = left = block = v
    at, state, rel = me, None, {0: v}
    for d in range(1, n):
        right = lax.ppermute(right, axis, [(i, i + 1) for i in range(d - 1, n - 1)])
        left = lax.ppermute(left, axis, [(i, i - 1) for i in range(1, n - d + 1)])
        state = work(block, at, state)
        right, left, *state = tie(right, left, *state)
        rel[-d], rel[d] = right, left
        block = choose([rel[near[m][d - 1] - m] for m in range(n)], me)
        at = choose([near[m][d - 1] for m in range(n)], me)
    state = work(block, at, state)
    whole_v = jnp.concatenate(
        [choose([rel[j - m] for m in range(n)], me) for j in range(n)], 0
    )
    return whole_v, state


def hop_gather(v):
    return hop_both(v, None)[0]


def hop_scatter(x):
    return hop_both(None, x)[1]


def pair_total(v, axis):
    n = lax.axis_size(axis)
    bit = 1
    while bit < n:
        v = v + lax.ppermute(v, axis, [(i, i ^ bit) for i in range(n)])
        bit *= 2
    return v


def pair_gather(v, axis="tp"):
    n, me = lax.axis_size(axis), lax.axis_index(axis)
    bit = 1
    while bit < n:
        other = lax.ppermute(v, axis, [(i, i ^ bit) for i in range(n)])
        high = (me & bit) > 0
        v = jnp.concatenate([jnp.where(high, other, v), jnp.where(high, v, other)], 0)
        bit *= 2
    return v


def pair_scatter(v, axis="tp"):
    n, me = lax.axis_size(axis), lax.axis_index(axis)
    bit = n // 2
    while bit:
        half = v.shape[0] // 2
        side = (me & bit) > 0
        first, second = v[:half], v[half:]
        got = lax.ppermute(
            jnp.where(side, first, second), axis, [(i, i ^ bit) for i in range(n)]
        )
        v = jnp.where(side, second, first).astype(f32) + got.astype(f32)
        v = v.astype(first.dtype) if bit > 1 else v
        bit //= 2
    return v


def pair_swap(v, axis="tp"):
    n, me = lax.axis_size(axis), lax.axis_index(axis)
    got = [lax.dynamic_index_in_dim(v, me, 0, keepdims=False)]
    for d in range(1, n):
        send = lax.dynamic_index_in_dim(v, me ^ d, 0, keepdims=False)
        got.append(lax.ppermute(send, axis, [(i, i ^ d) for i in range(n)]))
    outs = []
    for j in range(n):
        out = got[j]
        for m in range(1, n):
            out = jnp.where(me == m, got[j ^ m], out)
        outs.append(out)
    return jnp.stack(outs, 0)


def carried_state(through, state, direction, *beside):
    n = lax.axis_size("seq")
    rest = []

    def fetch(steps):
        high, low = split16(through)
        rows = [state.astype(bf16), high, low, jnp.zeros((14, state.shape[1]), bf16)]
        block = jnp.concatenate(rows, 0)
        got = []
        parts = [shift_seq(block, direction * step) for step in steps]
        if window == 0:
            parts = tie(*parts, *beside)
            rest[:] = parts[len(steps) :]
        for part in parts[: len(steps)]:
            decay = part[STATE : STATE + 1].astype(f32) + part[STATE + 1 : STATE + 2].astype(f32)
            got.append((decay, part[:STATE].astype(f32)))
        return got

    window = 0
    while window < n - 1:
        if window == 0:
            steps = [k for k in (1, 2, 3) if k < n]
            terms = fetch(steps)
            reach = 3
        else:
            steps = [k * window for k in (1, 2) if k * window < n]
            terms = [(through, state)] + fetch(steps)
            reach = 3 * window
        through, state = terms[0]
        for decay, part in terms[1:]:
            state = state + through * part
            through = through * decay
        window = reach
    return state, *rest


def shift_seq(v, steps):
    n = lax.axis_size("seq")
    first, last = max(0, -steps), min(n, n - steps)
    return lax.ppermute(v, "seq", [(i, i + steps) for i in range(first, last)])


def sigmoid(v):
    return 1.0 / (1.0 + jnp.exp(-v))


def shift_down(block, halo, j):
    rolled = pltpu.roll(block, j, 0)
    edge = pltpu.roll(halo, j, 0)
    row = lax.broadcasted_iota(jnp.int32, halo.shape, 0)
    return jnp.concatenate([jnp.where(row < j, edge, rolled[:8]), rolled[8:]], 0)


def shift_up(block, after, j):
    rows = block.shape[0]
    rolled = pltpu.roll(block, rows - j, 0)
    edge = pltpu.roll(after, 8 - j, 0)
    row = lax.broadcasted_iota(jnp.int32, after.shape, 0)
    return jnp.concatenate(
        [rolled[: rows - 8], jnp.where(row >= 8 - j, edge, rolled[rows - 8 :])], 0
    )


def conv_pre(block, halo, taps_ref, aux):
    pre = taps_ref[0:1, :] * block
    for j in (1, 2, 3):
        pre = pre + taps_ref[j : j + 1, :] * (aux[:, j : j + 1] * shift_down(block, halo, j))
    return pre


def softplus(v):
    return jnp.maximum(v, 0.0) + jnp.log(1.0 + jnp.exp(-jnp.abs(v)))


def split16(value):
    high = value.astype(bf16)
    return high, (value - high.astype(f32)).astype(bf16)


def widen(value, ex_ref):
    high, low = split16(value)
    return mm(jnp.concatenate([high, low], 1), ex_ref[...])


def head_sums(value, ex_ref):
    high, low = split16(value)
    spread = ex_ref[:LANES, :]
    return mm(high, spread, NT) + mm(low, spread, NT)


def triangle(n, upper=False):
    row = lax.broadcasted_iota(jnp.int32, (n, n), 0)
    col = lax.broadcasted_iota(jnp.int32, (n, n), 1)
    return jnp.where(row <= col if upper else row >= col, 1.0, 0.0).astype(f32)


def gap_mask(aux, auxr):
    n = aux.shape[0]
    row = lax.broadcasted_iota(jnp.int32, (n, n), 0)
    col = lax.broadcasted_iota(jnp.int32, (n, n), 1)
    return jnp.where((row >= col) & (aux[:, 4:5] == auxr[0:1, :]), 0.0, FAR).astype(f32)


def states_kernel(
    u_ref, bc_ref, dt_ref, edge_ref, taps_ref, head_ref, aux_ref, ex_ref,
    xs_ref, bcs_ref, lc_ref, lt_ref, dtv_ref, thr_ref, ent_ref, fin_ref,
    halo, state,
):
    c = pl.program_id(0)
    n, inner = xs_ref.shape

    @pl.when(c == 0)
    def _():
        halo[...] = edge_ref[...]
        state[...] = jnp.zeros_like(state)

    aux = aux_ref[...]
    block = jnp.concatenate([u_ref[...], bc_ref[...]], 1)
    pre = conv_pre(block, halo[...], taps_ref, aux)
    halo[...] = block[n - 8 :]
    act = pre * sigmoid(pre)
    xs = act[:, :inner]
    bcs = act[:, inner:].astype(bf16)
    dtv = softplus(dt_ref[...] + head_ref[0:1, :])
    lc = mm(triangle(n), head_ref[1:2, :] * dtv, precision=highest)
    total = lc[n - 1 : n, :]
    xs_ref[...] = xs.astype(bf16)
    bcs_ref[...] = bcs
    lc_ref[...] = lc
    lt_ref[...] = lc.T
    dtv_ref[...] = dtv
    scale = widen(jnp.exp(total - lc) * aux[:, 6:7] * dtv, ex_ref)
    through = jnp.exp(jnp.broadcast_to(total, (8, LANES))) * aux[n - 1 : n, 5:6]
    through = widen(through, ex_ref)
    thr_ref[0] = through
    ent_ref[0] = state[...]
    state[...] = through[0:1, :] * state[...] + mm(
        bcs[:, :STATE], (xs * scale).astype(bf16), TN
    )
    fin_ref[...] = state[...]


def intra_kernel(xs_ref, bcs_ref, lc_ref, lt_ref, dtv_ref, aux_ref, auxr_ref, ex_ref, y_ref):
    inner = xs_ref.shape[1]
    mask = gap_mask(aux_ref[...], auxr_ref[...])
    scores = mm(bcs_ref[:, STATE:], bcs_ref[:, :STATE], NT)
    xd = xs_ref[...].astype(f32) * widen(dtv_ref[...], ex_ref)
    lane = lax.broadcasted_iota(jnp.int32, (1, LANES), 1)
    for p in range(inner // LANES):
        pair = xd[:, p * LANES : (p + 1) * LANES]
        total = None
        for side in range(2):
            h = 2 * p + side
            decay = jnp.exp(lc_ref[:, h : h + 1] - lt_ref[h : h + 1, :] + mask)
            mine = (lane < HEAD_DIM) if side == 0 else (lane >= HEAD_DIM)
            term = mm((decay * scores).astype(bf16), jnp.where(mine, pair, 0.0).astype(bf16))
            total = term if total is None else total + term
        y_ref[:, p * LANES : (p + 1) * LANES] = total


def read_kernel(
    z_ref, yi_ref, xs_ref, bcs_ref, lc_ref, aux_ref, ex_ref, ent_ref, car_ref, thr_ref, rows_ref,
    y_ref, gg_ref, ss_ref, st_ref, pre,
):
    c = pl.program_id(0)

    @pl.when(c == 0)
    def _():
        pre[...] = jnp.ones_like(pre)

    entering = ent_ref[0] + pre[0:1, :] * car_ref[...]
    pre[...] = pre[...] * thr_ref[0]
    st_ref[0] = entering
    read = mm(bcs_ref[:, STATE:], entering.astype(bf16))
    entry = widen(jnp.exp(lc_ref[...]) * aux_ref[:, 5:6], ex_ref)
    y = yi_ref[...] + entry * read + rows_ref[0:1, :] * xs_ref[...].astype(f32)
    z = z_ref[...]
    gated = y * (z * sigmoid(z))
    y_ref[...] = y
    gg_ref[...] = (gated * rows_ref[1:2, :]).astype(bf16)
    ss_ref[...] = jnp.broadcast_to(
        jnp.sum(gated * gated, axis=1, keepdims=True), ss_ref.shape
    )


def gate_back_kernel(
    dg_ref, z_ref, y_ref, c2_ref, rows_ref, xs_ref, bcs_ref, lc_ref, aux_ref, ex_ref, thr_ref,
    dy_ref, dz_ref, lg_ref, fin_ref, acc_ref, run,
):
    @pl.when(pl.program_id(0) == 0)
    def _():
        run[...] = jnp.zeros_like(run)
        acc_ref[...] = jnp.zeros_like(acc_ref)

    z, y, back = z_ref[...], y_ref[...], dg_ref[...]
    sig = sigmoid(z)
    open_ = z * sig
    gated = y * open_
    d_gated = back * rows_ref[1:2, :] - gated * c2_ref[:, 0:1]
    dy = d_gated * open_
    dz_ref[...] = (d_gated * y * (sig * (1.0 + z * (1.0 - sig)))).astype(bf16)
    dy_ref[...] = dy.astype(bf16)
    acc_ref[0:1, :] += jnp.sum(back * gated, axis=0, keepdims=True)
    acc_ref[1:2, :] += jnp.sum(dy * xs_ref[...].astype(f32), axis=0, keepdims=True)
    entry = widen(jnp.exp(lc_ref[...]) * aux_ref[:, 5:6], ex_ref)
    lg_ref[0] = run[...]
    run[...] = thr_ref[0, 0:1, :] * run[...] + mm(
        bcs_ref[:, STATE:], (entry * dy).astype(bf16), TN
    )
    fin_ref[...] = run[...]


def scan_back_kernel(
    u_ref, bc_ref, uh_ref, bch_ref, edge_ref, dt_ref, dz_ref, taps_ref, head_ref, rows_ref, aux_ref, auxr_ref, ex_ref,
    lc_ref, lt_ref, dtv_ref, dy_ref, st_ref, lg_ref, car_ref, thr_ref,
    dp_ref, last_ref, back_ref, tacc_ref, hacc_ref,
    post, nxt, later,
):
    step = pl.program_id(0)
    chunks = pl.num_programs(0)
    n, inner = dy_ref.shape

    @pl.when(step == 0)
    def _():
        post[...] = jnp.ones_like(post)
        nxt[...] = jnp.zeros_like(nxt)
        tacc_ref[...] = jnp.zeros_like(tacc_ref)
        hacc_ref[...] = jnp.zeros_like(hacc_ref)
        later[...] = jnp.zeros_like(later)

    aux = aux_ref[...]
    block = jnp.concatenate([u_ref[...], bc_ref[...]], 1)
    halo = jnp.concatenate([uh_ref[...], bch_ref[...]], 1)
    halo = jnp.where(step == chunks - 1, edge_ref[...], halo)
    shifted = [block] + [aux[:, j : j + 1] * shift_down(block, halo, j) for j in (1, 2, 3)]
    pre = taps_ref[0:1, :] * block
    for j in (1, 2, 3):
        pre = pre + taps_ref[j : j + 1, :] * shifted[j]
    sig = sigmoid(pre)
    act = pre * sig
    slope = sig * (1.0 + pre * (1.0 - sig))
    xs = act[:, :inner]
    bcs = act[:, inner:].astype(bf16)
    keys, queries = bcs[:, :STATE], bcs[:, STATE:]
    lc, dtv = lc_ref[...], dtv_ref[...]
    total = lc[n - 1 : n, :]
    dt_wide = widen(dtv, ex_ref)
    tail_wide = widen(jnp.exp(total - lc) * aux[:, 6:7], ex_ref)
    entry_wide = widen(jnp.exp(lc) * aux[:, 5:6], ex_ref)
    xd = xs * dt_wide
    dy = dy_ref[...]
    dyf = dy.astype(f32)
    entering = st_ref[0]
    leaving = lg_ref[0] + post[0:1, :] * car_ref[...]
    post[...] = post[...] * thr_ref[0]
    ent16, lea16 = entering.astype(bf16), leaving.astype(bf16)

    row = lax.broadcasted_iota(jnp.int32, (n, n), 0)
    col = lax.broadcasted_iota(jnp.int32, (n, n), 1)
    mask = jnp.where((row <= col) & (aux[:, 4:5] == auxr_ref[0:1, :]), 0.0, FAR).astype(f32)
    scores = mm(keys, queries, NT)
    lane = lax.broadcasted_iota(jnp.int32, (1, LANES), 1)
    earlier = jnp.zeros((n, LANES), f32)
    d_scores = jnp.zeros((n, n), f32)
    parts = []
    for p in range(inner // LANES):
        cut = slice(p * LANES, (p + 1) * LANES)
        xd_pair, dy_pair = xd[:, cut].astype(bf16), dyf[:, cut]
        d_pair = None
        for side in range(2):
            h = 2 * p + side
            mine = (lane < HEAD_DIM) if side == 0 else (lane >= HEAD_DIM)
            dy_mine = jnp.where(mine, dy_pair, 0.0).astype(bf16)
            decay = jnp.exp(lt_ref[h : h + 1, :] - lc_ref[:, h : h + 1] + mask)
            weights = decay * scores
            d_weights = mm(xd_pair, dy_mine, NT)
            both = weights * d_weights
            earlier = jnp.where(lane == h, jnp.sum(both, axis=1, keepdims=True), earlier)
            later[h : h + 1, :] = jnp.sum(both, axis=0, keepdims=True)
            d_scores = d_scores + decay * d_weights
            term = mm(weights.astype(bf16), dy_mine)
            d_pair = term if d_pair is None else d_pair + term
        parts.append(d_pair)
    d_scores16 = d_scores.astype(bf16)
    through_lea = tail_wide * mm(keys, lea16)
    dxd = jnp.concatenate(parts, 1) + through_lea
    dxs = dt_wide * dxd + rows_ref[0:1, :] * dyf
    entry_dy = entry_wide * dyf
    d_queries = mm(d_scores16, keys, TN) + mm(entry_dy.astype(bf16), ent16, NT)
    d_keys = mm(d_scores16, queries) + mm((tail_wide * xd).astype(bf16), lea16, NT)
    d_act = jnp.concatenate([dxs, d_keys, d_queries], 1)
    dpre = d_act * slope

    into = head_sums(entry_dy * mm(queries, ent16), ex_ref)
    outof = head_sums(xd * through_lea, ex_ref)
    ends = head_sums(
        jnp.sum(entering * leaving, axis=0, keepdims=True) * thr_ref[0], ex_ref
    )
    d_log = later[...].T - earlier + into - outof
    row = lax.broadcasted_iota(jnp.int32, (n, 1), 0)
    d_log = d_log + jnp.where(
        row == n - 1, jnp.sum(outof, axis=0, keepdims=True) + ends[0:1, :], 0.0
    )
    d_rate = mm(triangle(n, True), d_log, precision=highest)
    d_dt = head_sums(xs * dxd, ex_ref) + d_rate * head_ref[1:2, :]
    d_step = d_dt * sigmoid(dt_ref[...] + head_ref[0:1, :])
    hacc_ref[0:1, :] += jnp.sum(d_rate * dtv, axis=0, keepdims=True) * head_ref[1:2, :]
    hacc_ref[1:2, :] += jnp.sum(d_step, axis=0, keepdims=True)

    d_block = taps_ref[0:1, :] * dpre
    tacc_ref[0:1, :] += jnp.sum(dpre * block, axis=0, keepdims=True)
    before = jnp.zeros((8, block.shape[1]), f32)
    row8 = lax.broadcasted_iota(jnp.int32, (8, 1), 0)
    for j in (1, 2, 3):
        tacc_ref[j : j + 1, :] += jnp.sum(dpre * shifted[j], axis=0, keepdims=True)
        lagged = taps_ref[j : j + 1, :] * (dpre * aux[:, j : j + 1])
        d_block = d_block + shift_up(lagged, nxt[j - 1], j)
        nxt[j - 1] = lagged[:8]
        before = before + jnp.where(row8 >= 8 - j, pltpu.roll(lagged[:8], 8 - j, 0), 0.0)
    back_ref[...] = before

    @pl.when(step == 0)
    def _():
        last_ref[...] = d_block[n - 8 :]

    dp_ref[:, :inner] = dz_ref[...]
    dp_ref[:, inner : inner + block.shape[1]] = d_block.astype(bf16)
    ends_at = inner + block.shape[1] + LANES
    dp_ref[:, inner + block.shape[1] : ends_at] = d_step.astype(bf16)
    dp_ref[:, ends_at:] = jnp.zeros((n, LANES), bf16)


def sds(shape, dtype):
    return jax.ShapeDtypeStruct(shape, dtype)


def params(mib):
    return pltpu.CompilerParams(
        dimension_semantics=("arbitrary",), vmem_limit_bytes=mib * 1024 * 1024
    )


def whole(shape):
    return pl.BlockSpec(shape, lambda c: (0,) * len(shape))


def mixer_specs(rows, inner, reverse):
    chunks = rows // CHUNK
    at = (lambda c: chunks - 1 - c) if reverse else (lambda c: c)
    return {
        "uh": pl.BlockSpec(
            (8, inner), lambda c: (jnp.maximum(at(c) * (CHUNK // 8) - 1, 0), 0)
        ),
        "bch": pl.BlockSpec(
            (8, 2 * STATE),
            lambda c: (jnp.maximum(at(c) * (CHUNK // 8) - 1, 0), inner // (2 * STATE)),
        ),
        "bc": pl.BlockSpec((CHUNK, 2 * STATE), lambda c: (at(c), inner // (2 * STATE))),
        "dt": pl.BlockSpec((CHUNK, LANES), lambda c: (at(c), (inner + 2 * STATE) // LANES)),
        "wide": pl.BlockSpec((CHUNK, inner), lambda c: (at(c), 0)),
        "bcs": pl.BlockSpec((CHUNK, 2 * STATE), lambda c: (at(c), 0)),
        "col": pl.BlockSpec((CHUNK, LANES), lambda c: (at(c), 0)),
        "lt": pl.BlockSpec((LANES, CHUNK), lambda c: (0, at(c))),
        "auxr": pl.BlockSpec((8, CHUNK), lambda c: (0, at(c))),
        "state": pl.BlockSpec((1, STATE, inner), lambda c: (at(c), 0, 0)),
        "thr": pl.BlockSpec((1, 8, inner), lambda c: (at(c), 0, 0)),
        "dp": pl.BlockSpec((CHUNK, 2 * inner + 2 * STATE + 2 * LANES), lambda c: (at(c), 0)),
        "edge": whole((8, inner + 2 * STATE)),
        "head": whole((8, LANES)),
        "rows": whole((8, inner)),
        "ex": whole((2 * LANES, inner)),
        "one": whole((STATE, inner)),
    }


def mixer_states(pu, edge, taps, head, aux, ex, inner):
    rows = pu.shape[0]
    chunks = rows // CHUNK
    s = mixer_specs(rows, inner, False)
    return pl.pallas_call(
        states_kernel,
        grid=(chunks,),
        in_specs=[
            s["wide"], s["bc"], s["dt"], s["edge"], s["edge"], s["head"], s["col"], s["ex"],
        ],
        out_specs=[
            s["wide"], s["bcs"], s["col"], s["lt"], s["col"], s["thr"], s["state"], s["one"],
        ],
        out_shape=[
            sds((rows, inner), bf16),
            sds((rows, 2 * STATE), bf16),
            sds((rows, LANES), f32),
            sds((LANES, rows), f32),
            sds((rows, LANES), f32),
            sds((chunks, 8, inner), f32),
            sds((chunks, STATE, inner), f32),
            sds((STATE, inner), f32),
        ],
        scratch_shapes=[
            pltpu.VMEM((8, inner + 2 * STATE), f32),
            pltpu.VMEM((STATE, inner), f32),
        ],
        compiler_params=params(32),
        name="mixer_states",
    )(pu, pu, pu, edge, taps, head, aux, ex)


def mixer_intra(xs, bcs, lc, lt, dtv, aux, auxr, ex):
    rows, inner = xs.shape
    s = mixer_specs(rows, inner, False)
    return pl.pallas_call(
        intra_kernel,
        grid=(rows // CHUNK,),
        in_specs=[
            s["wide"], s["bcs"], s["col"], s["lt"], s["col"], s["col"], s["auxr"], s["ex"],
        ],
        out_specs=s["wide"],
        out_shape=sds((rows, inner), f32),
        compiler_params=params(32),
        name="mixer_intra",
    )(xs, bcs, lc, lt, dtv, aux, auxr, ex)


def mixer_read(pz, yi, xs, bcs, lc, aux, ex, ent, carried, thr, head_rows):
    rows, inner = xs.shape
    chunks = rows // CHUNK
    s = mixer_specs(rows, inner, False)
    return pl.pallas_call(
        read_kernel,
        grid=(chunks,),
        in_specs=[
            s["wide"], s["wide"], s["wide"], s["bcs"], s["col"], s["col"], s["ex"],
            s["state"], s["one"], s["thr"], s["rows"],
        ],
        out_specs=[s["wide"], s["wide"], s["col"], s["state"]],
        out_shape=[
            sds((rows, inner), f32),
            sds((rows, inner), bf16),
            sds((rows, LANES), f32),
            sds((chunks, STATE, inner), f32),
        ],
        scratch_shapes=[pltpu.VMEM((8, inner), f32)],
        compiler_params=params(32),
        name="mixer_read",
    )(pz, yi, xs, bcs, lc, aux, ex, ent, carried, thr, head_rows)


def mixer_gate_back(dg, pz, y, c2, head_rows, xs, bcs, lc, aux, ex, thr):
    rows, inner = xs.shape
    chunks = rows // CHUNK
    s = mixer_specs(rows, inner, True)
    return pl.pallas_call(
        gate_back_kernel,
        grid=(chunks,),
        in_specs=[
            s["wide"], s["wide"], s["wide"], s["col"], s["rows"], s["wide"], s["bcs"],
            s["col"], s["col"], s["ex"], s["thr"],
        ],
        out_specs=[s["wide"], s["wide"], s["state"], s["one"], s["rows"]],
        out_shape=[
            sds((rows, inner), bf16),
            sds((rows, inner), bf16),
            sds((chunks, STATE, inner), f32),
            sds((STATE, inner), f32),
            sds((8, inner), f32),
        ],
        scratch_shapes=[pltpu.VMEM((STATE, inner), f32)],
        compiler_params=params(40),
        name="mixer_gate_back",
    )(dg, pz, y, c2, head_rows, xs, bcs, lc, aux, ex, thr)


def mixer_scan_back(
    pu, edge, dz, taps, head, head_rows, aux, auxr, ex, lc, lt, dtv, dy, st, lg, carried, thr
):
    rows, inner = dy.shape
    chunks = rows // CHUNK
    s = mixer_specs(rows, inner, True)
    wide = inner + 2 * STATE
    return pl.pallas_call(
        scan_back_kernel,
        grid=(chunks,),
        in_specs=[
            s["wide"], s["bc"], s["uh"], s["bch"], s["edge"], s["dt"], s["wide"], s["edge"],
            s["head"], s["rows"], s["col"], s["auxr"], s["ex"], s["col"], s["lt"], s["col"], s["wide"], s["state"], s["state"],
            s["one"], s["thr"],
        ],
        out_specs=[s["dp"], s["edge"], s["edge"], s["edge"], s["head"]],
        out_shape=[
            sds((rows, wide + inner + 2 * LANES), bf16),
            sds((8, wide), f32),
            sds((8, wide), f32),
            sds((8, wide), f32),
            sds((8, LANES), f32),
        ],
        scratch_shapes=[
            pltpu.VMEM((8, inner), f32),
            pltpu.VMEM((3, 8, wide), f32),
            pltpu.VMEM((LANES, CHUNK), f32),
        ],
        compiler_params=params(48),
        name="mixer_scan_back",
    )(
        pu, pu, pu, pu, edge, pu, dz, taps, head, head_rows, aux, auxr, ex, lc, lt, dtv, dy, st,
        lg, carried, thr,
    )


def up_kernel(at_ref, x_ref, w_ref, router_ref, named_ref, pat_ref, *refs):
    h_ref, act_ref, gates_ref, cols = refs[-4:]

    @pl.when(pl.program_id(0) == 0)
    def _():
        logits = mm(x_ref[...], router_ref[...], NT)
        mask = named_ref[...] > 0
        peak = jnp.max(jnp.where(mask, logits, FAR), axis=1, keepdims=True)
        raised = jnp.where(mask, jnp.exp(jnp.where(mask, logits - peak, 0.0)), 0.0)
        gates = raised / jnp.sum(raised, axis=1, keepdims=True)
        gates_ref[...] = gates
        cols[...] = gate_columns(gates)

    hidden = mm(x_ref[...], w_ref[...])
    g, w = hidden[:, :FF_BLOCK], hidden[:, FF_BLOCK:]
    gate = mm(cols[...], pat_ref[...])
    h_ref[...] = hidden.astype(bf16)
    act_ref[...] = (g * sigmoid(g) * w * gate).astype(bf16)


def gate_columns(gates):
    lane = lax.broadcasted_iota(jnp.int32, gates.shape, 1)
    high, low = split16(jnp.where(lane == LANES - 1, 1.0, gates))
    return jnp.concatenate([high, low], 1)


def down_back_kernel(at_ref, gs_ref, w_ref, h_ref, gates_ref, pat_ref, *refs):
    dh_ref, dgate_ref, cols = refs[-3:]

    @pl.when(pl.program_id(0) == 0)
    def _():
        dgate_ref[...] = jnp.zeros_like(dgate_ref)
        cols[...] = gate_columns(gates_ref[...])

    for start in range(0, gs_ref.shape[0], ROW_TILE):
        cut = slice(start, start + ROW_TILE)
        q = mm(gs_ref[cut, :], w_ref[...], NT)
        g = h_ref[cut, :FF_BLOCK].astype(f32)
        w = h_ref[cut, FF_BLOCK:].astype(f32)
        sig = sigmoid(g)
        opened = g * sig
        gate = mm(cols[cut, :], pat_ref[...])
        dgate_ref[cut, :] += mm((opened * w * q).astype(bf16), pat_ref[:LANES, :], NT)
        d_act = gate * q
        dh_ref[cut, :FF_BLOCK] = (d_act * w * (sig * (1.0 + g * (1.0 - sig)))).astype(bf16)
        dh_ref[cut, FF_BLOCK:] = (d_act * opened).astype(bf16)


def in_place(state, inputs):
    held = [] if state is None else list(state)
    specs = [pl.BlockSpec(memory_space=pl.ANY)] * len(held)
    return held, specs, {inputs + 1 + i: i for i in range(len(held))}


def experts_up(x, at, w_up, router_w, named, pattern, state):
    own, depth = x.shape
    rows = named.shape[0]
    blocks = w_up.shape[1] // (2 * FF_BLOCK)
    held, specs, aliases = in_place(state, 5)
    return pl.pallas_call(
        up_kernel,
        grid_spec=pltpu.PrefetchScalarGridSpec(
            num_scalar_prefetch=1,
            grid=(blocks,),
            in_specs=[
                pl.BlockSpec((own, depth), lambda i, at: (0, 0)),
                pl.BlockSpec((depth, 2 * FF_BLOCK), lambda i, at: (0, i)),
                pl.BlockSpec((LANES, depth), lambda i, at: (0, 0)),
                pl.BlockSpec((own, LANES), lambda i, at: (at[0], 0)),
                pl.BlockSpec((2 * LANES, FF_BLOCK), lambda i, at: (0, i)),
            ]
            + specs,
            out_specs=[
                pl.BlockSpec((own, 2 * FF_BLOCK), lambda i, at: (at[0], i)),
                pl.BlockSpec((own, FF_BLOCK), lambda i, at: (at[0], i)),
                pl.BlockSpec((own, LANES), lambda i, at: (at[0], 0)),
            ],
            scratch_shapes=[pltpu.VMEM((own, 2 * LANES), bf16)],
        ),
        out_shape=[
            sds((rows, 2 * FF_BLOCK * blocks), bf16),
            sds((rows, FF_BLOCK * blocks), bf16),
            sds((rows, LANES), f32),
        ],
        input_output_aliases=aliases,
        compiler_params=params(58),
        name="experts_up",
    )(at.astype(jnp.int32).reshape(1), x, w_up, router_w, named, pattern, *held)


def experts_down_back(gs, at, w_down, hidden, gates, pattern, state):
    depth = gs.shape[1]
    rows = hidden.shape[0]
    own = gs.shape[0]
    blocks = w_down.shape[0] // FF_BLOCK
    held, specs, aliases = in_place(state, 5)
    return pl.pallas_call(
        down_back_kernel,
        grid_spec=pltpu.PrefetchScalarGridSpec(
            num_scalar_prefetch=1,
            grid=(blocks,),
            in_specs=[
                pl.BlockSpec((own, depth), lambda i, at: (0, 0)),
                pl.BlockSpec((FF_BLOCK, depth), lambda i, at: (i, 0)),
                pl.BlockSpec((own, 2 * FF_BLOCK), lambda i, at: (at[0], i)),
                pl.BlockSpec((own, LANES), lambda i, at: (at[0], 0)),
                pl.BlockSpec((2 * LANES, FF_BLOCK), lambda i, at: (0, i)),
            ]
            + specs,
            out_specs=[
                pl.BlockSpec((own, 2 * FF_BLOCK), lambda i, at: (at[0], i)),
                pl.BlockSpec((own, LANES), lambda i, at: (at[0], 0)),
            ],
            scratch_shapes=[pltpu.VMEM((own, 2 * LANES), bf16)],
        ),
        out_shape=[
            sds((rows, 2 * FF_BLOCK * blocks), bf16),
            sds((rows, LANES), f32),
        ],
        input_output_aliases=aliases,
        compiler_params=params(32 if own == rows else 58),
        name="experts_down_back",
    )(at.astype(jnp.int32).reshape(1), gs, w_down, hidden, gates, pattern, *held)


def row_norm(values):
    return lax.rsqrt(jnp.mean(values * values, axis=-1, keepdims=True) + epsilon)


def norm_back(values, inverse, gain, grad):
    weighted = grad * gain
    mean = jnp.mean(weighted * values, axis=-1, keepdims=True)
    return inverse * weighted - values * (inverse * inverse * inverse * mean)


def pad_rows(parts, rows, width):
    value = jnp.concatenate([jnp.atleast_2d(part) for part in parts], 0)
    return jnp.pad(value, ((0, rows - value.shape[0]), (0, width - value.shape[1])))


def to_line(column):
    value = column.reshape(-1, LANES)
    return jnp.pad(value, ((0, 8 - value.shape[0]), (0, 0)))


def local(
    tokens, inner_proj, step_proj, state_proj, inner_conv, state_conv, decay_log, step_bias,
    skip_gain, gate_gain, outer_proj, norm_gains, router, expert_up, expert_down, shared_up,
    shared_down, routes, packed_lengths, cotangent,
):
    ns, nt = lax.axis_size("seq"), lax.axis_size("tp")
    sq, tp = lax.axis_index("seq"), lax.axis_index("tp")
    layers = inner_proj.shape[0]
    own, depth = tokens.shape
    rows = own * nt
    chunks = rows // CHUNK
    inner = gate_gain.shape[1]
    heads = decay_log.shape[1]
    inner_all = inner * nt
    cut = inner_proj.shape[1]
    fine = state_proj.shape[1]
    devices = ns * nt
    experts = router.shape[2]
    mine = expert_up.shape[1]
    ff = expert_down.shape[2] * ns
    ff_cut = expert_down.shape[2]
    shared = shared_down.shape[1] * ns
    sh_cut = shared_down.shape[1]
    tap_cut = state_conv.shape[2]
    width = inner + 2 * STATE
    hidden_units = mine * ff + shared
    ff_blocks = hidden_units // FF_BLOCK
    per_seq = mine * ff_cut + sh_cut

    ends = jnp.cumsum(packed_lengths, dtype=jnp.int32)
    starts = ends - packed_lengths

    def count(positions):
        return jnp.sum(
            (starts[None, :] <= positions[:, None]).astype(f32), axis=1
        )

    first = sq * rows
    here = first + jnp.arange(rows, dtype=jnp.int32)
    seg = count(here)
    chunk_of = jnp.arange(rows, dtype=jnp.int32) // CHUNK
    lags = [jnp.ones_like(seg)] + [(count(here - j) == seg).astype(f32) for j in (1, 2, 3)]
    alive = (count(first + chunk_of * CHUNK - 1) == seg).astype(f32)
    tail = (count(first + chunk_of * CHUNK + CHUNK - 1) == seg).astype(f32)
    aux = jnp.pad(jnp.stack(lags + [seg, alive, tail], 1), ((0, 0), (0, LANES - 7)))
    auxr = jnp.broadcast_to(seg[None, :], (8, rows))
    lane_head = jnp.arange(inner, dtype=jnp.int32) // HEAD_DIM
    ex_row = jnp.arange(2 * LANES, dtype=jnp.int32)[:, None] % LANES
    ex = (ex_row == lane_head[None, :]).astype(bf16)
    unit = jnp.arange(hidden_units, dtype=jnp.int32) % per_seq
    unit_gate = jnp.where(unit < mine * ff_cut, tp * mine + unit // ff_cut, LANES - 1)
    pat_row = jnp.arange(2 * LANES, dtype=jnp.int32)[:, None] % LANES
    pattern = (pat_row == unit_gate[None, :]).astype(bf16)

    inv1 = row_norm(tokens)
    scaled = (tokens * inv1).astype(bf16)
    smalls, ups = [], []
    for l in range(layers):
        taps_col = jnp.pad(state_conv[l].reshape(-1), (0, fine - 4 * tap_cut))[:, None]
        small = jnp.concatenate([state_proj[l], router[l], norm_gains[l].T, taps_col], 1)
        smalls.append(jnp.pad(small, ((0, 0), (0, 2 * STATE + LANES - small.shape[1]))))
        up = shared_up[l].reshape(fine, 2, ns, nt, sh_cut)
        ups.append(jnp.transpose(up, (3, 0, 1, 2, 4)).reshape(nt, fine, 2 * shared))
    plain, _, riders = hop_both(
        scaled,
        None,
        (jnp.concatenate(smalls, 1), expert_up, jnp.stack(ups, 1), routes, expert_down, shared_down),
    )
    small_all, expert_up, ups, routes, expert_down, shared_down = riders
    small_all = pair_gather(small_all)
    up_all = pair_swap(ups)

    def mixer_weights(l):
        dt_cols = jnp.pad(step_proj[l], ((0, 0), (0, LANES - heads)))
        small = small_all[:, l * (2 * STATE + LANES) : (l + 1) * (2 * STATE + LANES)]
        pack = jnp.concatenate(
            [
                inner_proj[l, :, 0],
                inner_proj[l, :, 1],
                small[:, : 2 * STATE],
                dt_cols,
                small[:, 2 * STATE :],
            ],
            1,
        )
        return pack, outer_proj[l].T

    def over_seq(value):
        return lax.all_gather(value, "seq", axis=0, tiled=True)

    def expert_weights(l):
        halves = jnp.transpose(expert_up[l].reshape(mine, cut, 2, ns, ff_cut), (2, 1, 3, 0, 4))
        halves = halves.reshape(2, cut, ns, mine * ff_cut)
        extra = jnp.transpose(up_all[:, l].reshape(cut, 2, ns, sh_cut), (1, 0, 2, 3))
        halves = jnp.concatenate([halves, extra], 3).reshape(2, cut, ff_blocks, FF_BLOCK)
        local_up = jnp.transpose(halves, (1, 2, 0, 3)).reshape(cut, 2 * hidden_units)
        local_down = jnp.concatenate(
            [expert_down[l].reshape(mine * ff_cut, depth), shared_down[l]], 0
        )
        return local_up, local_down

    packs = [list(mixer_weights(l) + expert_weights(l)) for l in range(layers)]
    plain, *packs[0][2:] = tie(plain, *packs[0][2:])
    w_in, w_out, w_up, w_down = [[None] * layers for _ in range(4)]
    w_in[0], w_out[0] = over_seq(packs[0][0]), over_seq(packs[0][1])

    named = jnp.any(
        routes[:, :, :, None] == jnp.arange(experts, dtype=jnp.int32), axis=2
    ).astype(bf16)
    named = pair_gather(
        jnp.transpose(named, (1, 0, 2)).reshape(own, layers * experts)
    ).reshape(rows, layers, experts)
    named = jnp.pad(named, ((0, 0), (0, 0), (0, LANES - experts))).astype(f32)

    residual = tokens
    saved = []
    last_cot = None
    for l in range(layers):
        small_in = tie(w_in[l][:, inner + width + LANES :].astype(f32).T)[0]
        router_w = jnp.pad(small_in[:experts], ((0, LANES - experts), (0, 0))).astype(bf16)
        gain1 = small_in[experts]
        gain2 = small_in[experts + 1]
        taps_bc = small_in[experts + 2].reshape(devices, fine)[:, : 4 * tap_cut]
        taps_bc = jnp.transpose(taps_bc.reshape(devices, 4, tap_cut), (1, 0, 2))
        taps_bc = taps_bc.reshape(4, 2 * STATE)
        taps = jnp.pad(
            jnp.concatenate([inner_conv[l], taps_bc], 1), ((0, 4), (0, 0))
        )
        head = pad_rows([step_bias[l], -jnp.exp(decay_log[l])], 8, LANES)
        head_rows = pad_rows([jnp.repeat(skip_gain[l], HEAD_DIM), gate_gain[l]], 8, inner)

        if l > 0:
            inv1 = row_norm(residual)
            scaled = (residual * inv1).astype(bf16)
            plain = hop_gather(scaled)
        normed = (plain.astype(f32) * gain1).astype(bf16)
        pu = mm(normed, w_in[l][:, inner : inner + width + LANES])
        edge = shift_seq(pu[rows - 8 :, :width], 1)
        xs, bcs, lc, lt, dtv, thr, ent, fin = mixer_states(pu, edge, taps, head, aux, ex, inner)
        through = thr[0, 0:1]
        for c in range(1, chunks):
            through = through * thr[c, 0:1]
        pz = mm(normed, w_in[l][:, :inner])
        yi = mixer_intra(xs, bcs, lc, lt, dtv, aux, auxr, ex)
        carried, pz, yi = carried_state(through, fin, 1, pz, yi)
        cot16 = cotangent.astype(bf16)
        if l == 0:
            carried, cot16 = tie(carried, cot16)
        carried, up_pack, down_pack = tie(carried, packs[l][2], packs[l][3])
        w_up[l], w_down[l] = over_seq(up_pack), over_seq(down_pack)
        y, gg, ss, st = mixer_read(pz, yi, xs, bcs, lc, aux, ex, ent, carried, thr, head_rows)
        squares = pair_total(ss[:, 0].reshape(rows // LANES, LANES), "tp")
        squares = lax.dynamic_slice_in_dim(
            squares, tp * (own // LANES), own // LANES, 0
        ).reshape(own)
        partial_out = mm(gg, w_out[l], NT).astype(bf16)
        if l == 0:
            last_cot, out_sum, (squares,) = hop_both(cot16, partial_out, (squares,))
            out_sum, last_cot = tie(out_sum, last_cot)
        else:
            _, out_sum, (squares,) = hop_both(None, partial_out, (squares,))
        inv_gate = lax.rsqrt(squares / inner_all + epsilon)
        mixed = inv_gate[:, None] * out_sum
        mid = residual + mixed

        inv2 = row_norm(mid)
        moe_own = (mid * inv2 * gain2).astype(bf16)
        mask = named[:, l]

        def up_block(block, at, state):
            return experts_up(block, at, w_up[l], router_w, mask, pattern, state)

        moe_in, (hidden, act, gates) = gather_work(moe_own, up_block)
        if l < layers - 1:
            act, *packs[l + 1][:2] = tie(act, *packs[l + 1][:2])
            w_in[l + 1], w_out[l + 1] = over_seq(packs[l + 1][0]), over_seq(packs[l + 1][1])
        saved.append(
            dict(
                router_w=router_w, gain1=gain1, gain2=gain2, taps=taps, head=head,
                head_rows=head_rows, residual=residual, inv1=inv1, plain=plain, normed=normed,
                pu=pu, pz=pz, edge=edge, xs=xs, bcs=bcs, lc=lc, lt=lt, dtv=dtv, thr=thr,
                through=through, y=y, gg=gg, st=st, inv_gate=inv_gate, mixed=mixed,
                mid=mid, inv2=inv2, moe_own=moe_own, moe_in=moe_in, gates=gates,
                hidden=hidden, act=act,
            )
        )
        if l < layers - 1:

            moe_out = hop_scatter(mm(act, w_down[l]).astype(bf16))
            moe_out, *packs[l + 1][2:] = tie(moe_out, *packs[l + 1][2:])
            residual = mid + moe_out

    def finish(r):
        late, early, sums = r["late"], r["early"], r["sums"]
        halves = r["up"].reshape(cut, ff_blocks, 2, FF_BLOCK)
        halves = jnp.transpose(halves, (2, 0, 1, 3)).reshape(2, cut, ns, per_seq)
        mine_up = halves[..., : mine * ff_cut].reshape(2, cut, ns, mine, ff_cut)
        mine_up = jnp.transpose(mine_up, (3, 1, 0, 2, 4)).reshape(mine, cut, 2 * ff)
        mine_up = row_major(mine_up)
        shared_cols = jnp.transpose(halves[..., mine * ff_cut :], (1, 0, 2, 3))
        shared_grad = pair_swap(shared_cols.reshape(nt, fine, 2 * shared))
        shared_grad = jnp.transpose(
            shared_grad.reshape(nt, fine, 2, ns, sh_cut), (1, 2, 3, 0, 4)
        ).reshape(fine, -1)
        common = pair_scatter(late[:, inner:])
        small = common[:, 2 * STATE + heads :]
        return [
            jnp.stack([early[:, inner:], late[:, :inner]], 1),
            late[:, width : width + heads].astype(f32),
            common[:, : 2 * STATE],
            sums[:4],
            small[: 4 * tap_cut, experts + 2].reshape(4, tap_cut),
            sums[6, :heads],
            sums[6, LANES : LANES + heads],
            jnp.sum(sums[5].reshape(heads, HEAD_DIM), axis=1),
            sums[4],
            early[:, :inner].T,
            jnp.transpose(small[:, experts : experts + 2]),
            small[:, :experts],
            mine_up,
            r["down"][: mine * ff_cut].reshape(mine, ff_cut, depth),
            shared_grad,
            r["down"][mine * ff_cut :],
        ]

    grad = cotangent
    finished = [None] * layers
    for l in reversed(range(layers)):
        k = saved[l]
        top = l == layers - 1
        state = None

        def back_block(block, at, state):
            return experts_down_back(
                block, at, w_down[l], k["hidden"], k["gates"], pattern, state
            )

        def gate_sums():
            lines = state[1][:, :experts].reshape(rows // per_line, LANES)
            return pair_total(lines, "tp")

        per_line = LANES // experts
        if top:
            gs = last_cot
            last_out = mm(k["act"], w_down[l]).astype(bf16)
            state = back_block(gs, jnp.int32(0), None)
        else:
            gs, state = gather_work(grad.astype(bf16), back_block)
            first, above["late"] = tie(state[0], above["late"])
            state = (first, state[1])
        d_hidden = state[0]
        up_part = mm(k["moe_in"], d_hidden, TN).astype(bf16)
        _, d_moe, (d_gate_all, up_part) = hop_both(
            None, mm(d_hidden, w_up[l], NT).astype(bf16), (gate_sums(), up_part)
        )
        up_grad = lax.psum_scatter(up_part, "seq", scatter_dimension=0, tiled=True)
        down_part = mm(k["act"], gs, TN).astype(bf16)
        if top:
            d_moe, last_out = tie(d_moe, last_out)
        d_gate_own = lax.dynamic_slice_in_dim(
            d_gate_all, tp * (own // per_line), own // per_line, 0
        ).reshape(own, experts)
        d_gate_own = jnp.pad(d_gate_own, ((0, 0), (0, LANES - experts)))
        gates_own = lax.dynamic_slice_in_dim(k["gates"], tp * own, own, 0)
        d_logits = gates_own * (
            d_gate_own - jnp.sum(gates_own * d_gate_own, axis=1, keepdims=True)
        )
        d_logits16 = d_logits.astype(bf16)
        router_grad = mm(k["moe_own"], d_logits16, TN)[:, :experts]
        d_moe = d_moe + mm(d_logits16, k["router_w"])
        gain2_grad = jnp.sum(d_moe * k["mid"] * k["inv2"], axis=0)
        grad_mid = grad + norm_back(k["mid"], k["inv2"], k["gain2"], d_moe)

        inv_gate = k["inv_gate"]
        cross = inv_gate * inv_gate * jnp.sum(grad_mid * k["mixed"], axis=1) / inner_all
        cross_all = pair_gather(to_line(cross)).reshape(nt, 8 * LANES)[:, :own].reshape(rows)
        send = (grad_mid * inv_gate[:, None]).astype(bf16)
        if top:
            d_mixed, moe_out, riders = hop_both(send, last_out, (cross_all, down_part))
            residual = k["mid"] + moe_out
        else:
            d_mixed, _, riders = hop_both(send, None, (cross_all, down_part))
        cross_all, down_part = riders
        down_grad = lax.psum_scatter(down_part, "seq", scatter_dimension=0, tiled=True)
        c2 = jnp.broadcast_to(cross_all[:, None], (rows, LANES))
        dg = mm(d_mixed, w_out[l])
        dy, dz, lg, fin, acc = mixer_gate_back(
            dg, k["pz"], k["y"], c2, k["head_rows"], k["xs"], k["bcs"], k["lc"], aux, ex, k["thr"]
        )
        early_out = row_major(mm(d_mixed, k["gg"], TN).astype(bf16))
        early_z = row_major(mm(k["normed"], dz, TN).astype(bf16))
        carried, early_out, early_z = carried_state(k["through"], fin, -1, early_out, early_z)
        early = jnp.concatenate([early_out, early_z], 1)
        carried, early, up_grad = tie(carried, early, up_grad)
        if top:
            carried, residual = tie(carried, residual)
        early = lax.psum_scatter(early, "seq", scatter_dimension=0, tiled=True)
        dp, last, back, tacc, hacc = mixer_scan_back(
            k["pu"], k["edge"], dz, k["taps"], k["head"], k["head_rows"], aux, auxr, ex,
            k["lc"], k["lt"], k["dtv"], dy, k["st"], lg, carried, k["thr"],
        )
        last = (last + shift_seq(back, -1)).astype(bf16)
        dp = lax.dynamic_update_slice(dp, last, (rows - 8, inner))
        dp, down_grad = tie(dp, down_grad)
        d_normed = mm(dp, w_in[l], NT)
        gain1_grad = jnp.sum(d_normed * k["plain"].astype(f32), axis=0)
        taps_col = jnp.transpose(tacc[:4, inner:].reshape(4, devices, tap_cut), (1, 0, 2))
        taps_col = jnp.pad(taps_col.reshape(devices, 4 * tap_cut), ((0, 0), (0, fine - 4 * tap_cut)))
        small = jnp.concatenate(
            [router_grad, gain1_grad[:, None], gain2_grad[:, None], taps_col.reshape(-1)[:, None]],
            1,
        )
        late = mm(k["normed"], dp[:, inner : inner + width + LANES], TN).astype(bf16)
        block = late[:, width:] + jnp.pad(
            small, ((0, 0), (heads, LANES - heads - small.shape[1]))
        ).astype(bf16)
        late = lax.dynamic_update_slice(late, block, (0, width))
        sums = jnp.concatenate(
            [tacc[:4, :inner], acc[:2], pad_rows([hacc[:2].reshape(-1)], 2, inner)], 0
        )
        names = ("up", "down", "early", "sums")
        now = dict(up=up_grad, down=down_grad, early=early, sums=sums)
        held = [late]
        if not top:
            held += [now[name] for name in names] + [above[name] for name in names]
            held += [above["late"]]
        _, d_own, riders = hop_both(None, d_normed.astype(bf16), held)
        late = lax.psum_scatter(riders[0], "seq", scatter_dimension=0, tiled=True)
        if top:
            d_own, now["early"] = tie(d_own, early)
        else:
            now.update(zip(names, riders[1:5]))
            above.update(zip(names, riders[5:9]))
            above["late"] = riders[9]
            both = pair_total(jnp.concatenate([now["sums"], above["sums"]], 0), "seq")
            now["sums"], above["sums"] = both[: sums.shape[0]], both[sums.shape[0] :]
            finished[l + 1] = finish(above)
        grad = grad_mid + norm_back(k["residual"], k["inv1"], k["gain1"], d_own)
        above = dict(now, late=late)

    finished[0] = finish(above)
    stacked = [jnp.stack([part[i] for part in finished], 0).astype(f32) for i in range(16)]
    return (residual, grad, *stacked)


def solution(mesh):
    both = ("seq", "tp")
    in_specs = (
        P(both, None),
        P(None, "seq", None, "tp"),
        P(None, "seq", "tp"),
        P(None, both, None),
        P(None, None, "tp"),
        P(None, None, both),
        P(None, "tp"),
        P(None, "tp"),
        P(None, "tp"),
        P(None, "tp"),
        P(None, "tp", "seq"),
        P(None, None, both),
        P(None, both, None),
        P(None, "tp", "seq", None),
        P(None, "tp", "seq", None),
        P(None, both, None),
        P(None, both, None),
        P(None, both, None),
        P(),
        P(both, None),
    )
    out_specs = (
        P(both, None),
        P(both, None),
        P(None, "seq", None, "tp"),
        P(None, "seq", "tp"),
        P(None, both, None),
        P(None, None, "tp"),
        P(None, None, both),
        P(None, "tp"),
        P(None, "tp"),
        P(None, "tp"),
        P(None, "tp"),
        P(None, "tp", "seq"),
        P(None, None, both),
        P(None, both, None),
        P(None, "tp", "seq", None),
        P(None, "tp", "seq", None),
        P(None, both, None),
        P(None, both, None),
    )
    return jax.shard_map(local, mesh=mesh, in_specs=in_specs, out_specs=out_specs, check_vma=False)
```

```python
from functools import partial

import jax
import jax.numpy as jnp
from jax import lax
from jax.experimental import pallas as pl
from jax.experimental.layout import Layout, with_layout_constraint
from jax.experimental.pallas import tpu as pltpu
from jax.sharding import PartitionSpec as P

HEAD_DIM = 64
STATE = 128
TOP = 6
CHUNK = 256
LANES = 128
FF_BLOCK = 256
ROW_TILE = 256
FAR = -1e30

epsilon = 1e-05
highest = lax.Precision.HIGHEST
bf16 = jnp.bfloat16
f32 = jnp.float32

NN = (((1,), (0,)), ((), ()))
NT = (((1,), (1,)), ((), ()))
TN = (((0,), (0,)), ((), ()))


def mm(a, b, dims=NN, precision=None):
    return lax.dot_general(a, b, dims, precision=precision, preferred_element_type=f32)


def row_major(value):
    return with_layout_constraint(value, Layout(tuple(range(value.ndim))))


def tie(*values):
    return lax.optimization_barrier(values)


def hop_both(v, x, riders=(), last=(), axis="tp"):
    n, me = lax.axis_size(axis), lax.axis_index(axis)
    riders, last = tuple(riders), tuple(last)
    rel = {0: v}
    ahead = right = left = None
    if v is not None:
        ahead = (v, v)
    if x is not None:
        rows = x.shape[0] // n

        def piece(k):
            return lax.dynamic_slice_in_dim(x, jnp.clip(k, 0, n - 1) * rows, rows, 0)

        right, left = piece(n - 1 + me), piece(me - (n - 1))
    lead = 1 if v is not None and x is not None else 0
    for step in range(1, n + lead):
        held = []
        gathers, scatters = ahead is not None and step < n, right is not None and step > lead
        if gathers:
            held += list(ahead)
        if scatters:
            held += [right, left]
        if step > 1:
            count = len(held)
            extra = riders if step == 2 else last if step == n + lead - 1 else ()
            held = list(tie(*held, *extra))
            if step == 2:
                riders = tuple(held[count:])
            elif extra:
                last = tuple(held[count:])
            held = held[:count]
        if gathers:
            ahead = (
                lax.ppermute(held[0], axis, [(i, i + 1) for i in range(step - 1, n - 1)]),
                lax.ppermute(held[1], axis, [(i, i - 1) for i in range(1, n - step + 1)]),
            )
            rel[-step], rel[step] = ahead
            held = held[2:]
        if scatters:
            s = step - lead
            right = lax.ppermute(held[0], axis, [(i, i + 1) for i in range(0, s)])
            left = lax.ppermute(held[1], axis, [(i, i - 1) for i in range(n - s, n)])
            if s < n - 1:
                right = (right.astype(f32) + piece(n - 1 - s + me).astype(f32)).astype(x.dtype)
                left = (left.astype(f32) + piece(me - (n - 1 - s)).astype(f32)).astype(x.dtype)
    gathered = total = None
    if v is not None:
        outs = []
        for j in range(n):
            out = rel[j]
            for m in range(1, n):
                out = jnp.where(me == m, rel[j - m], out)
            outs.append(out)
        gathered = jnp.concatenate(outs, 0)
    if x is not None:
        total = piece(me).astype(f32) + right.astype(f32) + left.astype(f32)
    return gathered, total, riders + last


def choose(options, me):
    out = options[0]
    for m in range(1, len(options)):
        out = jnp.where(me == m, options[m], out)
    return out


def gather_work(v, work, axis="tp"):
    n, me = lax.axis_size(axis), lax.axis_index(axis)
    near = [sorted((j for j in range(n) if j != m), key=lambda j: abs(j - m)) for m in range(n)]
    right = left = block = v
    at, state, rel = me, None, {0: v}
    for d in range(1, n):
        right = lax.ppermute(right, axis, [(i, i + 1) for i in range(d - 1, n - 1)])
        left = lax.ppermute(left, axis, [(i, i - 1) for i in range(1, n - d + 1)])
        state = work(block, at, state)
        right, left, *state = tie(right, left, *state)
        rel[-d], rel[d] = right, left
        block = choose([rel[near[m][d - 1] - m] for m in range(n)], me)
        at = choose([near[m][d - 1] for m in range(n)], me)
    state = work(block, at, state)
    whole_v = jnp.concatenate(
        [choose([rel[j - m] for m in range(n)], me) for j in range(n)], 0
    )
    return whole_v, state


def hop_gather(v):
    return hop_both(v, None)[0]


def hop_scatter(x):
    return hop_both(None, x)[1]


def pair_total(v, axis):
    n = lax.axis_size(axis)
    bit = 1
    while bit < n:
        v = v + lax.ppermute(v, axis, [(i, i ^ bit) for i in range(n)])
        bit *= 2
    return v


def pair_gather(v, axis="tp"):
    n, me = lax.axis_size(axis), lax.axis_index(axis)
    bit = 1
    while bit < n:
        other = lax.ppermute(v, axis, [(i, i ^ bit) for i in range(n)])
        high = (me & bit) > 0
        v = jnp.concatenate([jnp.where(high, other, v), jnp.where(high, v, other)], 0)
        bit *= 2
    return v


def pair_scatter(v, axis="tp"):
    n, me = lax.axis_size(axis), lax.axis_index(axis)
    bit = n // 2
    while bit:
        half = v.shape[0] // 2
        side = (me & bit) > 0
        first, second = v[:half], v[half:]
        got = lax.ppermute(
            jnp.where(side, first, second), axis, [(i, i ^ bit) for i in range(n)]
        )
        v = jnp.where(side, second, first).astype(f32) + got.astype(f32)
        v = v.astype(first.dtype) if bit > 1 else v
        bit //= 2
    return v


def pair_swap(v, axis="tp"):
    n, me = lax.axis_size(axis), lax.axis_index(axis)
    got = [lax.dynamic_index_in_dim(v, me, 0, keepdims=False)]
    for d in range(1, n):
        send = lax.dynamic_index_in_dim(v, me ^ d, 0, keepdims=False)
        got.append(lax.ppermute(send, axis, [(i, i ^ d) for i in range(n)]))
    outs = []
    for j in range(n):
        out = got[j]
        for m in range(1, n):
            out = jnp.where(me == m, got[j ^ m], out)
        outs.append(out)
    return jnp.stack(outs, 0)


def carried_state(through, state, direction, *beside):
    n = lax.axis_size("seq")
    rest = []

    def fetch(steps):
        high, low = split16(through)
        rows = [state.astype(bf16), high, low, jnp.zeros((14, state.shape[1]), bf16)]
        block = jnp.concatenate(rows, 0)
        got = []
        parts = [shift_seq(block, direction * step) for step in steps]
        if window == 0:
            parts = tie(*parts, *beside)
            rest[:] = parts[len(steps) :]
        for part in parts[: len(steps)]:
            decay = part[STATE : STATE + 1].astype(f32) + part[STATE + 1 : STATE + 2].astype(f32)
            got.append((decay, part[:STATE].astype(f32)))
        return got

    window = 0
    while window < n - 1:
        if window == 0:
            steps = [k for k in (1, 2, 3) if k < n]
            terms = fetch(steps)
            reach = 3
        else:
            steps = [k * window for k in (1, 2) if k * window < n]
            terms = [(through, state)] + fetch(steps)
            reach = 3 * window
        through, state = terms[0]
        for decay, part in terms[1:]:
            state = state + through * part
            through = through * decay
        window = reach
    return state, *rest


def shift_seq(v, steps):
    n = lax.axis_size("seq")
    first, last = max(0, -steps), min(n, n - steps)
    return lax.ppermute(v, "seq", [(i, i + steps) for i in range(first, last)])


def sigmoid(v):
    return 1.0 / (1.0 + jnp.exp(-v))


def shift_down(block, halo, j):
    rolled = pltpu.roll(block, j, 0)
    edge = pltpu.roll(halo, j, 0)
    row = lax.broadcasted_iota(jnp.int32, halo.shape, 0)
    return jnp.concatenate([jnp.where(row < j, edge, rolled[:8]), rolled[8:]], 0)


def shift_up(block, after, j):
    rows = block.shape[0]
    rolled = pltpu.roll(block, rows - j, 0)
    edge = pltpu.roll(after, 8 - j, 0)
    row = lax.broadcasted_iota(jnp.int32, after.shape, 0)
    return jnp.concatenate(
        [rolled[: rows - 8], jnp.where(row >= 8 - j, edge, rolled[rows - 8 :])], 0
    )


def conv_pre(block, halo, taps_ref, aux):
    pre = taps_ref[0:1, :] * block
    for j in (1, 2, 3):
        pre = pre + taps_ref[j : j + 1, :] * (aux[:, j : j + 1] * shift_down(block, halo, j))
    return pre


def softplus(v):
    return jnp.maximum(v, 0.0) + jnp.log(1.0 + jnp.exp(-jnp.abs(v)))


def split16(value):
    high = value.astype(bf16)
    return high, (value - high.astype(f32)).astype(bf16)


def widen(value, ex_ref):
    high, low = split16(value)
    return mm(jnp.concatenate([high, low], 1), ex_ref[...])


def head_sums(value, ex_ref):
    high, low = split16(value)
    spread = ex_ref[:LANES, :]
    return mm(high, spread, NT) + mm(low, spread, NT)


def triangle(n, upper=False):
    row = lax.broadcasted_iota(jnp.int32, (n, n), 0)
    col = lax.broadcasted_iota(jnp.int32, (n, n), 1)
    return jnp.where(row <= col if upper else row >= col, 1.0, 0.0).astype(f32)


def gap_mask(aux, auxr):
    n = aux.shape[0]
    row = lax.broadcasted_iota(jnp.int32, (n, n), 0)
    col = lax.broadcasted_iota(jnp.int32, (n, n), 1)
    return jnp.where((row >= col) & (aux[:, 4:5] == auxr[0:1, :]), 0.0, FAR).astype(f32)


def states_kernel(
    u_ref, bc_ref, dt_ref, edge_ref, taps_ref, head_ref, aux_ref, ex_ref,
    xs_ref, bcs_ref, lc_ref, lt_ref, dtv_ref, thr_ref, ent_ref, fin_ref,
    halo, state,
):
    c = pl.program_id(0)
    n, inner = xs_ref.shape

    @pl.when(c == 0)
    def _():
        halo[...] = edge_ref[...]
        state[...] = jnp.zeros_like(state)

    aux = aux_ref[...]
    block = jnp.concatenate([u_ref[...], bc_ref[...]], 1)
    pre = conv_pre(block, halo[...], taps_ref, aux)
    halo[...] = block[n - 8 :]
    act = pre * sigmoid(pre)
    xs = act[:, :inner]
    bcs = act[:, inner:].astype(bf16)
    dtv = softplus(dt_ref[...] + head_ref[0:1, :])
    lc = mm(triangle(n), head_ref[1:2, :] * dtv, precision=highest)
    total = lc[n - 1 : n, :]
    xs_ref[...] = xs.astype(bf16)
    bcs_ref[...] = bcs
    lc_ref[...] = lc
    lt_ref[...] = lc.T
    dtv_ref[...] = dtv
    scale = widen(jnp.exp(total - lc) * aux[:, 6:7] * dtv, ex_ref)
    through = jnp.exp(jnp.broadcast_to(total, (8, LANES))) * aux[n - 1 : n, 5:6]
    through = widen(through, ex_ref)
    thr_ref[0] = through
    ent_ref[0] = state[...]
    state[...] = through[0:1, :] * state[...] + mm(
        bcs[:, :STATE], (xs * scale).astype(bf16), TN
    )
    fin_ref[...] = state[...]


def intra_kernel(xs_ref, bcs_ref, lc_ref, lt_ref, dtv_ref, aux_ref, auxr_ref, ex_ref, y_ref):
    inner = xs_ref.shape[1]
    mask = gap_mask(aux_ref[...], auxr_ref[...])
    scores = mm(bcs_ref[:, STATE:], bcs_ref[:, :STATE], NT)
    xd = xs_ref[...].astype(f32) * widen(dtv_ref[...], ex_ref)
    lane = lax.broadcasted_iota(jnp.int32, (1, LANES), 1)
    for p in range(inner // LANES):
        pair = xd[:, p * LANES : (p + 1) * LANES]
        total = None
        for side in range(2):
            h = 2 * p + side
            decay = jnp.exp(lc_ref[:, h : h + 1] - lt_ref[h : h + 1, :] + mask)
            mine = (lane < HEAD_DIM) if side == 0 else (lane >= HEAD_DIM)
            term = mm((decay * scores).astype(bf16), jnp.where(mine, pair, 0.0).astype(bf16))
            total = term if total is None else total + term
        y_ref[:, p * LANES : (p + 1) * LANES] = total


def read_kernel(
    z_ref, yi_ref, xs_ref, bcs_ref, lc_ref, aux_ref, ex_ref, ent_ref, car_ref, thr_ref, rows_ref,
    y_ref, gg_ref, ss_ref, st_ref, pre,
):
    c = pl.program_id(0)

    @pl.when(c == 0)
    def _():
        pre[...] = jnp.ones_like(pre)

    entering = ent_ref[0] + pre[0:1, :] * car_ref[...]
    pre[...] = pre[...] * thr_ref[0]
    st_ref[0] = entering
    read = mm(bcs_ref[:, STATE:], entering.astype(bf16))
    entry = widen(jnp.exp(lc_ref[...]) * aux_ref[:, 5:6], ex_ref)
    y = yi_ref[...] + entry * read + rows_ref[0:1, :] * xs_ref[...].astype(f32)
    z = z_ref[...]
    gated = y * (z * sigmoid(z))
    y_ref[...] = y
    gg_ref[...] = (gated * rows_ref[1:2, :]).astype(bf16)
    ss_ref[...] = jnp.broadcast_to(
        jnp.sum(gated * gated, axis=1, keepdims=True), ss_ref.shape
    )


def gate_back_kernel(
    dg_ref, z_ref, y_ref, c2_ref, rows_ref, xs_ref, bcs_ref, lc_ref, aux_ref, ex_ref, thr_ref,
    dy_ref, dz_ref, lg_ref, fin_ref, acc_ref, run,
):
    @pl.when(pl.program_id(0) == 0)
    def _():
        run[...] = jnp.zeros_like(run)
        acc_ref[...] = jnp.zeros_like(acc_ref)

    z, y, back = z_ref[...], y_ref[...], dg_ref[...]
    sig = sigmoid(z)
    open_ = z * sig
    gated = y * open_
    d_gated = back * rows_ref[1:2, :] - gated * c2_ref[:, 0:1]
    dy = d_gated * open_
    dz_ref[...] = (d_gated * y * (sig * (1.0 + z * (1.0 - sig)))).astype(bf16)
    dy_ref[...] = dy.astype(bf16)
    acc_ref[0:1, :] += jnp.sum(back * gated, axis=0, keepdims=True)
    acc_ref[1:2, :] += jnp.sum(dy * xs_ref[...].astype(f32), axis=0, keepdims=True)
    entry = widen(jnp.exp(lc_ref[...]) * aux_ref[:, 5:6], ex_ref)
    lg_ref[0] = run[...]
    run[...] = thr_ref[0, 0:1, :] * run[...] + mm(
        bcs_ref[:, STATE:], (entry * dy).astype(bf16), TN
    )
    fin_ref[...] = run[...]


def scan_back_kernel(
    u_ref, bc_ref, uh_ref, bch_ref, edge_ref, dt_ref, dz_ref, taps_ref, head_ref, rows_ref, aux_ref, auxr_ref, ex_ref,
    lc_ref, lt_ref, dtv_ref, dy_ref, st_ref, lg_ref, car_ref, thr_ref,
    dp_ref, last_ref, back_ref, tacc_ref, hacc_ref,
    post, nxt, later,
):
    step = pl.program_id(0)
    chunks = pl.num_programs(0)
    n, inner = dy_ref.shape

    @pl.when(step == 0)
    def _():
        post[...] = jnp.ones_like(post)
        nxt[...] = jnp.zeros_like(nxt)
        tacc_ref[...] = jnp.zeros_like(tacc_ref)
        hacc_ref[...] = jnp.zeros_like(hacc_ref)
        later[...] = jnp.zeros_like(later)

    aux = aux_ref[...]
    block = jnp.concatenate([u_ref[...], bc_ref[...]], 1)
    halo = jnp.concatenate([uh_ref[...], bch_ref[...]], 1)
    halo = jnp.where(step == chunks - 1, edge_ref[...], halo)
    shifted = [block] + [aux[:, j : j + 1] * shift_down(block, halo, j) for j in (1, 2, 3)]
    pre = taps_ref[0:1, :] * block
    for j in (1, 2, 3):
        pre = pre + taps_ref[j : j + 1, :] * shifted[j]
    sig = sigmoid(pre)
    act = pre * sig
    slope = sig * (1.0 + pre * (1.0 - sig))
    xs = act[:, :inner]
    bcs = act[:, inner:].astype(bf16)
    keys, queries = bcs[:, :STATE], bcs[:, STATE:]
    lc, dtv = lc_ref[...], dtv_ref[...]
    total = lc[n - 1 : n, :]
    dt_wide = widen(dtv, ex_ref)
    tail_wide = widen(jnp.exp(total - lc) * aux[:, 6:7], ex_ref)
    entry_wide = widen(jnp.exp(lc) * aux[:, 5:6], ex_ref)
    xd = xs * dt_wide
    dy = dy_ref[...]
    dyf = dy.astype(f32)
    entering = st_ref[0]
    leaving = lg_ref[0] + post[0:1, :] * car_ref[...]
    post[...] = post[...] * thr_ref[0]
    ent16, lea16 = entering.astype(bf16), leaving.astype(bf16)

    row = lax.broadcasted_iota(jnp.int32, (n, n), 0)
    col = lax.broadcasted_iota(jnp.int32, (n, n), 1)
    mask = jnp.where((row <= col) & (aux[:, 4:5] == auxr_ref[0:1, :]), 0.0, FAR).astype(f32)
    scores = mm(keys, queries, NT)
    lane = lax.broadcasted_iota(jnp.int32, (1, LANES), 1)
    earlier = jnp.zeros((n, LANES), f32)
    d_scores = jnp.zeros((n, n), f32)
    parts = []
    for p in range(inner // LANES):
        cut = slice(p * LANES, (p + 1) * LANES)
        xd_pair, dy_pair = xd[:, cut].astype(bf16), dyf[:, cut]
        d_pair = None
        for side in range(2):
            h = 2 * p + side
            mine = (lane < HEAD_DIM) if side == 0 else (lane >= HEAD_DIM)
            dy_mine = jnp.where(mine, dy_pair, 0.0).astype(bf16)
            decay = jnp.exp(lt_ref[h : h + 1, :] - lc_ref[:, h : h + 1] + mask)
            weights = decay * scores
            d_weights = mm(xd_pair, dy_mine, NT)
            both = weights * d_weights
            earlier = jnp.where(lane == h, jnp.sum(both, axis=1, keepdims=True), earlier)
            later[h : h + 1, :] = jnp.sum(both, axis=0, keepdims=True)
            d_scores = d_scores + decay * d_weights
            term = mm(weights.astype(bf16), dy_mine)
            d_pair = term if d_pair is None else d_pair + term
        parts.append(d_pair)
    d_scores16 = d_scores.astype(bf16)
    through_lea = tail_wide * mm(keys, lea16)
    dxd = jnp.concatenate(parts, 1) + through_lea
    dxs = dt_wide * dxd + rows_ref[0:1, :] * dyf
    entry_dy = entry_wide * dyf
    d_queries = mm(d_scores16, keys, TN) + mm(entry_dy.astype(bf16), ent16, NT)
    d_keys = mm(d_scores16, queries) + mm((tail_wide * xd).astype(bf16), lea16, NT)
    d_act = jnp.concatenate([dxs, d_keys, d_queries], 1)
    dpre = d_act * slope

    into = head_sums(entry_dy * mm(queries, ent16), ex_ref)
    outof = head_sums(xd * through_lea, ex_ref)
    ends = head_sums(
        jnp.sum(entering * leaving, axis=0, keepdims=True) * thr_ref[0], ex_ref
    )
    d_log = later[...].T - earlier + into - outof
    row = lax.broadcasted_iota(jnp.int32, (n, 1), 0)
    d_log = d_log + jnp.where(
        row == n - 1, jnp.sum(outof, axis=0, keepdims=True) + ends[0:1, :], 0.0
    )
    d_rate = mm(triangle(n, True), d_log, precision=highest)
    d_dt = head_sums(xs * dxd, ex_ref) + d_rate * head_ref[1:2, :]
    d_step = d_dt * sigmoid(dt_ref[...] + head_ref[0:1, :])
    hacc_ref[0:1, :] += jnp.sum(d_rate * dtv, axis=0, keepdims=True) * head_ref[1:2, :]
    hacc_ref[1:2, :] += jnp.sum(d_step, axis=0, keepdims=True)

    d_block = taps_ref[0:1, :] * dpre
    tacc_ref[0:1, :] += jnp.sum(dpre * block, axis=0, keepdims=True)
    before = jnp.zeros((8, block.shape[1]), f32)
    row8 = lax.broadcasted_iota(jnp.int32, (8, 1), 0)
    for j in (1, 2, 3):
        tacc_ref[j : j + 1, :] += jnp.sum(dpre * shifted[j], axis=0, keepdims=True)
        lagged = taps_ref[j : j + 1, :] * (dpre * aux[:, j : j + 1])
        d_block = d_block + shift_up(lagged, nxt[j - 1], j)
        nxt[j - 1] = lagged[:8]
        before = before + jnp.where(row8 >= 8 - j, pltpu.roll(lagged[:8], 8 - j, 0), 0.0)
    back_ref[...] = before

    @pl.when(step == 0)
    def _():
        last_ref[...] = d_block[n - 8 :]

    dp_ref[:, :inner] = dz_ref[...]
    dp_ref[:, inner : inner + block.shape[1]] = d_block.astype(bf16)
    ends_at = inner + block.shape[1] + LANES
    dp_ref[:, inner + block.shape[1] : ends_at] = d_step.astype(bf16)
    dp_ref[:, ends_at:] = jnp.zeros((n, LANES), bf16)


def sds(shape, dtype):
    return jax.ShapeDtypeStruct(shape, dtype)


def params(mib):
    return pltpu.CompilerParams(
        dimension_semantics=("arbitrary",), vmem_limit_bytes=mib * 1024 * 1024
    )


def whole(shape):
    return pl.BlockSpec(shape, lambda c: (0,) * len(shape))


def mixer_specs(rows, inner, reverse):
    chunks = rows // CHUNK
    at = (lambda c: chunks - 1 - c) if reverse else (lambda c: c)
    return {
        "uh": pl.BlockSpec(
            (8, inner), lambda c: (jnp.maximum(at(c) * (CHUNK // 8) - 1, 0), 0)
        ),
        "bch": pl.BlockSpec(
            (8, 2 * STATE),
            lambda c: (jnp.maximum(at(c) * (CHUNK // 8) - 1, 0), inner // (2 * STATE)),
        ),
        "bc": pl.BlockSpec((CHUNK, 2 * STATE), lambda c: (at(c), inner // (2 * STATE))),
        "dt": pl.BlockSpec((CHUNK, LANES), lambda c: (at(c), (inner + 2 * STATE) // LANES)),
        "wide": pl.BlockSpec((CHUNK, inner), lambda c: (at(c), 0)),
        "bcs": pl.BlockSpec((CHUNK, 2 * STATE), lambda c: (at(c), 0)),
        "col": pl.BlockSpec((CHUNK, LANES), lambda c: (at(c), 0)),
        "lt": pl.BlockSpec((LANES, CHUNK), lambda c: (0, at(c))),
        "auxr": pl.BlockSpec((8, CHUNK), lambda c: (0, at(c))),
        "state": pl.BlockSpec((1, STATE, inner), lambda c: (at(c), 0, 0)),
        "thr": pl.BlockSpec((1, 8, inner), lambda c: (at(c), 0, 0)),
        "dp": pl.BlockSpec((CHUNK, 2 * inner + 2 * STATE + 2 * LANES), lambda c: (at(c), 0)),
        "edge": whole((8, inner + 2 * STATE)),
        "head": whole((8, LANES)),
        "rows": whole((8, inner)),
        "ex": whole((2 * LANES, inner)),
        "one": whole((STATE, inner)),
    }


def mixer_states(pu, edge, taps, head, aux, ex, inner):
    rows = pu.shape[0]
    chunks = rows // CHUNK
    s = mixer_specs(rows, inner, False)
    return pl.pallas_call(
        states_kernel,
        grid=(chunks,),
        in_specs=[
            s["wide"], s["bc"], s["dt"], s["edge"], s["edge"], s["head"], s["col"], s["ex"],
        ],
        out_specs=[
            s["wide"], s["bcs"], s["col"], s["lt"], s["col"], s["thr"], s["state"], s["one"],
        ],
        out_shape=[
            sds((rows, inner), bf16),
            sds((rows, 2 * STATE), bf16),
            sds((rows, LANES), f32),
            sds((LANES, rows), f32),
            sds((rows, LANES), f32),
            sds((chunks, 8, inner), f32),
            sds((chunks, STATE, inner), f32),
            sds((STATE, inner), f32),
        ],
        scratch_shapes=[
            pltpu.VMEM((8, inner + 2 * STATE), f32),
            pltpu.VMEM((STATE, inner), f32),
        ],
        compiler_params=params(32),
        name="mixer_states",
    )(pu, pu, pu, edge, taps, head, aux, ex)


def mixer_intra(xs, bcs, lc, lt, dtv, aux, auxr, ex):
    rows, inner = xs.shape
    s = mixer_specs(rows, inner, False)
    return pl.pallas_call(
        intra_kernel,
        grid=(rows // CHUNK,),
        in_specs=[
            s["wide"], s["bcs"], s["col"], s["lt"], s["col"], s["col"], s["auxr"], s["ex"],
        ],
        out_specs=s["wide"],
        out_shape=sds((rows, inner), f32),
        compiler_params=params(32),
        name="mixer_intra",
    )(xs, bcs, lc, lt, dtv, aux, auxr, ex)


def mixer_read(pz, yi, xs, bcs, lc, aux, ex, ent, carried, thr, head_rows):
    rows, inner = xs.shape
    chunks = rows // CHUNK
    s = mixer_specs(rows, inner, False)
    return pl.pallas_call(
        read_kernel,
        grid=(chunks,),
        in_specs=[
            s["wide"], s["wide"], s["wide"], s["bcs"], s["col"], s["col"], s["ex"],
            s["state"], s["one"], s["thr"], s["rows"],
        ],
        out_specs=[s["wide"], s["wide"], s["col"], s["state"]],
        out_shape=[
            sds((rows, inner), f32),
            sds((rows, inner), bf16),
            sds((rows, LANES), f32),
            sds((chunks, STATE, inner), f32),
        ],
        scratch_shapes=[pltpu.VMEM((8, inner), f32)],
        compiler_params=params(32),
        name="mixer_read",
    )(pz, yi, xs, bcs, lc, aux, ex, ent, carried, thr, head_rows)


def mixer_gate_back(dg, pz, y, c2, head_rows, xs, bcs, lc, aux, ex, thr):
    rows, inner = xs.shape
    chunks = rows // CHUNK
    s = mixer_specs(rows, inner, True)
    return pl.pallas_call(
        gate_back_kernel,
        grid=(chunks,),
        in_specs=[
            s["wide"], s["wide"], s["wide"], s["col"], s["rows"], s["wide"], s["bcs"],
            s["col"], s["col"], s["ex"], s["thr"],
        ],
        out_specs=[s["wide"], s["wide"], s["state"], s["one"], s["rows"]],
        out_shape=[
            sds((rows, inner), bf16),
            sds((rows, inner), bf16),
            sds((chunks, STATE, inner), f32),
            sds((STATE, inner), f32),
            sds((8, inner), f32),
        ],
        scratch_shapes=[pltpu.VMEM((STATE, inner), f32)],
        compiler_params=params(40),
        name="mixer_gate_back",
    )(dg, pz, y, c2, head_rows, xs, bcs, lc, aux, ex, thr)


def mixer_scan_back(
    pu, edge, dz, taps, head, head_rows, aux, auxr, ex, lc, lt, dtv, dy, st, lg, carried, thr
):
    rows, inner = dy.shape
    chunks = rows // CHUNK
    s = mixer_specs(rows, inner, True)
    wide = inner + 2 * STATE
    return pl.pallas_call(
        scan_back_kernel,
        grid=(chunks,),
        in_specs=[
            s["wide"], s["bc"], s["uh"], s["bch"], s["edge"], s["dt"], s["wide"], s["edge"],
            s["head"], s["rows"], s["col"], s["auxr"], s["ex"], s["col"], s["lt"], s["col"], s["wide"], s["state"], s["state"],
            s["one"], s["thr"],
        ],
        out_specs=[s["dp"], s["edge"], s["edge"], s["edge"], s["head"]],
        out_shape=[
            sds((rows, wide + inner + 2 * LANES), bf16),
            sds((8, wide), f32),
            sds((8, wide), f32),
            sds((8, wide), f32),
            sds((8, LANES), f32),
        ],
        scratch_shapes=[
            pltpu.VMEM((8, inner), f32),
            pltpu.VMEM((3, 8, wide), f32),
            pltpu.VMEM((LANES, CHUNK), f32),
        ],
        compiler_params=params(48),
        name="mixer_scan_back",
    )(
        pu, pu, pu, pu, edge, pu, dz, taps, head, head_rows, aux, auxr, ex, lc, lt, dtv, dy, st,
        lg, carried, thr,
    )


def up_kernel(at_ref, x_ref, w_ref, router_ref, named_ref, pat_ref, *refs):
    h_ref, act_ref, gates_ref, cols = refs[-4:]

    @pl.when(pl.program_id(0) == 0)
    def _():
        logits = mm(x_ref[...], router_ref[...], NT)
        mask = named_ref[...] > 0
        peak = jnp.max(jnp.where(mask, logits, FAR), axis=1, keepdims=True)
        raised = jnp.where(mask, jnp.exp(jnp.where(mask, logits - peak, 0.0)), 0.0)
        gates = raised / jnp.sum(raised, axis=1, keepdims=True)
        gates_ref[...] = gates
        cols[...] = gate_columns(gates)

    hidden = mm(x_ref[...], w_ref[...])
    g, w = hidden[:, :FF_BLOCK], hidden[:, FF_BLOCK:]
    gate = mm(cols[...], pat_ref[...])
    h_ref[...] = hidden.astype(bf16)
    act_ref[...] = (g * sigmoid(g) * w * gate).astype(bf16)


def gate_columns(gates):
    lane = lax.broadcasted_iota(jnp.int32, gates.shape, 1)
    high, low = split16(jnp.where(lane == LANES - 1, 1.0, gates))
    return jnp.concatenate([high, low], 1)


def down_back_kernel(at_ref, gs_ref, w_ref, h_ref, gates_ref, pat_ref, *refs):
    dh_ref, dgate_ref, cols = refs[-3:]

    @pl.when(pl.program_id(0) == 0)
    def _():
        dgate_ref[...] = jnp.zeros_like(dgate_ref)
        cols[...] = gate_columns(gates_ref[...])

    for start in range(0, gs_ref.shape[0], ROW_TILE):
        cut = slice(start, start + ROW_TILE)
        q = mm(gs_ref[cut, :], w_ref[...], NT)
        g = h_ref[cut, :FF_BLOCK].astype(f32)
        w = h_ref[cut, FF_BLOCK:].astype(f32)
        sig = sigmoid(g)
        opened = g * sig
        gate = mm(cols[cut, :], pat_ref[...])
        dgate_ref[cut, :] += mm((opened * w * q).astype(bf16), pat_ref[:LANES, :], NT)
        d_act = gate * q
        dh_ref[cut, :FF_BLOCK] = (d_act * w * (sig * (1.0 + g * (1.0 - sig)))).astype(bf16)
        dh_ref[cut, FF_BLOCK:] = (d_act * opened).astype(bf16)


def in_place(state, inputs):
    held = [] if state is None else list(state)
    specs = [pl.BlockSpec(memory_space=pl.ANY)] * len(held)
    return held, specs, {inputs + 1 + i: i for i in range(len(held))}


def experts_up(x, at, w_up, router_w, named, pattern, state):
    own, depth = x.shape
    rows = named.shape[0]
    blocks = w_up.shape[1] // (2 * FF_BLOCK)
    held, specs, aliases = in_place(state, 5)
    return pl.pallas_call(
        up_kernel,
        grid_spec=pltpu.PrefetchScalarGridSpec(
            num_scalar_prefetch=1,
            grid=(blocks,),
            in_specs=[
                pl.BlockSpec((own, depth), lambda i, at: (0, 0)),
                pl.BlockSpec((depth, 2 * FF_BLOCK), lambda i, at: (0, i)),
                pl.BlockSpec((LANES, depth), lambda i, at: (0, 0)),
                pl.BlockSpec((own, LANES), lambda i, at: (at[0], 0)),
                pl.BlockSpec((2 * LANES, FF_BLOCK), lambda i, at: (0, i)),
            ]
            + specs,
            out_specs=[
                pl.BlockSpec((own, 2 * FF_BLOCK), lambda i, at: (at[0], i)),
                pl.BlockSpec((own, FF_BLOCK), lambda i, at: (at[0], i)),
                pl.BlockSpec((own, LANES), lambda i, at: (at[0], 0)),
            ],
            scratch_shapes=[pltpu.VMEM((own, 2 * LANES), bf16)],
        ),
        out_shape=[
            sds((rows, 2 * FF_BLOCK * blocks), bf16),
            sds((rows, FF_BLOCK * blocks), bf16),
            sds((rows, LANES), f32),
        ],
        input_output_aliases=aliases,
        compiler_params=params(58),
        name="experts_up",
    )(at.astype(jnp.int32).reshape(1), x, w_up, router_w, named, pattern, *held)


def experts_down_back(gs, at, w_down, hidden, gates, pattern, state):
    depth = gs.shape[1]
    rows = hidden.shape[0]
    own = gs.shape[0]
    blocks = w_down.shape[0] // FF_BLOCK
    held, specs, aliases = in_place(state, 5)
    return pl.pallas_call(
        down_back_kernel,
        grid_spec=pltpu.PrefetchScalarGridSpec(
            num_scalar_prefetch=1,
            grid=(blocks,),
            in_specs=[
                pl.BlockSpec((own, depth), lambda i, at: (0, 0)),
                pl.BlockSpec((FF_BLOCK, depth), lambda i, at: (i, 0)),
                pl.BlockSpec((own, 2 * FF_BLOCK), lambda i, at: (at[0], i)),
                pl.BlockSpec((own, LANES), lambda i, at: (at[0], 0)),
                pl.BlockSpec((2 * LANES, FF_BLOCK), lambda i, at: (0, i)),
            ]
            + specs,
            out_specs=[
                pl.BlockSpec((own, 2 * FF_BLOCK), lambda i, at: (at[0], i)),
                pl.BlockSpec((own, LANES), lambda i, at: (at[0], 0)),
            ],
            scratch_shapes=[pltpu.VMEM((own, 2 * LANES), bf16)],
        ),
        out_shape=[
            sds((rows, 2 * FF_BLOCK * blocks), bf16),
            sds((rows, LANES), f32),
        ],
        input_output_aliases=aliases,
        compiler_params=params(32 if own == rows else 58),
        name="experts_down_back",
    )(at.astype(jnp.int32).reshape(1), gs, w_down, hidden, gates, pattern, *held)


def row_norm(values):
    return lax.rsqrt(jnp.mean(values * values, axis=-1, keepdims=True) + epsilon)


def norm_back(values, inverse, gain, grad):
    weighted = grad * gain
    mean = jnp.mean(weighted * values, axis=-1, keepdims=True)
    return inverse * weighted - values * (inverse * inverse * inverse * mean)


def pad_rows(parts, rows, width):
    value = jnp.concatenate([jnp.atleast_2d(part) for part in parts], 0)
    return jnp.pad(value, ((0, rows - value.shape[0]), (0, width - value.shape[1])))


def to_line(column):
    value = column.reshape(-1, LANES)
    return jnp.pad(value, ((0, 8 - value.shape[0]), (0, 0)))


def local(
    tokens, inner_proj, step_proj, state_proj, inner_conv, state_conv, decay_log, step_bias,
    skip_gain, gate_gain, outer_proj, norm_gains, router, expert_up, expert_down, shared_up,
    shared_down, routes, packed_lengths, cotangent,
):
    ns, nt = lax.axis_size("seq"), lax.axis_size("tp")
    sq, tp = lax.axis_index("seq"), lax.axis_index("tp")
    layers = inner_proj.shape[0]
    own, depth = tokens.shape
    rows = own * nt
    chunks = rows // CHUNK
    inner = gate_gain.shape[1]
    heads = decay_log.shape[1]
    inner_all = inner * nt
    cut = inner_proj.shape[1]
    fine = state_proj.shape[1]
    devices = ns * nt
    experts = router.shape[2]
    mine = expert_up.shape[1]
    ff = expert_down.shape[2] * ns
    ff_cut = expert_down.shape[2]
    shared = shared_down.shape[1] * ns
    sh_cut = shared_down.shape[1]
    tap_cut = state_conv.shape[2]
    width = inner + 2 * STATE
    hidden_units = mine * ff + shared
    ff_blocks = hidden_units // FF_BLOCK
    per_seq = mine * ff_cut + sh_cut

    ends = jnp.cumsum(packed_lengths, dtype=jnp.int32)
    starts = ends - packed_lengths

    def count(positions):
        return jnp.sum(
            (starts[None, :] <= positions[:, None]).astype(f32), axis=1
        )

    first = sq * rows
    here = first + jnp.arange(rows, dtype=jnp.int32)
    seg = count(here)
    chunk_of = jnp.arange(rows, dtype=jnp.int32) // CHUNK
    lags = [jnp.ones_like(seg)] + [(count(here - j) == seg).astype(f32) for j in (1, 2, 3)]
    alive = (count(first + chunk_of * CHUNK - 1) == seg).astype(f32)
    tail = (count(first + chunk_of * CHUNK + CHUNK - 1) == seg).astype(f32)
    aux = jnp.pad(jnp.stack(lags + [seg, alive, tail], 1), ((0, 0), (0, LANES - 7)))
    auxr = jnp.broadcast_to(seg[None, :], (8, rows))
    lane_head = jnp.arange(inner, dtype=jnp.int32) // HEAD_DIM
    ex_row = jnp.arange(2 * LANES, dtype=jnp.int32)[:, None] % LANES
    ex = (ex_row == lane_head[None, :]).astype(bf16)
    unit = jnp.arange(hidden_units, dtype=jnp.int32) % per_seq
    unit_gate = jnp.where(unit < mine * ff_cut, tp * mine + unit // ff_cut, LANES - 1)
    pat_row = jnp.arange(2 * LANES, dtype=jnp.int32)[:, None] % LANES
    pattern = (pat_row == unit_gate[None, :]).astype(bf16)

    inv1 = row_norm(tokens)
    scaled = (tokens * inv1).astype(bf16)
    smalls, ups = [], []
    for l in range(layers):
        taps_col = jnp.pad(state_conv[l].reshape(-1), (0, fine - 4 * tap_cut))[:, None]
        small = jnp.concatenate([state_proj[l], router[l], norm_gains[l].T, taps_col], 1)
        smalls.append(jnp.pad(small, ((0, 0), (0, 2 * STATE + LANES - small.shape[1]))))
        up = shared_up[l].reshape(fine, 2, ns, nt, sh_cut)
        ups.append(jnp.transpose(up, (3, 0, 1, 2, 4)).reshape(nt, fine, 2 * shared))
    plain, _, riders = hop_both(
        scaled,
        None,
        (jnp.concatenate(smalls, 1), expert_up, jnp.stack(ups, 1), routes, expert_down, shared_down),
    )
    small_all, expert_up, ups, routes, expert_down, shared_down = riders
    small_all = pair_gather(small_all)
    up_all = pair_swap(ups)

    def mixer_weights(l):
        dt_cols = jnp.pad(step_proj[l], ((0, 0), (0, LANES - heads)))
        small = small_all[:, l * (2 * STATE + LANES) : (l + 1) * (2 * STATE + LANES)]
        pack = jnp.concatenate(
            [
                inner_proj[l, :, 0],
                inner_proj[l, :, 1],
                small[:, : 2 * STATE],
                dt_cols,
                small[:, 2 * STATE :],
            ],
            1,
        )
        return pack, outer_proj[l].T

    def over_seq(value):
        return lax.all_gather(value, "seq", axis=0, tiled=True)

    def expert_weights(l):
        halves = jnp.transpose(expert_up[l].reshape(mine, cut, 2, ns, ff_cut), (2, 1, 3, 0, 4))
        halves = halves.reshape(2, cut, ns, mine * ff_cut)
        extra = jnp.transpose(up_all[:, l].reshape(cut, 2, ns, sh_cut), (1, 0, 2, 3))
        halves = jnp.concatenate([halves, extra], 3).reshape(2, cut, ff_blocks, FF_BLOCK)
        local_up = jnp.transpose(halves, (1, 2, 0, 3)).reshape(cut, 2 * hidden_units)
        local_down = jnp.concatenate(
            [expert_down[l].reshape(mine * ff_cut, depth), shared_down[l]], 0
        )
        return local_up, local_down

    packs = [list(mixer_weights(l) + expert_weights(l)) for l in range(layers)]
    plain, *packs[0][2:] = tie(plain, *packs[0][2:])
    w_in, w_out, w_up, w_down = [[None] * layers for _ in range(4)]
    w_in[0], w_out[0] = over_seq(packs[0][0]), over_seq(packs[0][1])

    named = jnp.any(
        routes[:, :, :, None] == jnp.arange(experts, dtype=jnp.int32), axis=2
    ).astype(bf16)
    named = pair_gather(
        jnp.transpose(named, (1, 0, 2)).reshape(own, layers * experts)
    ).reshape(rows, layers, experts)
    named = jnp.pad(named, ((0, 0), (0, 0), (0, LANES - experts))).astype(f32)

    residual = tokens
    saved = []
    last_cot = None
    for l in range(layers):
        small_in = tie(w_in[l][:, inner + width + LANES :].astype(f32).T)[0]
        router_w = jnp.pad(small_in[:experts], ((0, LANES - experts), (0, 0))).astype(bf16)
        gain1 = small_in[experts]
        gain2 = small_in[experts + 1]
        taps_bc = small_in[experts + 2].reshape(devices, fine)[:, : 4 * tap_cut]
        taps_bc = jnp.transpose(taps_bc.reshape(devices, 4, tap_cut), (1, 0, 2))
        taps_bc = taps_bc.reshape(4, 2 * STATE)
        taps = jnp.pad(
            jnp.concatenate([inner_conv[l], taps_bc], 1), ((0, 4), (0, 0))
        )
        head = pad_rows([step_bias[l], -jnp.exp(decay_log[l])], 8, LANES)
        head_rows = pad_rows([jnp.repeat(skip_gain[l], HEAD_DIM), gate_gain[l]], 8, inner)

        if l > 0:
            inv1 = row_norm(residual)
            scaled = (residual * inv1).astype(bf16)
            plain = hop_gather(scaled)
        normed = (plain.astype(f32) * gain1).astype(bf16)
        pu = mm(normed, w_in[l][:, inner : inner + width + LANES])
        edge = shift_seq(pu[rows - 8 :, :width], 1)
        xs, bcs, lc, lt, dtv, thr, ent, fin = mixer_states(pu, edge, taps, head, aux, ex, inner)
        through = thr[0, 0:1]
        for c in range(1, chunks):
            through = through * thr[c, 0:1]
        pz = mm(normed, w_in[l][:, :inner])
        yi = mixer_intra(xs, bcs, lc, lt, dtv, aux, auxr, ex)
        carried, pz, yi = carried_state(through, fin, 1, pz, yi)
        cot16 = cotangent.astype(bf16)
        if l == 0:
            carried, cot16 = tie(carried, cot16)
        carried, up_pack, down_pack = tie(carried, packs[l][2], packs[l][3])
        w_up[l], w_down[l] = over_seq(up_pack), over_seq(down_pack)
        y, gg, ss, st = mixer_read(pz, yi, xs, bcs, lc, aux, ex, ent, carried, thr, head_rows)
        squares = pair_total(ss[:, 0].reshape(rows // LANES, LANES), "tp")
        squares = lax.dynamic_slice_in_dim(
            squares, tp * (own // LANES), own // LANES, 0
        ).reshape(own)
        partial_out = mm(gg, w_out[l], NT).astype(bf16)
        if l == 0:
            last_cot, out_sum, (squares,) = hop_both(cot16, partial_out, (squares,))
            out_sum, last_cot = tie(out_sum, last_cot)
        else:
            _, out_sum, (squares,) = hop_both(None, partial_out, (squares,))
        inv_gate = lax.rsqrt(squares / inner_all + epsilon)
        mixed = inv_gate[:, None] * out_sum
        mid = residual + mixed

        inv2 = row_norm(mid)
        moe_own = (mid * inv2 * gain2).astype(bf16)
        mask = named[:, l]

        def up_block(block, at, state):
            return experts_up(block, at, w_up[l], router_w, mask, pattern, state)

        moe_in, (hidden, act, gates) = gather_work(moe_own, up_block)
        if l < layers - 1:
            act, *packs[l + 1][:2] = tie(act, *packs[l + 1][:2])
            w_in[l + 1], w_out[l + 1] = over_seq(packs[l + 1][0]), over_seq(packs[l + 1][1])
        saved.append(
            dict(
                router_w=router_w, gain1=gain1, gain2=gain2, taps=taps, head=head,
                head_rows=head_rows, residual=residual, inv1=inv1, plain=plain, normed=normed,
                pu=pu, pz=pz, edge=edge, xs=xs, bcs=bcs, lc=lc, lt=lt, dtv=dtv, thr=thr,
                through=through, y=y, gg=gg, st=st, inv_gate=inv_gate, mixed=mixed,
                mid=mid, inv2=inv2, moe_own=moe_own, moe_in=moe_in, gates=gates,
                hidden=hidden, act=act,
            )
        )
        if l < layers - 1:

            moe_out = hop_scatter(mm(act, w_down[l]).astype(bf16))
            moe_out, *packs[l + 1][2:] = tie(moe_out, *packs[l + 1][2:])
            residual = mid + moe_out

    def finish_up(up):
        halves = up.reshape(cut, ff_blocks, 2, FF_BLOCK)
        halves = jnp.transpose(halves, (2, 0, 1, 3)).reshape(2, cut, ns, per_seq)
        mine_up = halves[..., : mine * ff_cut].reshape(2, cut, ns, mine, ff_cut)
        mine_up = jnp.transpose(mine_up, (3, 1, 0, 2, 4)).reshape(mine, cut, 2 * ff)
        mine_up = row_major(mine_up)
        shared_cols = jnp.transpose(halves[..., mine * ff_cut :], (1, 0, 2, 3))
        shared_grad = pair_swap(shared_cols.reshape(nt, fine, 2 * shared))
        shared_grad = jnp.transpose(
            shared_grad.reshape(nt, fine, 2, ns, sh_cut), (1, 2, 3, 0, 4)
        ).reshape(fine, -1)
        return mine_up, shared_grad

    def finish_in(early, late):
        return jnp.stack([early[:, inner:], late[:, :inner]], 1), pair_scatter(late[:, inner:])

    def outputs(r):
        sums, common, down = r["sums"], r["common"], r["down"]
        small = common[:, 2 * STATE + heads :]
        return [
            r["inner"],
            r["late"][:, width : width + heads].astype(f32),
            common[:, : 2 * STATE],
            sums[:4],
            small[: 4 * tap_cut, experts + 2].reshape(4, tap_cut),
            sums[6, :heads],
            sums[6, LANES : LANES + heads],
            jnp.sum(sums[5].reshape(heads, HEAD_DIM), axis=1),
            sums[4],
            r["early"][:, :inner].T,
            jnp.transpose(small[:, experts : experts + 2]),
            small[:, :experts],
            r["mine_up"],
            down[: mine * ff_cut].reshape(mine, ff_cut, depth),
            r["shared_up"],
            down[mine * ff_cut :],
        ]

    grad = cotangent
    finished = [None] * layers
    for l in reversed(range(layers)):
        k = saved[l]
        top = l == layers - 1
        state = None

        def back_block(block, at, state):
            return experts_down_back(
                block, at, w_down[l], k["hidden"], k["gates"], pattern, state
            )

        def gate_sums():
            lines = state[1][:, :experts].reshape(rows // per_line, LANES)
            return pair_total(lines, "tp")

        per_line = LANES // experts
        if top:
            gs = last_cot
            last_out = mm(k["act"], w_down[l]).astype(bf16)
            state = back_block(gs, jnp.int32(0), None)
        else:
            gs, state = gather_work(grad.astype(bf16), back_block)
            first, above["late"] = tie(state[0], above["late"])
            state = (first, state[1])
        d_hidden = state[0]
        up_part = mm(k["moe_in"], d_hidden, TN).astype(bf16)
        _, d_moe, riders = hop_both(
            None,
            mm(d_hidden, w_up[l], NT).astype(bf16),
            (gate_sums(), up_part) + (() if top else (above["up"],)),
        )
        d_gate_all, up_part, *riders = riders
        if not top:
            above["mine_up"], above["shared_up"] = finish_up(riders[0])
        up_grad = lax.psum_scatter(up_part, "seq", scatter_dimension=0, tiled=True)
        down_part = mm(k["act"], gs, TN).astype(bf16)
        if top:
            d_moe, last_out = tie(d_moe, last_out)
        d_gate_own = lax.dynamic_slice_in_dim(
            d_gate_all, tp * (own // per_line), own // per_line, 0
        ).reshape(own, experts)
        d_gate_own = jnp.pad(d_gate_own, ((0, 0), (0, LANES - experts)))
        gates_own = lax.dynamic_slice_in_dim(k["gates"], tp * own, own, 0)
        d_logits = gates_own * (
            d_gate_own - jnp.sum(gates_own * d_gate_own, axis=1, keepdims=True)
        )
        d_logits16 = d_logits.astype(bf16)
        router_grad = mm(k["moe_own"], d_logits16, TN)[:, :experts]
        d_moe = d_moe + mm(d_logits16, k["router_w"])
        gain2_grad = jnp.sum(d_moe * k["mid"] * k["inv2"], axis=0)
        grad_mid = grad + norm_back(k["mid"], k["inv2"], k["gain2"], d_moe)

        inv_gate = k["inv_gate"]
        cross = inv_gate * inv_gate * jnp.sum(grad_mid * k["mixed"], axis=1) / inner_all
        cross_all = pair_gather(to_line(cross)).reshape(nt, 8 * LANES)[:, :own].reshape(rows)
        send = (grad_mid * inv_gate[:, None]).astype(bf16)
        if top:
            d_mixed, moe_out, riders = hop_both(send, last_out, (cross_all, down_part))
            residual = k["mid"] + moe_out
        else:
            names = ("mine_up", "shared_up", "early", "late")
            d_mixed, _, riders = hop_both(
                send, None, [cross_all, down_part] + [above[name] for name in names]
            )
            above.update(zip(names, riders[2:]))
            above["inner"], above["common"] = finish_in(above["early"], above["late"])
        cross_all, down_part = riders[:2]
        down_grad = lax.psum_scatter(down_part, "seq", scatter_dimension=0, tiled=True)
        c2 = jnp.broadcast_to(cross_all[:, None], (rows, LANES))
        dg = mm(d_mixed, w_out[l])
        dy, dz, lg, fin, acc = mixer_gate_back(
            dg, k["pz"], k["y"], c2, k["head_rows"], k["xs"], k["bcs"], k["lc"], aux, ex, k["thr"]
        )
        early_out = row_major(mm(d_mixed, k["gg"], TN).astype(bf16))
        early_z = row_major(mm(k["normed"], dz, TN).astype(bf16))
        carried, early_out, early_z = carried_state(k["through"], fin, -1, early_out, early_z)
        early = jnp.concatenate([early_out, early_z], 1)
        carried, early, up_grad = tie(carried, early, up_grad)
        if top:
            carried, residual = tie(carried, residual)
        else:
            carried, above["inner"], above["common"] = tie(
                carried, above["inner"], above["common"]
            )
        early = lax.psum_scatter(early, "seq", scatter_dimension=0, tiled=True)
        dp, last, back, tacc, hacc = mixer_scan_back(
            k["pu"], k["edge"], dz, k["taps"], k["head"], k["head_rows"], aux, auxr, ex,
            k["lc"], k["lt"], k["dtv"], dy, k["st"], lg, carried, k["thr"],
        )
        last = (last + shift_seq(back, -1)).astype(bf16)
        dp = lax.dynamic_update_slice(dp, last, (rows - 8, inner))
        dp, down_grad = tie(dp, down_grad)
        d_normed = mm(dp, w_in[l], NT)
        gain1_grad = jnp.sum(d_normed * k["plain"].astype(f32), axis=0)
        taps_col = jnp.transpose(tacc[:4, inner:].reshape(4, devices, tap_cut), (1, 0, 2))
        taps_col = jnp.pad(taps_col.reshape(devices, 4 * tap_cut), ((0, 0), (0, fine - 4 * tap_cut)))
        small = jnp.concatenate(
            [router_grad, gain1_grad[:, None], gain2_grad[:, None], taps_col.reshape(-1)[:, None]],
            1,
        )
        late = mm(k["normed"], dp[:, inner : inner + width + LANES], TN).astype(bf16)
        block = late[:, width:] + jnp.pad(
            small, ((0, 0), (heads, LANES - heads - small.shape[1]))
        ).astype(bf16)
        late = lax.dynamic_update_slice(late, block, (0, width))
        sums = jnp.concatenate(
            [tacc[:4, :inner], acc[:2], pad_rows([hacc[:2].reshape(-1)], 2, inner)], 0
        )
        if top:
            _, d_own, riders = hop_both(None, d_normed.astype(bf16), (late, sums))
            late, sums = riders
        else:
            _, d_own, riders = hop_both(
                None,
                d_normed.astype(bf16),
                (late, early),
                (sums, above["sums"], up_grad),
            )
            late, early, sums = riders[:3]
        late = lax.psum_scatter(late, "seq", scatter_dimension=0, tiled=True)
        if top:
            d_own, early = tie(d_own, early)
        else:
            both = pair_total(jnp.concatenate([sums, riders[3]], 0), "seq")
            sums, above["sums"] = both[: sums.shape[0]], both[sums.shape[0] :]
            finished[l + 1] = outputs(above)
            d_own, down_grad = tie(d_own, down_grad)
        grad = grad_mid + norm_back(k["residual"], k["inv1"], k["gain1"], d_own)
        above = dict(up=up_grad, down=down_grad, early=early, late=late, sums=sums)
        if not top:
            above["mine_up"], above["shared_up"] = finish_up(riders[4])

    above["inner"], above["common"] = finish_in(above["early"], above["late"])
    finished[0] = outputs(above)
    stacked = [jnp.stack([part[i] for part in finished], 0).astype(f32) for i in range(16)]
    return (residual, grad, *stacked)


def solution(mesh):
    both = ("seq", "tp")
    in_specs = (
        P(both, None),
        P(None, "seq", None, "tp"),
        P(None, "seq", "tp"),
        P(None, both, None),
        P(None, None, "tp"),
        P(None, None, both),
        P(None, "tp"),
        P(None, "tp"),
        P(None, "tp"),
        P(None, "tp"),
        P(None, "tp", "seq"),
        P(None, None, both),
        P(None, both, None),
        P(None, "tp", "seq", None),
        P(None, "tp", "seq", None),
        P(None, both, None),
        P(None, both, None),
        P(None, both, None),
        P(),
        P(both, None),
    )
    out_specs = (
        P(both, None),
        P(both, None),
        P(None, "seq", None, "tp"),
        P(None, "seq", "tp"),
        P(None, both, None),
        P(None, None, "tp"),
        P(None, None, both),
        P(None, "tp"),
        P(None, "tp"),
        P(None, "tp"),
        P(None, "tp"),
        P(None, "tp", "seq"),
        P(None, None, both),
        P(None, both, None),
        P(None, "tp", "seq", None),
        P(None, "tp", "seq", None),
        P(None, both, None),
        P(None, both, None),
    )
    return jax.shard_map(local, mesh=mesh, in_specs=in_specs, out_specs=out_specs, check_vma=False)
```

```python
from functools import partial

import jax
import jax.numpy as jnp
from jax import lax
from jax.experimental import pallas as pl
from jax.experimental.layout import Layout, with_layout_constraint
from jax.experimental.pallas import tpu as pltpu
from jax.sharding import PartitionSpec as P

HEAD_DIM = 64
STATE = 128
TOP = 6
CHUNK = 256
LANES = 128
FF_BLOCK = 256
ROW_TILE = 256
FAR = -1e30

epsilon = 1e-05
highest = lax.Precision.HIGHEST
bf16 = jnp.bfloat16
f32 = jnp.float32

NN = (((1,), (0,)), ((), ()))
NT = (((1,), (1,)), ((), ()))
TN = (((0,), (0,)), ((), ()))


def mm(a, b, dims=NN, precision=None):
    return lax.dot_general(a, b, dims, precision=precision, preferred_element_type=f32)


def row_major(value):
    return with_layout_constraint(value, Layout(tuple(range(value.ndim))))


def tie(*values):
    return lax.optimization_barrier(values)


def hop_both(v, x, riders=(), last=(), axis="tp"):
    n, me = lax.axis_size(axis), lax.axis_index(axis)
    riders, last = tuple(riders), tuple(last)
    rel = {0: v}
    ahead = right = left = None
    if v is not None:
        ahead = (v, v)
    if x is not None:
        rows = x.shape[0] // n

        def piece(k):
            return lax.dynamic_slice_in_dim(x, jnp.clip(k, 0, n - 1) * rows, rows, 0)

        right, left = piece(n - 1 + me), piece(me - (n - 1))
    lead = 1 if v is not None and x is not None else 0
    for step in range(1, n + lead):
        held = []
        gathers, scatters = ahead is not None and step < n, right is not None and step > lead
        if gathers:
            held += list(ahead)
        if scatters:
            held += [right, left]
        if step > 1:
            count = len(held)
            extra = riders if step == 2 else last if step == n + lead - 1 else ()
            held = list(tie(*held, *extra))
            if step == 2:
                riders = tuple(held[count:])
            elif extra:
                last = tuple(held[count:])
            held = held[:count]
        if gathers:
            ahead = (
                lax.ppermute(held[0], axis, [(i, i + 1) for i in range(step - 1, n - 1)]),
                lax.ppermute(held[1], axis, [(i, i - 1) for i in range(1, n - step + 1)]),
            )
            rel[-step], rel[step] = ahead
            held = held[2:]
        if scatters:
            s = step - lead
            right = lax.ppermute(held[0], axis, [(i, i + 1) for i in range(0, s)])
            left = lax.ppermute(held[1], axis, [(i, i - 1) for i in range(n - s, n)])
            if s < n - 1:
                right = (right.astype(f32) + piece(n - 1 - s + me).astype(f32)).astype(x.dtype)
                left = (left.astype(f32) + piece(me - (n - 1 - s)).astype(f32)).astype(x.dtype)
    gathered = total = None
    if v is not None:
        outs = []
        for j in range(n):
            out = rel[j]
            for m in range(1, n):
                out = jnp.where(me == m, rel[j - m], out)
            outs.append(out)
        gathered = jnp.concatenate(outs, 0)
    if x is not None:
        total = piece(me).astype(f32) + right.astype(f32) + left.astype(f32)
    return gathered, total, riders + last


def choose(options, me):
    out = options[0]
    for m in range(1, len(options)):
        out = jnp.where(me == m, options[m], out)
    return out


def gather_work(v, work, axis="tp"):
    n, me = lax.axis_size(axis), lax.axis_index(axis)
    near = [sorted((j for j in range(n) if j != m), key=lambda j: abs(j - m)) for m in range(n)]
    right = left = block = v
    at, state, rel = me, None, {0: v}
    for d in range(1, n):
        right = lax.ppermute(right, axis, [(i, i + 1) for i in range(d - 1, n - 1)])
        left = lax.ppermute(left, axis, [(i, i - 1) for i in range(1, n - d + 1)])
        state = work(block, at, state)
        right, left, *state = tie(right, left, *state)
        rel[-d], rel[d] = right, left
        block = choose([rel[near[m][d - 1] - m] for m in range(n)], me)
        at = choose([near[m][d - 1] for m in range(n)], me)
    state = work(block, at, state)
    whole_v = jnp.concatenate(
        [choose([rel[j - m] for m in range(n)], me) for j in range(n)], 0
    )
    return whole_v, state


def hop_gather(v):
    return hop_both(v, None)[0]


def hop_scatter(x):
    return hop_both(None, x)[1]


def pair_total(v, axis):
    n = lax.axis_size(axis)
    bit = 1
    while bit < n:
        v = v + lax.ppermute(v, axis, [(i, i ^ bit) for i in range(n)])
        bit *= 2
    return v


def pair_gather(v, axis="tp"):
    n, me = lax.axis_size(axis), lax.axis_index(axis)
    bit = 1
    while bit < n:
        other = lax.ppermute(v, axis, [(i, i ^ bit) for i in range(n)])
        high = (me & bit) > 0
        v = jnp.concatenate([jnp.where(high, other, v), jnp.where(high, v, other)], 0)
        bit *= 2
    return v


def pair_scatter(v, axis="tp"):
    n, me = lax.axis_size(axis), lax.axis_index(axis)
    bit = n // 2
    while bit:
        half = v.shape[0] // 2
        side = (me & bit) > 0
        first, second = v[:half], v[half:]
        got = lax.ppermute(
            jnp.where(side, first, second), axis, [(i, i ^ bit) for i in range(n)]
        )
        v = jnp.where(side, second, first).astype(f32) + got.astype(f32)
        v = v.astype(first.dtype) if bit > 1 else v
        bit //= 2
    return v


def pair_swap(v, axis="tp"):
    n, me = lax.axis_size(axis), lax.axis_index(axis)
    got = [lax.dynamic_index_in_dim(v, me, 0, keepdims=False)]
    for d in range(1, n):
        send = lax.dynamic_index_in_dim(v, me ^ d, 0, keepdims=False)
        got.append(lax.ppermute(send, axis, [(i, i ^ d) for i in range(n)]))
    outs = []
    for j in range(n):
        out = got[j]
        for m in range(1, n):
            out = jnp.where(me == m, got[j ^ m], out)
        outs.append(out)
    return jnp.stack(outs, 0)


def carried_state(through, state, direction, *beside):
    n = lax.axis_size("seq")
    rest = []

    def fetch(steps):
        high, low = split16(through)
        rows = [state.astype(bf16), high, low, jnp.zeros((14, state.shape[1]), bf16)]
        block = jnp.concatenate(rows, 0)
        got = []
        parts = [shift_seq(block, direction * step) for step in steps]
        if window == 0:
            parts = tie(*parts, *beside)
            rest[:] = parts[len(steps) :]
        for part in parts[: len(steps)]:
            decay = part[STATE : STATE + 1].astype(f32) + part[STATE + 1 : STATE + 2].astype(f32)
            got.append((decay, part[:STATE].astype(f32)))
        return got

    window = 0
    while window < n - 1:
        if window == 0:
            steps = [k for k in (1, 2, 3) if k < n]
            terms = fetch(steps)
            reach = 3
        else:
            steps = [k * window for k in (1, 2) if k * window < n]
            terms = [(through, state)] + fetch(steps)
            reach = 3 * window
        through, state = terms[0]
        for decay, part in terms[1:]:
            state = state + through * part
            through = through * decay
        window = reach
    return state, *rest


def shift_seq(v, steps):
    n = lax.axis_size("seq")
    first, last = max(0, -steps), min(n, n - steps)
    return lax.ppermute(v, "seq", [(i, i + steps) for i in range(first, last)])


def sigmoid(v):
    return 1.0 / (1.0 + jnp.exp(-v))


def shift_down(block, halo, j):
    rolled = pltpu.roll(block, j, 0)
    edge = pltpu.roll(halo, j, 0)
    row = lax.broadcasted_iota(jnp.int32, halo.shape, 0)
    return jnp.concatenate([jnp.where(row < j, edge, rolled[:8]), rolled[8:]], 0)


def shift_up(block, after, j):
    rows = block.shape[0]
    rolled = pltpu.roll(block, rows - j, 0)
    edge = pltpu.roll(after, 8 - j, 0)
    row = lax.broadcasted_iota(jnp.int32, after.shape, 0)
    return jnp.concatenate(
        [rolled[: rows - 8], jnp.where(row >= 8 - j, edge, rolled[rows - 8 :])], 0
    )


def conv_pre(block, halo, taps_ref, aux):
    pre = taps_ref[0:1, :] * block
    for j in (1, 2, 3):
        pre = pre + taps_ref[j : j + 1, :] * (aux[:, j : j + 1] * shift_down(block, halo, j))
    return pre


def softplus(v):
    return jnp.maximum(v, 0.0) + jnp.log(1.0 + jnp.exp(-jnp.abs(v)))


def split16(value):
    high = value.astype(bf16)
    return high, (value - high.astype(f32)).astype(bf16)


def widen(value, ex_ref):
    high, low = split16(value)
    return mm(jnp.concatenate([high, low], 1), ex_ref[...])


def head_sums(value, ex_ref):
    high, low = split16(value)
    spread = ex_ref[:LANES, :]
    return mm(high, spread, NT) + mm(low, spread, NT)


def triangle(n, upper=False):
    row = lax.broadcasted_iota(jnp.int32, (n, n), 0)
    col = lax.broadcasted_iota(jnp.int32, (n, n), 1)
    return jnp.where(row <= col if upper else row >= col, 1.0, 0.0).astype(f32)


def gap_mask(aux, auxr):
    n = aux.shape[0]
    row = lax.broadcasted_iota(jnp.int32, (n, n), 0)
    col = lax.broadcasted_iota(jnp.int32, (n, n), 1)
    return jnp.where((row >= col) & (aux[:, 4:5] == auxr[0:1, :]), 0.0, FAR).astype(f32)


def states_kernel(
    u_ref, bc_ref, dt_ref, edge_ref, taps_ref, head_ref, aux_ref, ex_ref,
    xs_ref, bcs_ref, lc_ref, lt_ref, dtv_ref, thr_ref, ent_ref, fin_ref,
    halo, state,
):
    c = pl.program_id(0)
    n, inner = xs_ref.shape

    @pl.when(c == 0)
    def _():
        halo[...] = edge_ref[...]
        state[...] = jnp.zeros_like(state)

    aux = aux_ref[...]
    block = jnp.concatenate([u_ref[...], bc_ref[...]], 1)
    pre = conv_pre(block, halo[...], taps_ref, aux)
    halo[...] = block[n - 8 :]
    act = pre * sigmoid(pre)
    xs = act[:, :inner]
    bcs = act[:, inner:].astype(bf16)
    dtv = softplus(dt_ref[...] + head_ref[0:1, :])
    lc = mm(triangle(n), head_ref[1:2, :] * dtv, precision=highest)
    total = lc[n - 1 : n, :]
    xs_ref[...] = xs.astype(bf16)
    bcs_ref[...] = bcs
    lc_ref[...] = lc
    lt_ref[...] = lc.T
    dtv_ref[...] = dtv
    scale = widen(jnp.exp(total - lc) * aux[:, 6:7] * dtv, ex_ref)
    through = jnp.exp(jnp.broadcast_to(total, (8, LANES))) * aux[n - 1 : n, 5:6]
    through = widen(through, ex_ref)
    thr_ref[0] = through
    ent_ref[0] = state[...]
    state[...] = through[0:1, :] * state[...] + mm(
        bcs[:, :STATE], (xs * scale).astype(bf16), TN
    )
    fin_ref[...] = state[...]


def intra_kernel(xs_ref, bcs_ref, lc_ref, lt_ref, dtv_ref, aux_ref, auxr_ref, ex_ref, y_ref):
    inner = xs_ref.shape[1]
    mask = gap_mask(aux_ref[...], auxr_ref[...])
    scores = mm(bcs_ref[:, STATE:], bcs_ref[:, :STATE], NT)
    xd = xs_ref[...].astype(f32) * widen(dtv_ref[...], ex_ref)
    lane = lax.broadcasted_iota(jnp.int32, (1, LANES), 1)
    for p in range(inner // LANES):
        pair = xd[:, p * LANES : (p + 1) * LANES]
        total = None
        for side in range(2):
            h = 2 * p + side
            decay = jnp.exp(lc_ref[:, h : h + 1] - lt_ref[h : h + 1, :] + mask)
            mine = (lane < HEAD_DIM) if side == 0 else (lane >= HEAD_DIM)
            term = mm((decay * scores).astype(bf16), jnp.where(mine, pair, 0.0).astype(bf16))
            total = term if total is None else total + term
        y_ref[:, p * LANES : (p + 1) * LANES] = total


def read_kernel(
    z_ref, yi_ref, xs_ref, bcs_ref, lc_ref, aux_ref, ex_ref, ent_ref, car_ref, thr_ref, rows_ref,
    y_ref, gg_ref, ss_ref, st_ref, pre,
):
    c = pl.program_id(0)

    @pl.when(c == 0)
    def _():
        pre[...] = jnp.ones_like(pre)

    entering = ent_ref[0] + pre[0:1, :] * car_ref[...]
    pre[...] = pre[...] * thr_ref[0]
    st_ref[0] = entering
    read = mm(bcs_ref[:, STATE:], entering.astype(bf16))
    entry = widen(jnp.exp(lc_ref[...]) * aux_ref[:, 5:6], ex_ref)
    y = yi_ref[...] + entry * read + rows_ref[0:1, :] * xs_ref[...].astype(f32)
    z = z_ref[...]
    gated = y * (z * sigmoid(z))
    y_ref[...] = y
    gg_ref[...] = (gated * rows_ref[1:2, :]).astype(bf16)
    ss_ref[...] = jnp.broadcast_to(
        jnp.sum(gated * gated, axis=1, keepdims=True), ss_ref.shape
    )


def gate_back_kernel(
    dg_ref, z_ref, y_ref, c2_ref, rows_ref, xs_ref, bcs_ref, lc_ref, aux_ref, ex_ref, thr_ref,
    dy_ref, dz_ref, lg_ref, fin_ref, acc_ref, run,
):
    @pl.when(pl.program_id(0) == 0)
    def _():
        run[...] = jnp.zeros_like(run)
        acc_ref[...] = jnp.zeros_like(acc_ref)

    z, y, back = z_ref[...], y_ref[...], dg_ref[...]
    sig = sigmoid(z)
    open_ = z * sig
    gated = y * open_
    d_gated = back * rows_ref[1:2, :] - gated * c2_ref[:, 0:1]
    dy = d_gated * open_
    dz_ref[...] = (d_gated * y * (sig * (1.0 + z * (1.0 - sig)))).astype(bf16)
    dy_ref[...] = dy.astype(bf16)
    acc_ref[0:1, :] += jnp.sum(back * gated, axis=0, keepdims=True)
    acc_ref[1:2, :] += jnp.sum(dy * xs_ref[...].astype(f32), axis=0, keepdims=True)
    entry = widen(jnp.exp(lc_ref[...]) * aux_ref[:, 5:6], ex_ref)
    lg_ref[0] = run[...]
    run[...] = thr_ref[0, 0:1, :] * run[...] + mm(
        bcs_ref[:, STATE:], (entry * dy).astype(bf16), TN
    )
    fin_ref[...] = run[...]


def scan_back_kernel(
    u_ref, bc_ref, uh_ref, bch_ref, edge_ref, dt_ref, dz_ref, taps_ref, head_ref, rows_ref, aux_ref, auxr_ref, ex_ref,
    lc_ref, lt_ref, dtv_ref, dy_ref, st_ref, lg_ref, car_ref, thr_ref,
    dp_ref, last_ref, back_ref, tacc_ref, hacc_ref,
    post, nxt, later,
):
    step = pl.program_id(0)
    chunks = pl.num_programs(0)
    n, inner = dy_ref.shape

    @pl.when(step == 0)
    def _():
        post[...] = jnp.ones_like(post)
        nxt[...] = jnp.zeros_like(nxt)
        tacc_ref[...] = jnp.zeros_like(tacc_ref)
        hacc_ref[...] = jnp.zeros_like(hacc_ref)
        later[...] = jnp.zeros_like(later)

    aux = aux_ref[...]
    block = jnp.concatenate([u_ref[...], bc_ref[...]], 1)
    halo = jnp.concatenate([uh_ref[...], bch_ref[...]], 1)
    halo = jnp.where(step == chunks - 1, edge_ref[...], halo)
    shifted = [block] + [aux[:, j : j + 1] * shift_down(block, halo, j) for j in (1, 2, 3)]
    pre = taps_ref[0:1, :] * block
    for j in (1, 2, 3):
        pre = pre + taps_ref[j : j + 1, :] * shifted[j]
    sig = sigmoid(pre)
    act = pre * sig
    slope = sig * (1.0 + pre * (1.0 - sig))
    xs = act[:, :inner]
    bcs = act[:, inner:].astype(bf16)
    keys, queries = bcs[:, :STATE], bcs[:, STATE:]
    lc, dtv = lc_ref[...], dtv_ref[...]
    total = lc[n - 1 : n, :]
    dt_wide = widen(dtv, ex_ref)
    tail_wide = widen(jnp.exp(total - lc) * aux[:, 6:7], ex_ref)
    entry_wide = widen(jnp.exp(lc) * aux[:, 5:6], ex_ref)
    xd = xs * dt_wide
    dy = dy_ref[...]
    dyf = dy.astype(f32)
    entering = st_ref[0]
    leaving = lg_ref[0] + post[0:1, :] * car_ref[...]
    post[...] = post[...] * thr_ref[0]
    ent16, lea16 = entering.astype(bf16), leaving.astype(bf16)

    row = lax.broadcasted_iota(jnp.int32, (n, n), 0)
    col = lax.broadcasted_iota(jnp.int32, (n, n), 1)
    mask = jnp.where((row <= col) & (aux[:, 4:5] == auxr_ref[0:1, :]), 0.0, FAR).astype(f32)
    scores = mm(keys, queries, NT)
    lane = lax.broadcasted_iota(jnp.int32, (1, LANES), 1)
    earlier = jnp.zeros((n, LANES), f32)
    d_scores = jnp.zeros((n, n), f32)
    parts = []
    for p in range(inner // LANES):
        cut = slice(p * LANES, (p + 1) * LANES)
        xd_pair, dy_pair = xd[:, cut].astype(bf16), dyf[:, cut]
        d_pair = None
        for side in range(2):
            h = 2 * p + side
            mine = (lane < HEAD_DIM) if side == 0 else (lane >= HEAD_DIM)
            dy_mine = jnp.where(mine, dy_pair, 0.0).astype(bf16)
            decay = jnp.exp(lt_ref[h : h + 1, :] - lc_ref[:, h : h + 1] + mask)
            weights = decay * scores
            d_weights = mm(xd_pair, dy_mine, NT)
            both = weights * d_weights
            earlier = jnp.where(lane == h, jnp.sum(both, axis=1, keepdims=True), earlier)
            later[h : h + 1, :] = jnp.sum(both, axis=0, keepdims=True)
            d_scores = d_scores + decay * d_weights
            term = mm(weights.astype(bf16), dy_mine)
            d_pair = term if d_pair is None else d_pair + term
        parts.append(d_pair)
    d_scores16 = d_scores.astype(bf16)
    through_lea = tail_wide * mm(keys, lea16)
    dxd = jnp.concatenate(parts, 1) + through_lea
    dxs = dt_wide * dxd + rows_ref[0:1, :] * dyf
    entry_dy = entry_wide * dyf
    d_queries = mm(d_scores16, keys, TN) + mm(entry_dy.astype(bf16), ent16, NT)
    d_keys = mm(d_scores16, queries) + mm((tail_wide * xd).astype(bf16), lea16, NT)
    d_act = jnp.concatenate([dxs, d_keys, d_queries], 1)
    dpre = d_act * slope

    into = head_sums(entry_dy * mm(queries, ent16), ex_ref)
    outof = head_sums(xd * through_lea, ex_ref)
    ends = head_sums(
        jnp.sum(entering * leaving, axis=0, keepdims=True) * thr_ref[0], ex_ref
    )
    d_log = later[...].T - earlier + into - outof
    row = lax.broadcasted_iota(jnp.int32, (n, 1), 0)
    d_log = d_log + jnp.where(
        row == n - 1, jnp.sum(outof, axis=0, keepdims=True) + ends[0:1, :], 0.0
    )
    d_rate = mm(triangle(n, True), d_log, precision=highest)
    d_dt = head_sums(xs * dxd, ex_ref) + d_rate * head_ref[1:2, :]
    d_step = d_dt * sigmoid(dt_ref[...] + head_ref[0:1, :])
    hacc_ref[0:1, :] += jnp.sum(d_rate * dtv, axis=0, keepdims=True) * head_ref[1:2, :]
    hacc_ref[1:2, :] += jnp.sum(d_step, axis=0, keepdims=True)

    d_block = taps_ref[0:1, :] * dpre
    tacc_ref[0:1, :] += jnp.sum(dpre * block, axis=0, keepdims=True)
    before = jnp.zeros((8, block.shape[1]), f32)
    row8 = lax.broadcasted_iota(jnp.int32, (8, 1), 0)
    for j in (1, 2, 3):
        tacc_ref[j : j + 1, :] += jnp.sum(dpre * shifted[j], axis=0, keepdims=True)
        lagged = taps_ref[j : j + 1, :] * (dpre * aux[:, j : j + 1])
        d_block = d_block + shift_up(lagged, nxt[j - 1], j)
        nxt[j - 1] = lagged[:8]
        before = before + jnp.where(row8 >= 8 - j, pltpu.roll(lagged[:8], 8 - j, 0), 0.0)
    back_ref[...] = before

    @pl.when(step == 0)
    def _():
        last_ref[...] = d_block[n - 8 :]

    dp_ref[:, :inner] = dz_ref[...]
    dp_ref[:, inner : inner + block.shape[1]] = d_block.astype(bf16)
    ends_at = inner + block.shape[1] + LANES
    dp_ref[:, inner + block.shape[1] : ends_at] = d_step.astype(bf16)
    dp_ref[:, ends_at:] = jnp.zeros((n, LANES), bf16)


def sds(shape, dtype):
    return jax.ShapeDtypeStruct(shape, dtype)


def params(mib):
    return pltpu.CompilerParams(
        dimension_semantics=("arbitrary",), vmem_limit_bytes=mib * 1024 * 1024
    )


def whole(shape):
    return pl.BlockSpec(shape, lambda c: (0,) * len(shape))


def mixer_specs(rows, inner, reverse):
    chunks = rows // CHUNK
    at = (lambda c: chunks - 1 - c) if reverse else (lambda c: c)
    return {
        "uh": pl.BlockSpec(
            (8, inner), lambda c: (jnp.maximum(at(c) * (CHUNK // 8) - 1, 0), 0)
        ),
        "bch": pl.BlockSpec(
            (8, 2 * STATE),
            lambda c: (jnp.maximum(at(c) * (CHUNK // 8) - 1, 0), inner // (2 * STATE)),
        ),
        "bc": pl.BlockSpec((CHUNK, 2 * STATE), lambda c: (at(c), inner // (2 * STATE))),
        "dt": pl.BlockSpec((CHUNK, LANES), lambda c: (at(c), (inner + 2 * STATE) // LANES)),
        "wide": pl.BlockSpec((CHUNK, inner), lambda c: (at(c), 0)),
        "bcs": pl.BlockSpec((CHUNK, 2 * STATE), lambda c: (at(c), 0)),
        "col": pl.BlockSpec((CHUNK, LANES), lambda c: (at(c), 0)),
        "lt": pl.BlockSpec((LANES, CHUNK), lambda c: (0, at(c))),
        "auxr": pl.BlockSpec((8, CHUNK), lambda c: (0, at(c))),
        "state": pl.BlockSpec((1, STATE, inner), lambda c: (at(c), 0, 0)),
        "thr": pl.BlockSpec((1, 8, inner), lambda c: (at(c), 0, 0)),
        "dp": pl.BlockSpec((CHUNK, 2 * inner + 2 * STATE + 2 * LANES), lambda c: (at(c), 0)),
        "edge": whole((8, inner + 2 * STATE)),
        "head": whole((8, LANES)),
        "rows": whole((8, inner)),
        "ex": whole((2 * LANES, inner)),
        "one": whole((STATE, inner)),
    }


def mixer_states(pu, edge, taps, head, aux, ex, inner):
    rows = pu.shape[0]
    chunks = rows // CHUNK
    s = mixer_specs(rows, inner, False)
    return pl.pallas_call(
        states_kernel,
        grid=(chunks,),
        in_specs=[
            s["wide"], s["bc"], s["dt"], s["edge"], s["edge"], s["head"], s["col"], s["ex"],
        ],
        out_specs=[
            s["wide"], s["bcs"], s["col"], s["lt"], s["col"], s["thr"], s["state"], s["one"],
        ],
        out_shape=[
            sds((rows, inner), bf16),
            sds((rows, 2 * STATE), bf16),
            sds((rows, LANES), f32),
            sds((LANES, rows), f32),
            sds((rows, LANES), f32),
            sds((chunks, 8, inner), f32),
            sds((chunks, STATE, inner), f32),
            sds((STATE, inner), f32),
        ],
        scratch_shapes=[
            pltpu.VMEM((8, inner + 2 * STATE), f32),
            pltpu.VMEM((STATE, inner), f32),
        ],
        compiler_params=params(32),
        name="mixer_states",
    )(pu, pu, pu, edge, taps, head, aux, ex)


def mixer_intra(xs, bcs, lc, lt, dtv, aux, auxr, ex):
    rows, inner = xs.shape
    s = mixer_specs(rows, inner, False)
    return pl.pallas_call(
        intra_kernel,
        grid=(rows // CHUNK,),
        in_specs=[
            s["wide"], s["bcs"], s["col"], s["lt"], s["col"], s["col"], s["auxr"], s["ex"],
        ],
        out_specs=s["wide"],
        out_shape=sds((rows, inner), f32),
        compiler_params=params(32),
        name="mixer_intra",
    )(xs, bcs, lc, lt, dtv, aux, auxr, ex)


def mixer_read(pz, yi, xs, bcs, lc, aux, ex, ent, carried, thr, head_rows):
    rows, inner = xs.shape
    chunks = rows // CHUNK
    s = mixer_specs(rows, inner, False)
    return pl.pallas_call(
        read_kernel,
        grid=(chunks,),
        in_specs=[
            s["wide"], s["wide"], s["wide"], s["bcs"], s["col"], s["col"], s["ex"],
            s["state"], s["one"], s["thr"], s["rows"],
        ],
        out_specs=[s["wide"], s["wide"], s["col"], s["state"]],
        out_shape=[
            sds((rows, inner), f32),
            sds((rows, inner), bf16),
            sds((rows, LANES), f32),
            sds((chunks, STATE, inner), f32),
        ],
        scratch_shapes=[pltpu.VMEM((8, inner), f32)],
        compiler_params=params(32),
        name="mixer_read",
    )(pz, yi, xs, bcs, lc, aux, ex, ent, carried, thr, head_rows)


def mixer_gate_back(dg, pz, y, c2, head_rows, xs, bcs, lc, aux, ex, thr):
    rows, inner = xs.shape
    chunks = rows // CHUNK
    s = mixer_specs(rows, inner, True)
    return pl.pallas_call(
        gate_back_kernel,
        grid=(chunks,),
        in_specs=[
            s["wide"], s["wide"], s["wide"], s["col"], s["rows"], s["wide"], s["bcs"],
            s["col"], s["col"], s["ex"], s["thr"],
        ],
        out_specs=[s["wide"], s["wide"], s["state"], s["one"], s["rows"]],
        out_shape=[
            sds((rows, inner), bf16),
            sds((rows, inner), bf16),
            sds((chunks, STATE, inner), f32),
            sds((STATE, inner), f32),
            sds((8, inner), f32),
        ],
        scratch_shapes=[pltpu.VMEM((STATE, inner), f32)],
        compiler_params=params(40),
        name="mixer_gate_back",
    )(dg, pz, y, c2, head_rows, xs, bcs, lc, aux, ex, thr)


def mixer_scan_back(
    pu, edge, dz, taps, head, head_rows, aux, auxr, ex, lc, lt, dtv, dy, st, lg, carried, thr
):
    rows, inner = dy.shape
    chunks = rows // CHUNK
    s = mixer_specs(rows, inner, True)
    wide = inner + 2 * STATE
    return pl.pallas_call(
        scan_back_kernel,
        grid=(chunks,),
        in_specs=[
            s["wide"], s["bc"], s["uh"], s["bch"], s["edge"], s["dt"], s["wide"], s["edge"],
            s["head"], s["rows"], s["col"], s["auxr"], s["ex"], s["col"], s["lt"], s["col"], s["wide"], s["state"], s["state"],
            s["one"], s["thr"],
        ],
        out_specs=[s["dp"], s["edge"], s["edge"], s["edge"], s["head"]],
        out_shape=[
            sds((rows, wide + inner + 2 * LANES), bf16),
            sds((8, wide), f32),
            sds((8, wide), f32),
            sds((8, wide), f32),
            sds((8, LANES), f32),
        ],
        scratch_shapes=[
            pltpu.VMEM((8, inner), f32),
            pltpu.VMEM((3, 8, wide), f32),
            pltpu.VMEM((LANES, CHUNK), f32),
        ],
        compiler_params=params(48),
        name="mixer_scan_back",
    )(
        pu, pu, pu, pu, edge, pu, dz, taps, head, head_rows, aux, auxr, ex, lc, lt, dtv, dy, st,
        lg, carried, thr,
    )


def up_kernel(at_ref, x_ref, w_ref, router_ref, named_ref, pat_ref, *refs):
    h_ref, act_ref, gates_ref, cols = refs[-4:]

    @pl.when(pl.program_id(0) == 0)
    def _():
        logits = mm(x_ref[...], router_ref[...], NT)
        mask = named_ref[...] > 0
        peak = jnp.max(jnp.where(mask, logits, FAR), axis=1, keepdims=True)
        raised = jnp.where(mask, jnp.exp(jnp.where(mask, logits - peak, 0.0)), 0.0)
        gates = raised / jnp.sum(raised, axis=1, keepdims=True)
        gates_ref[...] = gates
        cols[...] = gate_columns(gates)

    hidden = mm(x_ref[...], w_ref[...])
    g, w = hidden[:, :FF_BLOCK], hidden[:, FF_BLOCK:]
    gate = mm(cols[...], pat_ref[...])
    h_ref[...] = hidden.astype(bf16)
    act_ref[...] = (g * sigmoid(g) * w * gate).astype(bf16)


def gate_columns(gates):
    lane = lax.broadcasted_iota(jnp.int32, gates.shape, 1)
    high, low = split16(jnp.where(lane == LANES - 1, 1.0, gates))
    return jnp.concatenate([high, low], 1)


def down_back_kernel(at_ref, gs_ref, w_ref, h_ref, gates_ref, pat_ref, *refs):
    dh_ref, dgate_ref, cols = refs[-3:]

    @pl.when(pl.program_id(0) == 0)
    def _():
        dgate_ref[...] = jnp.zeros_like(dgate_ref)
        cols[...] = gate_columns(gates_ref[...])

    for start in range(0, gs_ref.shape[0], ROW_TILE):
        cut = slice(start, start + ROW_TILE)
        q = mm(gs_ref[cut, :], w_ref[...], NT)
        g = h_ref[cut, :FF_BLOCK].astype(f32)
        w = h_ref[cut, FF_BLOCK:].astype(f32)
        sig = sigmoid(g)
        opened = g * sig
        gate = mm(cols[cut, :], pat_ref[...])
        dgate_ref[cut, :] += mm((opened * w * q).astype(bf16), pat_ref[:LANES, :], NT)
        d_act = gate * q
        dh_ref[cut, :FF_BLOCK] = (d_act * w * (sig * (1.0 + g * (1.0 - sig)))).astype(bf16)
        dh_ref[cut, FF_BLOCK:] = (d_act * opened).astype(bf16)


def in_place(state, inputs):
    held = [] if state is None else list(state)
    specs = [pl.BlockSpec(memory_space=pl.ANY)] * len(held)
    return held, specs, {inputs + 1 + i: i for i in range(len(held))}


def experts_up(x, at, w_up, router_w, named, pattern, state):
    own, depth = x.shape
    rows = named.shape[0]
    blocks = w_up.shape[1] // (2 * FF_BLOCK)
    held, specs, aliases = in_place(state, 5)
    return pl.pallas_call(
        up_kernel,
        grid_spec=pltpu.PrefetchScalarGridSpec(
            num_scalar_prefetch=1,
            grid=(blocks,),
            in_specs=[
                pl.BlockSpec((own, depth), lambda i, at: (0, 0)),
                pl.BlockSpec((depth, 2 * FF_BLOCK), lambda i, at: (0, i)),
                pl.BlockSpec((LANES, depth), lambda i, at: (0, 0)),
                pl.BlockSpec((own, LANES), lambda i, at: (at[0], 0)),
                pl.BlockSpec((2 * LANES, FF_BLOCK), lambda i, at: (0, i)),
            ]
            + specs,
            out_specs=[
                pl.BlockSpec((own, 2 * FF_BLOCK), lambda i, at: (at[0], i)),
                pl.BlockSpec((own, FF_BLOCK), lambda i, at: (at[0], i)),
                pl.BlockSpec((own, LANES), lambda i, at: (at[0], 0)),
            ],
            scratch_shapes=[pltpu.VMEM((own, 2 * LANES), bf16)],
        ),
        out_shape=[
            sds((rows, 2 * FF_BLOCK * blocks), bf16),
            sds((rows, FF_BLOCK * blocks), bf16),
            sds((rows, LANES), f32),
        ],
        input_output_aliases=aliases,
        compiler_params=params(58),
        name="experts_up",
    )(at.astype(jnp.int32).reshape(1), x, w_up, router_w, named, pattern, *held)


def experts_down_back(gs, at, w_down, hidden, gates, pattern, state):
    depth = gs.shape[1]
    rows = hidden.shape[0]
    own = gs.shape[0]
    blocks = w_down.shape[0] // FF_BLOCK
    held, specs, aliases = in_place(state, 5)
    return pl.pallas_call(
        down_back_kernel,
        grid_spec=pltpu.PrefetchScalarGridSpec(
            num_scalar_prefetch=1,
            grid=(blocks,),
            in_specs=[
                pl.BlockSpec((own, depth), lambda i, at: (0, 0)),
                pl.BlockSpec((FF_BLOCK, depth), lambda i, at: (i, 0)),
                pl.BlockSpec((own, 2 * FF_BLOCK), lambda i, at: (at[0], i)),
                pl.BlockSpec((own, LANES), lambda i, at: (at[0], 0)),
                pl.BlockSpec((2 * LANES, FF_BLOCK), lambda i, at: (0, i)),
            ]
            + specs,
            out_specs=[
                pl.BlockSpec((own, 2 * FF_BLOCK), lambda i, at: (at[0], i)),
                pl.BlockSpec((own, LANES), lambda i, at: (at[0], 0)),
            ],
            scratch_shapes=[pltpu.VMEM((own, 2 * LANES), bf16)],
        ),
        out_shape=[
            sds((rows, 2 * FF_BLOCK * blocks), bf16),
            sds((rows, LANES), f32),
        ],
        input_output_aliases=aliases,
        compiler_params=params(32 if own == rows else 58),
        name="experts_down_back",
    )(at.astype(jnp.int32).reshape(1), gs, w_down, hidden, gates, pattern, *held)


def row_norm(values):
    return lax.rsqrt(jnp.mean(values * values, axis=-1, keepdims=True) + epsilon)


def norm_back(values, inverse, gain, grad):
    weighted = grad * gain
    mean = jnp.mean(weighted * values, axis=-1, keepdims=True)
    return inverse * weighted - values * (inverse * inverse * inverse * mean)


def pad_rows(parts, rows, width):
    value = jnp.concatenate([jnp.atleast_2d(part) for part in parts], 0)
    return jnp.pad(value, ((0, rows - value.shape[0]), (0, width - value.shape[1])))


def to_line(column):
    value = column.reshape(-1, LANES)
    return jnp.pad(value, ((0, 8 - value.shape[0]), (0, 0)))


def local(
    tokens, inner_proj, step_proj, state_proj, inner_conv, state_conv, decay_log, step_bias,
    skip_gain, gate_gain, outer_proj, norm_gains, router, expert_up, expert_down, shared_up,
    shared_down, routes, packed_lengths, cotangent,
):
    ns, nt = lax.axis_size("seq"), lax.axis_size("tp")
    sq, tp = lax.axis_index("seq"), lax.axis_index("tp")
    layers = inner_proj.shape[0]
    own, depth = tokens.shape
    rows = own * nt
    chunks = rows // CHUNK
    inner = gate_gain.shape[1]
    heads = decay_log.shape[1]
    inner_all = inner * nt
    cut = inner_proj.shape[1]
    fine = state_proj.shape[1]
    devices = ns * nt
    experts = router.shape[2]
    mine = expert_up.shape[1]
    ff = expert_down.shape[2] * ns
    ff_cut = expert_down.shape[2]
    shared = shared_down.shape[1] * ns
    sh_cut = shared_down.shape[1]
    tap_cut = state_conv.shape[2]
    width = inner + 2 * STATE
    hidden_units = mine * ff + shared
    ff_blocks = hidden_units // FF_BLOCK
    per_seq = mine * ff_cut + sh_cut

    ends = jnp.cumsum(packed_lengths, dtype=jnp.int32)
    starts = ends - packed_lengths

    def count(positions):
        return jnp.sum(
            (starts[None, :] <= positions[:, None]).astype(f32), axis=1
        )

    first = sq * rows
    here = first + jnp.arange(rows, dtype=jnp.int32)
    seg = count(here)
    chunk_of = jnp.arange(rows, dtype=jnp.int32) // CHUNK
    lags = [jnp.ones_like(seg)] + [(count(here - j) == seg).astype(f32) for j in (1, 2, 3)]
    alive = (count(first + chunk_of * CHUNK - 1) == seg).astype(f32)
    tail = (count(first + chunk_of * CHUNK + CHUNK - 1) == seg).astype(f32)
    aux = jnp.pad(jnp.stack(lags + [seg, alive, tail], 1), ((0, 0), (0, LANES - 7)))
    auxr = jnp.broadcast_to(seg[None, :], (8, rows))
    lane_head = jnp.arange(inner, dtype=jnp.int32) // HEAD_DIM
    ex_row = jnp.arange(2 * LANES, dtype=jnp.int32)[:, None] % LANES
    ex = (ex_row == lane_head[None, :]).astype(bf16)
    unit = jnp.arange(hidden_units, dtype=jnp.int32) % per_seq
    unit_gate = jnp.where(unit < mine * ff_cut, tp * mine + unit // ff_cut, LANES - 1)
    pat_row = jnp.arange(2 * LANES, dtype=jnp.int32)[:, None] % LANES
    pattern = (pat_row == unit_gate[None, :]).astype(bf16)

    inv1 = row_norm(tokens)
    scaled = (tokens * inv1).astype(bf16)
    smalls, ups = [], []
    for l in range(layers):
        taps_col = jnp.pad(state_conv[l].reshape(-1), (0, fine - 4 * tap_cut))[:, None]
        small = jnp.concatenate([state_proj[l], router[l], norm_gains[l].T, taps_col], 1)
        smalls.append(jnp.pad(small, ((0, 0), (0, 2 * STATE + LANES - small.shape[1]))))
        up = shared_up[l].reshape(fine, 2, ns, nt, sh_cut)
        ups.append(jnp.transpose(up, (3, 0, 1, 2, 4)).reshape(nt, fine, 2 * shared))
    plain, _, riders = hop_both(
        scaled,
        None,
        (jnp.concatenate(smalls, 1), expert_up, jnp.stack(ups, 1), routes, expert_down, shared_down),
    )
    small_all, expert_up, ups, routes, expert_down, shared_down = riders
    small_all = pair_gather(small_all)
    up_all = pair_swap(ups)

    def mixer_weights(l):
        dt_cols = jnp.pad(step_proj[l], ((0, 0), (0, LANES - heads)))
        small = small_all[:, l * (2 * STATE + LANES) : (l + 1) * (2 * STATE + LANES)]
        pack = jnp.concatenate(
            [
                inner_proj[l, :, 0],
                inner_proj[l, :, 1],
                small[:, : 2 * STATE],
                dt_cols,
                small[:, 2 * STATE :],
            ],
            1,
        )
        return pack, outer_proj[l].T

    def over_seq(value):
        return lax.all_gather(value, "seq", axis=0, tiled=True)

    def expert_weights(l):
        halves = jnp.transpose(expert_up[l].reshape(mine, cut, 2, ns, ff_cut), (2, 1, 3, 0, 4))
        halves = halves.reshape(2, cut, ns, mine * ff_cut)
        extra = jnp.transpose(up_all[:, l].reshape(cut, 2, ns, sh_cut), (1, 0, 2, 3))
        halves = jnp.concatenate([halves, extra], 3).reshape(2, cut, ff_blocks, FF_BLOCK)
        local_up = jnp.transpose(halves, (1, 2, 0, 3)).reshape(cut, 2 * hidden_units)
        local_down = jnp.concatenate(
            [expert_down[l].reshape(mine * ff_cut, depth), shared_down[l]], 0
        )
        return local_up, local_down

    packs = [list(mixer_weights(l) + expert_weights(l)) for l in range(layers)]
    plain, *packs[0][2:] = tie(plain, *packs[0][2:])
    w_in, w_out, w_up, w_down = [[None] * layers for _ in range(4)]
    w_in[0], w_out[0] = over_seq(packs[0][0]), over_seq(packs[0][1])

    named = jnp.any(
        routes[:, :, :, None] == jnp.arange(experts, dtype=jnp.int32), axis=2
    ).astype(bf16)
    named = pair_gather(
        jnp.transpose(named, (1, 0, 2)).reshape(own, layers * experts)
    ).reshape(rows, layers, experts)
    named = jnp.pad(named, ((0, 0), (0, 0), (0, LANES - experts))).astype(f32)

    residual = tokens
    saved = []
    last_cot = None
    for l in range(layers):
        small_in = tie(w_in[l][:, inner + width + LANES :].astype(f32).T)[0]
        router_w = jnp.pad(small_in[:experts], ((0, LANES - experts), (0, 0))).astype(bf16)
        gain1 = small_in[experts]
        gain2 = small_in[experts + 1]
        taps_bc = small_in[experts + 2].reshape(devices, fine)[:, : 4 * tap_cut]
        taps_bc = jnp.transpose(taps_bc.reshape(devices, 4, tap_cut), (1, 0, 2))
        taps_bc = taps_bc.reshape(4, 2 * STATE)
        taps = jnp.pad(
            jnp.concatenate([inner_conv[l], taps_bc], 1), ((0, 4), (0, 0))
        )
        head = pad_rows([step_bias[l], -jnp.exp(decay_log[l])], 8, LANES)
        head_rows = pad_rows([jnp.repeat(skip_gain[l], HEAD_DIM), gate_gain[l]], 8, inner)

        if l > 0:
            inv1 = row_norm(residual)
            scaled = (residual * inv1).astype(bf16)
            plain = hop_gather(scaled)
        normed = (plain.astype(f32) * gain1).astype(bf16)
        pu = mm(normed, w_in[l][:, inner : inner + width + LANES])
        edge = shift_seq(pu[rows - 8 :, :width], 1)
        xs, bcs, lc, lt, dtv, thr, ent, fin = mixer_states(pu, edge, taps, head, aux, ex, inner)
        through = thr[0, 0:1]
        for c in range(1, chunks):
            through = through * thr[c, 0:1]
        pz = mm(normed, w_in[l][:, :inner])
        yi = mixer_intra(xs, bcs, lc, lt, dtv, aux, auxr, ex)
        carried, pz, yi = carried_state(through, fin, 1, pz, yi)
        cot16 = cotangent.astype(bf16)
        if l == 0:
            carried, cot16 = tie(carried, cot16)
        carried, up_pack, down_pack = tie(carried, packs[l][2], packs[l][3])
        w_up[l], w_down[l] = over_seq(up_pack), over_seq(down_pack)
        y, gg, ss, st = mixer_read(pz, yi, xs, bcs, lc, aux, ex, ent, carried, thr, head_rows)
        squares = pair_total(ss[:, 0].reshape(rows // LANES, LANES), "tp")
        squares = lax.dynamic_slice_in_dim(
            squares, tp * (own // LANES), own // LANES, 0
        ).reshape(own)
        partial_out = mm(gg, w_out[l], NT).astype(bf16)
        if l == 0:
            last_cot, out_sum, (squares,) = hop_both(cot16, partial_out, (squares,))
            out_sum, last_cot = tie(out_sum, last_cot)
        else:
            _, out_sum, (squares,) = hop_both(None, partial_out, (squares,))
        inv_gate = lax.rsqrt(squares / inner_all + epsilon)
        mixed = inv_gate[:, None] * out_sum
        mid = residual + mixed

        inv2 = row_norm(mid)
        moe_own = (mid * inv2 * gain2).astype(bf16)
        mask = named[:, l]

        def up_block(block, at, state):
            return experts_up(block, at, w_up[l], router_w, mask, pattern, state)

        moe_in, (hidden, act, gates) = gather_work(moe_own, up_block)
        if l < layers - 1:
            act, *packs[l + 1][:2] = tie(act, *packs[l + 1][:2])
            w_in[l + 1], w_out[l + 1] = over_seq(packs[l + 1][0]), over_seq(packs[l + 1][1])
        saved.append(
            dict(
                router_w=router_w, gain1=gain1, gain2=gain2, taps=taps, head=head,
                head_rows=head_rows, residual=residual, inv1=inv1, plain=plain, normed=normed,
                pu=pu, pz=pz, edge=edge, xs=xs, bcs=bcs, lc=lc, lt=lt, dtv=dtv, thr=thr,
                through=through, y=y, gg=gg, st=st, inv_gate=inv_gate, mixed=mixed,
                mid=mid, inv2=inv2, moe_own=moe_own, moe_in=moe_in, gates=gates,
                hidden=hidden, act=act,
            )
        )
        if l < layers - 1:

            moe_out = hop_scatter(mm(act, w_down[l]).astype(bf16))
            moe_out, *packs[l + 1][2:] = tie(moe_out, *packs[l + 1][2:])
            residual = mid + moe_out

    def finish_up(up):
        halves = up.reshape(cut, ff_blocks, 2, FF_BLOCK)
        halves = jnp.transpose(halves, (2, 0, 1, 3)).reshape(2, cut, ns, per_seq)
        mine_up = halves[..., : mine * ff_cut].reshape(2, cut, ns, mine, ff_cut)
        mine_up = jnp.transpose(mine_up, (3, 1, 0, 2, 4)).reshape(mine, cut, 2 * ff)
        mine_up = row_major(mine_up)
        shared_cols = jnp.transpose(halves[..., mine * ff_cut :], (1, 0, 2, 3))
        shared_grad = pair_swap(shared_cols.reshape(nt, fine, 2 * shared))
        shared_grad = jnp.transpose(
            shared_grad.reshape(nt, fine, 2, ns, sh_cut), (1, 2, 3, 0, 4)
        ).reshape(fine, -1)
        return mine_up, shared_grad

    def finish_in(early, late):
        return jnp.stack([early[:, inner:], late[:, :inner]], 1), pair_scatter(late[:, inner:])

    def outputs(r):
        sums, common, down = r["sums"], r["common"], r["down"]
        small = common[:, 2 * STATE + heads :]
        return [
            r["inner"],
            r["late"][:, width : width + heads].astype(f32),
            common[:, : 2 * STATE],
            sums[:4],
            small[: 4 * tap_cut, experts + 2].reshape(4, tap_cut),
            sums[6, :heads],
            sums[6, LANES : LANES + heads],
            jnp.sum(sums[5].reshape(heads, HEAD_DIM), axis=1),
            sums[4],
            r["early"][:, :inner].T,
            jnp.transpose(small[:, experts : experts + 2]),
            small[:, :experts],
            r["mine_up"],
            down[: mine * ff_cut].reshape(mine, ff_cut, depth),
            r["shared_up"],
            down[mine * ff_cut :],
        ]

    grad = cotangent
    finished = [None] * layers
    for l in reversed(range(layers)):
        k = saved[l]
        top = l == layers - 1
        state = None

        def back_block(block, at, state):
            return experts_down_back(
                block, at, w_down[l], k["hidden"], k["gates"], pattern, state
            )

        def gate_sums():
            lines = state[1][:, :experts].reshape(rows // per_line, LANES)
            return pair_total(lines, "tp")

        per_line = LANES // experts
        if top:
            gs = last_cot
            last_out = mm(k["act"], w_down[l]).astype(bf16)
            state = back_block(gs, jnp.int32(0), None)
        else:
            gs, state = gather_work(grad.astype(bf16), back_block)
            first, above["late"] = tie(state[0], above["late"])
            state = (first, state[1])
        d_hidden = state[0]
        up_part = mm(k["moe_in"], d_hidden, TN).astype(bf16)
        _, d_moe, riders = hop_both(
            None,
            mm(d_hidden, w_up[l], NT).astype(bf16),
            (gate_sums(), up_part) + (() if top else (above["up"],)),
        )
        d_gate_all, up_part, *riders = riders
        if not top:
            above["mine_up"], above["shared_up"] = finish_up(riders[0])
        up_grad = lax.psum_scatter(up_part, "seq", scatter_dimension=0, tiled=True)
        down_part = mm(k["act"], gs, TN).astype(bf16)
        if top:
            d_moe, last_out = tie(d_moe, last_out)
        d_gate_own = lax.dynamic_slice_in_dim(
            d_gate_all, tp * (own // per_line), own // per_line, 0
        ).reshape(own, experts)
        d_gate_own = jnp.pad(d_gate_own, ((0, 0), (0, LANES - experts)))
        gates_own = lax.dynamic_slice_in_dim(k["gates"], tp * own, own, 0)
        d_logits = gates_own * (
            d_gate_own - jnp.sum(gates_own * d_gate_own, axis=1, keepdims=True)
        )
        d_logits16 = d_logits.astype(bf16)
        router_grad = mm(k["moe_own"], d_logits16, TN)[:, :experts]
        d_moe = d_moe + mm(d_logits16, k["router_w"])
        gain2_grad = jnp.sum(d_moe * k["mid"] * k["inv2"], axis=0)
        grad_mid = grad + norm_back(k["mid"], k["inv2"], k["gain2"], d_moe)

        inv_gate = k["inv_gate"]
        cross = inv_gate * inv_gate * jnp.sum(grad_mid * k["mixed"], axis=1) / inner_all
        cross_all = pair_gather(to_line(cross)).reshape(nt, 8 * LANES)[:, :own].reshape(rows)
        send = (grad_mid * inv_gate[:, None]).astype(bf16)
        if top:
            d_mixed, moe_out, riders = hop_both(send, last_out, (cross_all, down_part))
            residual = k["mid"] + moe_out
        else:
            names = ("mine_up", "shared_up", "early", "late")
            d_mixed, _, riders = hop_both(
                send, None, [cross_all, down_part] + [above[name] for name in names]
            )
            above.update(zip(names, riders[2:]))
            above["inner"], above["common"] = finish_in(above["early"], above["late"])
        cross_all, down_part = riders[:2]
        down_grad = lax.psum_scatter(down_part, "seq", scatter_dimension=0, tiled=True)
        c2 = jnp.broadcast_to(cross_all[:, None], (rows, LANES))
        dg = mm(d_mixed, w_out[l])
        dy, dz, lg, fin, acc = mixer_gate_back(
            dg, k["pz"], k["y"], c2, k["head_rows"], k["xs"], k["bcs"], k["lc"], aux, ex, k["thr"]
        )
        early_out = row_major(mm(d_mixed, k["gg"], TN).astype(bf16))
        early_z = row_major(mm(k["normed"], dz, TN).astype(bf16))
        carried, early_out, early_z = carried_state(k["through"], fin, -1, early_out, early_z)
        early = jnp.concatenate([early_out, early_z], 1)
        carried, early, up_grad = tie(carried, early, up_grad)
        if top:
            carried, residual = tie(carried, residual)
        early = lax.psum_scatter(early, "seq", scatter_dimension=0, tiled=True)
        dp, last, back, tacc, hacc = mixer_scan_back(
            k["pu"], k["edge"], dz, k["taps"], k["head"], k["head_rows"], aux, auxr, ex,
            k["lc"], k["lt"], k["dtv"], dy, k["st"], lg, carried, k["thr"],
        )
        last = (last + shift_seq(back, -1)).astype(bf16)
        dp = lax.dynamic_update_slice(dp, last, (rows - 8, inner))
        dp, down_grad = tie(dp, down_grad)
        d_normed = mm(dp, w_in[l], NT)
        gain1_grad = jnp.sum(d_normed * k["plain"].astype(f32), axis=0)
        taps_col = jnp.transpose(tacc[:4, inner:].reshape(4, devices, tap_cut), (1, 0, 2))
        taps_col = jnp.pad(taps_col.reshape(devices, 4 * tap_cut), ((0, 0), (0, fine - 4 * tap_cut)))
        small = jnp.concatenate(
            [router_grad, gain1_grad[:, None], gain2_grad[:, None], taps_col.reshape(-1)[:, None]],
            1,
        )
        late = mm(k["normed"], dp[:, inner : inner + width + LANES], TN).astype(bf16)
        block = late[:, width:] + jnp.pad(
            small, ((0, 0), (heads, LANES - heads - small.shape[1]))
        ).astype(bf16)
        late = lax.dynamic_update_slice(late, block, (0, width))
        sums = jnp.concatenate(
            [tacc[:4, :inner], acc[:2], pad_rows([hacc[:2].reshape(-1)], 2, inner)], 0
        )
        if top:
            _, d_own, riders = hop_both(None, d_normed.astype(bf16), (late, sums))
            late, sums = riders
        else:
            _, d_own, riders = hop_both(
                None,
                d_normed.astype(bf16),
                (late, early, above["inner"], above["common"]),
                (sums, above["sums"], up_grad),
            )
            above["inner"], above["common"] = riders[2:4]
            riders = riders[:2] + riders[4:]
            late, early, sums = riders[:3]
        late = lax.psum_scatter(late, "seq", scatter_dimension=0, tiled=True)
        if top:
            d_own, early = tie(d_own, early)
        else:
            both = pair_total(jnp.concatenate([sums, riders[3]], 0), "seq")
            sums, above["sums"] = both[: sums.shape[0]], both[sums.shape[0] :]
            finished[l + 1] = outputs(above)
            d_own, down_grad = tie(d_own, down_grad)
        grad = grad_mid + norm_back(k["residual"], k["inv1"], k["gain1"], d_own)
        above = dict(up=up_grad, down=down_grad, early=early, late=late, sums=sums)
        if not top:
            above["mine_up"], above["shared_up"] = finish_up(riders[4])

    above["inner"], above["common"] = finish_in(above["early"], above["late"])
    finished[0] = outputs(above)
    stacked = [jnp.stack([part[i] for part in finished], 0).astype(f32) for i in range(16)]
    return (residual, grad, *stacked)


def solution(mesh):
    both = ("seq", "tp")
    in_specs = (
        P(both, None),
        P(None, "seq", None, "tp"),
        P(None, "seq", "tp"),
        P(None, both, None),
        P(None, None, "tp"),
        P(None, None, both),
        P(None, "tp"),
        P(None, "tp"),
        P(None, "tp"),
        P(None, "tp"),
        P(None, "tp", "seq"),
        P(None, None, both),
        P(None, both, None),
        P(None, "tp", "seq", None),
        P(None, "tp", "seq", None),
        P(None, both, None),
        P(None, both, None),
        P(None, both, None),
        P(),
        P(both, None),
    )
    out_specs = (
        P(both, None),
        P(both, None),
        P(None, "seq", None, "tp"),
        P(None, "seq", "tp"),
        P(None, both, None),
        P(None, None, "tp"),
        P(None, None, both),
        P(None, "tp"),
        P(None, "tp"),
        P(None, "tp"),
        P(None, "tp"),
        P(None, "tp", "seq"),
        P(None, None, both),
        P(None, both, None),
        P(None, "tp", "seq", None),
        P(None, "tp", "seq", None),
        P(None, both, None),
        P(None, both, None),
    )
    return jax.shard_map(local, mesh=mesh, in_specs=in_specs, out_specs=out_specs, check_vma=False)
```
